256 devices in a mesh: row: 8 (over x, y_hi), col: 8 (over z), dp: 4 (over y_lo, core).
Axes of the slice: x: 4, y: 4 (y_hi: 2, y_lo: 2; y = y_hi * 2 + y_lo), z: 8, core: 2. Of those that a mesh axis runs over, the one named last changes fastest.
Arguments:
- latent_image: bfloat16 [8, 448, 3072], P('dp', 'col'), may hold values from -127 to 127
- latent_text: bfloat16 [8, 64, 3072], P('dp', 'col'), may hold values from -127 to 127
- noise_image: bfloat16 [8, 448, 3072], P('dp', 'col'), may hold values from -5 to 5
- noise_text: bfloat16 [8, 64, 3072], P('dp', 'col'), may hold values from -5 to 5
- up_image: bfloat16 [3072, 12288], P('row', 'col'), may hold values from -0.109375 to 0.109375
- down_image: bfloat16 [3072, 12288], P('row', 'col'), may hold values from -0.0546875 to 0.0546875
- up_text: bfloat16 [3072, 12288], P('row', 'col'), may hold values from -0.109375 to 0.109375
- down_text: bfloat16 [3072, 12288], P('row', 'col'), may hold values from -0.0546875 to 0.0546875
- modulation: float32 [2, 3, 2, 3072], replicated, may hold values from -3 to 3
- timesteps: int32 [8], P('dp'), may hold values from 500 to 999
- skips: int32 [8], P('dp'), may hold values from 1 to 499
- text_lengths: int32 [8], P('dp'), may hold values from 1 to 64, 288 in all
Outputs:
- grad_up_image: float32 [3072, 12288], P('row', ('col', 'dp'))
- grad_down_image: float32 [3072, 12288], P('row', ('col', 'dp'))
- grad_up_text: float32 [3072, 12288], P('row', ('col', 'dp'))
- grad_down_text: float32 [3072, 12288], P('row', ('col', 'dp'))
The draws below stay inside these ranges and needn't reach their ends.
All inputs are finite; a program needn't handle non-finite values. No bound on the sum of `text_lengths` on one device may be relied on, other than what follows from the above.
Results may differ from the reference program's by a relative error of at most 0.03.
Values may be sent and summed in bfloat16 or wider, within the bound.
A program may use at most 64 MiB of HBM per device.

```python
import math
import jax
import jax.numpy as jnp
import numpy as np
from jax import lax

D = 3072
FF = 12288
IMG = 448
TXT = 64
SPD = 2
STEPS = 1000
SEQ = 512
SAMPLES = 8
N_ROW = 8
N_DP = 4


def spread_scales(key_channel, key_token, row_count):
    channel = 10.0 ** jax.random.uniform(key_channel, (D,), jnp.float32)
    token_scale = 10.0 ** (0.5 * jax.random.uniform(key_token, (SAMPLES, row_count, 1), jnp.float32))
    return channel[None, None, :] * token_scale


def draw_latent_image(key, part):
    key = jax.random.fold_in(key, 11)
    key_list = jax.random.split(key, 3)
    base_draw = jnp.clip(jax.random.normal(key_list[2], (SAMPLES, IMG, D), jnp.float32), -4.0, 4.0)
    return (base_draw * spread_scales(key_list[0], key_list[1], IMG)).astype(jnp.bfloat16)


def draw_latent_text(key, part):
    key = jax.random.fold_in(key, 23)
    key_list = jax.random.split(key, 3)
    base_draw = jnp.clip(jax.random.normal(key_list[2], (SAMPLES, TXT, D), jnp.float32), -4.0, 4.0)
    return (base_draw * spread_scales(key_list[0], key_list[1], TXT)).astype(jnp.bfloat16)


def plant(values, own_key, smallest, high):
    longest = values.shape.index(max(values.shape))
    spots = []
    for shift in (0, 1):
        where = [jax.random.randint(jax.random.fold_in(own_key, axis), (), 0, length) for axis, length in enumerate(values.shape)]
        where[longest] = (where[longest] + shift) % values.shape[longest]
        spots.append(tuple(where))
    return values.at[spots[0]].set(smallest).at[spots[1]].set(high)


def block_levels(own_key, shape, shards, least, top_value):
    loudness = 1.0
    for position, blocks in shards:
        steps = jax.random.uniform(jax.random.fold_in(jax.random.fold_in(own_key, 6), position), (blocks,), jnp.float32, least / len(shards), top_value / len(shards))
        loudness = loudness * jnp.repeat(jnp.exp(steps), shape[position] // blocks).reshape((-1,) + (1,) * (len(shape) - 1 - position))
    return loudness


def split_up(number_of, total, most, skew):
    portions = [(1 << 20) // math.isqrt(standing ** skew) + 1 for standing in range(2, number_of + 1)]
    surplus, holding = total - most - (number_of - 1), [1] * (number_of - 1)
    while surplus > 0:
        candidates = [i for i in range(number_of - 1) if holding[i] < most]
        mass, remaining = sum([portions[i] for i in candidates]), surplus
        for i in candidates:
            extra = min(most - holding[i], max(1, remaining * portions[i] // mass), surplus)
            holding[i] = holding[i] + extra
            surplus = surplus - extra
    return np.array([most] + holding)


def uneven(rng, number_of, total, bound, lean):
    if number_of == 2:
        one = jax.random.randint(rng, (), max(1, total - bound), min(bound, total - 1) + 1)
        return jnp.stack([one, total - one])
    tallies = jnp.asarray(split_up(number_of, total, bound, lean), jnp.int32)
    twos = (number_of - 1) // 2
    source_of, taker = tallies[1:1 + 2 * twos:2], tallies[2:2 + 2 * twos:2]
    slack = jnp.minimum(source_of - 1, bound - taker)
    moved = jax.random.randint(jax.random.fold_in(rng, 1), (twos,), 0, 1 << 20) % (slack + 1)
    tallies = tallies.at[1:1 + 2 * twos:2].set(source_of - moved).at[2:2 + 2 * twos:2].set(taker + moved)
    return tallies[jax.random.permutation(jax.random.fold_in(rng, 2), number_of)]


def noise(stream_key, dims, spread, limit, cuts=(), held_as=jnp.bfloat16):
    result = jax.random.normal(stream_key, dims, jnp.float32) * spread
    if len(cuts) > 0:
        result = block_levels(stream_key, dims, cuts, -0.22, 0.18) * result
    return jnp.clip(result, min=-limit, max=limit).astype(held_as)


def setup_inputs(seed: int = 0) -> dict:
    arg_keys = jax.random.split(jax.random.key(seed), 13)
    latent_image = draw_latent_image(jax.random.fold_in(arg_keys[12], 71), 0)
    latent_text = draw_latent_text(jax.random.fold_in(arg_keys[12], 71), 0)
    noise_image = noise(arg_keys[2], (SAMPLES, IMG, D), 1.0, 5.0, ((0, 4), (1, 8)))
    noise_text = noise(arg_keys[3], (SAMPLES, TXT, D), 1.0, 5.0, ((0, 4), (1, 8)))
    up_image = noise(arg_keys[4], (D, FF), D ** -0.5, 0.109375, ((0, 8), (1, 8)))
    down_image = noise(arg_keys[5], (D, FF), FF ** -0.5, 0.0546875, ((0, 8), (1, 8)))
    up_text = noise(arg_keys[6], (D, FF), D ** -0.5, 0.109375, ((0, 8), (1, 8)))
    down_text = noise(arg_keys[7], (D, FF), FF ** -0.5, 0.0546875, ((0, 8), (1, 8)))
    modulation = noise(arg_keys[8], (2, 3, 2, D), 0.5, 3.0, (), jnp.float32)
    timesteps = plant(jax.random.randint(arg_keys[9], (SAMPLES,), STEPS // 2, STEPS), jax.random.fold_in(arg_keys[9], 1), STEPS // 2, STEPS - 1).astype(jnp.int32)
    skips = plant(jax.random.randint(arg_keys[10], (SAMPLES,), 1, STEPS // 2), jax.random.fold_in(arg_keys[10], 1), 1, (STEPS // 2) - 1).astype(jnp.int32)
    text_lengths = uneven(arg_keys[11], SAMPLES, SAMPLES * TXT // 2 + TXT // 2, TXT, 1).astype(jnp.int32)
    return dict(latent_image=latent_image, latent_text=latent_text, noise_image=noise_image, noise_text=noise_text, up_image=up_image, down_image=down_image, up_text=up_text, down_text=down_text, modulation=modulation, timesteps=timesteps, skips=skips, text_lengths=text_lengths)


GELU_SCALE = 0.7978845608028654
GELU_CUBIC = 0.044715
NORM_EPS = 1e-06

def gelu_tanh(values):
    inner = GELU_SCALE * (values + GELU_CUBIC * values * values * values)
    return 0.5 * values * (1.0 + jnp.tanh(inner))

def gelu_slope(values):
    inner = GELU_SCALE * (values + GELU_CUBIC * values * values * values)
    tangent = jnp.tanh(inner)
    return 0.5 * (1.0 + tangent) + 0.5 * values * (1.0 - tangent * tangent) * GELU_SCALE * (1.0 + 3.0 * GELU_CUBIC * values * values)

def time_features(times_both, channels):
    half_width = channels // 2
    channel = jnp.arange(channels) % half_width
    frequency = jnp.exp(-math.log(10000.0) * channel.astype(jnp.float32) / half_width)
    angles = times_both[:, None] * frequency[None, :]
    return jnp.where(jnp.arange(channels)[None, :] < half_width, jnp.cos(angles), jnp.sin(angles))

def rounded(values):
    return lax.optimization_barrier(values.astype(jnp.bfloat16)).astype(jnp.float32)

def blocked_product(left, right):
    slab_width = D // N_ROW
    total = jnp.zeros((left.shape[0], right.shape[1]), jnp.float32)
    for block in range(N_ROW):
        first_col = block * slab_width
        partial_value = jnp.dot(left[:, first_col:first_col + slab_width], right[first_col:first_col + slab_width], preferred_element_type=jnp.float32)
        total = total + rounded(partial_value)
    return total

def stream_terms(clean_part, noise_part, up_weight, down_weight, mod_table, features, noise_level, weight_rows, mask_rows):
    seq_len = clean_part.shape[1]
    noisy_input = (1.0 - noise_level) * jnp.concatenate([clean_part, clean_part]) + noise_level * jnp.concatenate([noise_part, noise_part])
    shift_rows = mod_table[0, 0] + mod_table[0, 1] * features
    scale_rows = mod_table[1, 0] + mod_table[1, 1] * features
    gate_rows = mod_table[2, 0] + mod_table[2, 1] * features
    row_mean = lax.optimization_barrier(jnp.mean(noisy_input, axis=-1, keepdims=True))
    centered = noisy_input - row_mean
    variance = lax.optimization_barrier(jnp.mean(centered * centered, axis=-1, keepdims=True))
    normed = centered * lax.rsqrt(variance + NORM_EPS)
    u_rows = (normed * (1.0 + scale_rows[:, None, :]) + shift_rows[:, None, :]).astype(jnp.bfloat16)
    u_flat = u_rows.reshape(-1, D)
    preact = blocked_product(u_flat, up_weight)
    hidden = gelu_tanh(preact).astype(jnp.bfloat16)
    mlp_out = jnp.dot(hidden, down_weight.T, preferred_element_type=jnp.float32).reshape(noisy_input.shape)
    block_out = noisy_input + gate_rows[:, None, :] * mlp_out
    count = SPD
    out_grad = weight_rows[:, None, None] * mask_rows[:, :, None] * (block_out[:count] - block_out[count:])
    err_rows = (gate_rows[:count][:, None, :] * out_grad).astype(jnp.bfloat16).reshape(-1, D)
    student_rows = count * seq_len
    hid_grad = blocked_product(err_rows, down_weight)
    pre_grad = (hid_grad * gelu_slope(preact[:student_rows])).astype(jnp.bfloat16)
    grad_up = jnp.dot(u_flat[:student_rows].T, pre_grad, preferred_element_type=jnp.float32)
    grad_down = jnp.dot(err_rows.T, hidden[:student_rows], preferred_element_type=jnp.float32)
    return (rounded(grad_up), rounded(grad_down))

def reference(latent_image, latent_text, noise_image, noise_text, up_image, down_image, up_text, down_text, modulation, timesteps, skips, text_lengths):
    t_student = timesteps.astype(jnp.float32)
    t_target = (timesteps - skips).astype(jnp.float32)
    weight_all = SEQ / math.sqrt(SAMPLES * SEQ) / (IMG + text_lengths).astype(jnp.float32)
    text_mask = (jnp.arange(TXT)[None, :] < text_lengths[:, None]).astype(jnp.float32)
    image_mask = jnp.ones((SPD, IMG), jnp.float32)
    totals = [jnp.zeros((D, FF), jnp.float32) for _ in range(4)]
    for member in range(N_DP):
        first_row = member * SPD
        last_row = first_row + SPD
        times_both = jnp.concatenate([t_student[first_row:last_row], t_target[first_row:last_row]])
        features = time_features(times_both, D)
        noise_level = (times_both / STEPS)[:, None, None]
        weight_rows = weight_all[first_row:last_row]
        image_grads = stream_terms(latent_image[first_row:last_row].astype(jnp.float32), noise_image[first_row:last_row].astype(jnp.float32), up_image, down_image, modulation[0], features, noise_level, weight_rows, image_mask)
        text_grads = stream_terms(latent_text[first_row:last_row].astype(jnp.float32), noise_text[first_row:last_row].astype(jnp.float32), up_text, down_text, modulation[1], features, noise_level, weight_rows, text_mask[first_row:last_row])
        parts = image_grads + text_grads
        totals = [total + partial_value for total, partial_value in zip(totals, parts)]
    return (totals[0], totals[1], totals[2], totals[3])
```

```python
import functools
import math

import jax
import jax.numpy as jnp
from jax import lax
from jax.experimental import pallas as pl
from jax.experimental.pallas import tpu as pltpu
from jax.sharding import PartitionSpec as P

D = 3072
FF = 12288
IMG = 448
TXT = 64
STEPS = 1000
SEQ = 512

NX = 4
NZ = 8
CH = D // NX
HB = FF // NZ
HQ = HB // NX
RI = IMG // NZ
RT = TXT // NZ
NJ = 3
HJ = HQ // NJ
ROWS = D // 8
QR = ROWS // 4

GELU_SCALE = 0.7978845608028654
GELU_CUBIC = 0.044715
NORM_EPS = 1e-06
MESH = pl.DeviceIdType.MESH
F32 = jnp.float32
BF16 = jnp.bfloat16


def gelu_tanh(values):
    inner = GELU_SCALE * (values + GELU_CUBIC * values * values * values)
    return 0.5 * values * (1.0 + jnp.tanh(inner))


def gelu_slope(values):
    inner = GELU_SCALE * (values + GELU_CUBIC * values * values * values)
    tangent = jnp.tanh(inner)
    return 0.5 * (1.0 + tangent) + 0.5 * values * (1.0 - tangent * tangent) * GELU_SCALE * (
        1.0 + 3.0 * GELU_CUBIC * values * values
    )


def dot(a, b):
    return jnp.dot(a, b, preferred_element_type=F32)


def dot_nt(a, b):
    return lax.dot_general(a, b, (((1,), (1,)), ((), ())), preferred_element_type=F32)


def kernel(
    lat_i, lat_t, noi_i, noi_t, up_i, up_t, dn_i, dn_t, mod, coef, levels,
    out_ui, out_di, out_ut, out_dt,
    lbi, lbt, nbi, nbt, W, uimg, utxt, ndiff, u32,
    stg, stgt, rrs, rrst, hid, hidt, pre_c, h32, hc,
    zst, rem, zr, errz, e32, ec, uT, eT, uTt, eTt, hgs, hgr, pg, G, CR, YR,
    s_loc, s_wl, s_w1s, s_w1r, s_w2s, s_w2r, s_w3s, s_w3r,
    s_zis, s_zir, s_zts, s_ztr,
    s_rss, s_rsr, s_ags, s_agr, s_mzs, s_mzr, s_mrs, s_mrr, s_ezs, s_ezr,
    s_hgs, s_hgr, s_pgs, s_pgr, s_cs, s_cr, s_ys, s_yr,
):
    r = lax.axis_index("row")
    z = lax.axis_index("col")
    d = lax.axis_index("dp")
    x, hi, lo, c = r // 2, r % 2, d // 2, d % 2
    y = hi * 2 + lo

    def dev(x, hi, lo, c, z):
        return (x * 2 + hi, z, lo * 2 + c)

    def xdev(t):
        return dev((x + t) % NX, hi, lo, c, z)

    def zdev(t):
        return dev(x, hi, lo, c, (z + t + NZ) % NZ)

    def ydev(t):
        yy = (y + t) % 4
        return dev(x, yy // 2, yy % 2, c, z)

    core = dev(x, hi, lo, 1 - c, z)
    adj = dev(x, 1 - hi, 1 - lo, c, z)
    side = dev(x, hi, 1 - lo, c, z)

    def remote(src, dst, ss, rs, who):
        return pltpu.make_async_remote_copy(
            src_ref=src, dst_ref=dst, send_sem=ss, recv_sem=rs, device_id=who, device_id_type=MESH
        )

    bar = pltpu.get_barrier_semaphore()
    for t in range(1, NX):
        pl.semaphore_signal(bar, inc=1, device_id=xdev(t), device_id_type=MESH)
    for t in range(1, NZ):
        pl.semaphore_signal(bar, inc=1, device_id=zdev(t), device_id_type=MESH)
    for t in range(1, 4):
        pl.semaphore_signal(bar, inc=1, device_id=ydev(t), device_id_type=MESH)
    pl.semaphore_signal(bar, inc=1, device_id=core, device_id_type=MESH)

    reads = [
        pltpu.make_async_copy(lat_i.at[hi], lbi, s_loc.at[0]),
        pltpu.make_async_copy(lat_t.at[hi], lbt, s_loc.at[1]),
        pltpu.make_async_copy(noi_i.at[hi], nbi, s_loc.at[2]),
        pltpu.make_async_copy(noi_t.at[hi], nbt, s_loc.at[3]),
    ]
    for cp in reads:
        cp.start()
    weights = (up_i, up_t, dn_i, dn_t)
    wl = [
        pltpu.make_async_copy(
            weights[m], W.at[m, pl.ds(pl.multiple_of(hi * ROWS, ROWS), ROWS)], s_wl.at[m]
        )
        for m in range(4)
    ]

    pl.semaphore_wait(bar, 14)

    def wrows(m, half, quarter):
        return W.at[m, pl.ds(pl.multiple_of(half * ROWS + quarter * QR, QR), QR)]

    q_mine = lo * 2 + c
    q_side = (1 - lo) * 2 + c
    w1 = [
        remote(
            weights[m].at[pl.ds(pl.multiple_of(q_side * QR, QR), QR)],
            wrows(m, hi, q_side), s_w1s.at[m], s_w1r.at[m], adj,
        )
        for m in range(4)
    ]
    w1in = [remote(wrows(m, 1 - hi, q_mine), wrows(m, 1 - hi, q_mine), s_w1s.at[m], s_w1r.at[m], adj) for m in range(4)]
    w2 = [remote(wrows(m, 1 - hi, q_mine), wrows(m, 1 - hi, q_mine), s_w2s.at[m], s_w2r.at[m], side) for m in range(4)]
    w2in = [remote(wrows(m, 1 - hi, q_side), wrows(m, 1 - hi, q_side), s_w2s.at[m], s_w2r.at[m], side) for m in range(4)]
    w3a = [remote(wrows(m, 1 - hi, q_mine), wrows(m, 1 - hi, q_mine), s_w3s.at[m, 0], s_w3r.at[m, 0], core) for m in range(4)]
    w3b = [remote(wrows(m, 1 - hi, q_side), wrows(m, 1 - hi, q_side), s_w3s.at[m, 1], s_w3r.at[m, 1], core) for m in range(4)]

    def w_step1(m):
        w1in[m].wait_recv()
        w2[m].start()
        w3a[m].start()

    def w_step2(m):
        w2in[m].wait_recv()
        w3b[m].start()

    def w_step3(m):
        wl[m].wait()
        w3a[m].wait_recv()
        w3b[m].wait_recv()

    for m in range(4):
        w1[m].start()
    for m in range(4):
        wl[m].start()

    for cp in reads:
        cp.wait()
    lane0 = pl.multiple_of(x * CH, CH)
    for latb, noib, rows, stream, base in ((lbi, nbi, RI, 0, 0), (lbt, nbt, RT, 1, RI)):
        lat_own = latb[:, pl.ds(lane0, CH)].astype(F32)
        noi_own = noib[:, pl.ds(lane0, CH)].astype(F32)
        owns = []
        us = []
        for b in range(2):
            level = levels[b]
            full = (1.0 - level) * latb[...].astype(F32) + level * noib[...].astype(F32)
            mean = jnp.mean(full, axis=-1, keepdims=True)
            cen = full - mean
            var = jnp.mean(cen * cen, axis=-1, keepdims=True)
            own = (1.0 - level) * lat_own + level * noi_own
            owns.append(own)
            normed = (own - mean) * lax.rsqrt(var + NORM_EPS)
            us.append(normed * (1.0 + mod[stream, 1, b : b + 1, :]) + mod[stream, 0, b : b + 1, :])
        ndiff[base : base + rows, :] = owns[0] - owns[1]
        both = jnp.concatenate(us, axis=0).astype(BF16)
        if stream == 0:
            uimg[0] = both
        else:
            utxt[0:16, :] = both

    def send_z(i, to, who):
        a = remote(uimg.at[i], uimg.at[to], s_zis.at[to], s_zir.at[to], who)
        b = remote(
            utxt.at[pl.ds(pl.multiple_of(i * 16, 16), 16)],
            utxt.at[pl.ds(pl.multiple_of(to * 16, 16), 16)],
            s_zts.at[to], s_ztr.at[to], who,
        )
        return a, b

    for to, who in ((1, zdev(1)), (2, zdev(-1))):
        for cp in send_z(0, to, who):
            cp.start()

    w_step1(0)
    w_step1(1)
    w_step2(0)
    w_step3(0)

    def rs_img(i, t):
        return remote(stg.at[i, (x + t) % NX], rrs.at[i, t - 1], s_rss.at[i, t - 1], s_rsr.at[i, t - 1], xdev(t))

    def ag_img(i, t):
        return remote(hid.at[i, x], hid.at[i, x], s_ags.at[i, t - 1], s_agr.at[i, t - 1], xdev(t))

    def ag_img_in(i, t):
        f = (x + NX - t) % NX
        return remote(hid.at[i, f], hid.at[i, f], s_ags.at[i, t - 1], s_agr.at[i, t - 1], xdev(t))

    def rs_txt(t):
        return remote(stgt.at[(x + t) % NX], rrst.at[t - 1], s_rss.at[8, t - 1], s_rsr.at[8, t - 1], xdev(t))

    def ag_txt(t):
        return remote(hidt.at[x], hidt.at[x], s_ags.at[8, t - 1], s_agr.at[8, t - 1], xdev(t))

    def ag_txt_in(t):
        f = (x + NX - t) % NX
        return remote(hidt.at[f], hidt.at[f], s_ags.at[8, t - 1], s_agr.at[8, t - 1], xdev(t))

    def up_chunk(i, _):
        @pl.when(i > 0)
        def _():
            a, b = send_z(i, i, zdev(1))
            a.wait_recv()
            b.wait_recv()

        @pl.when(jnp.logical_and(i > 0, i < 6))
        def _():
            for cp in send_z(i, i + 2, zdev((i % 2) * 2 - 1)):
                cp.start()

        u = uimg[i]
        for q in range(NX):
            stg[i, q] = dot(u, W[0, :, q * HQ : (q + 1) * HQ]).astype(BF16)
        for t in range(1, NX):
            rs_img(i, t).start()
        return 0

    lax.fori_loop(0, NZ, up_chunk, 0)

    w_step2(1)
    w_step3(1)
    for q in range(NX):
        stgt[q] = dot(utxt[...], W[1, :, q * HQ : (q + 1) * HQ]).astype(BF16)
    for t in range(1, NX):
        rs_txt(t).start()
    w_step1(2)
    w_step1(3)
    w_step2(2)
    w_step2(3)

    def pack_u(i, _):
        u32[pl.ds(pl.multiple_of(i * RI, 8), RI), :] = uimg[i].astype(F32)[0:RI]
        u32[pl.ds(pl.multiple_of(IMG + i * RT, 8), RT), :] = utxt[
            pl.ds(pl.multiple_of(i * 16, 16), 16), :
        ].astype(F32)[0:RT]
        return 0

    lax.fori_loop(0, NZ, pack_u, 0)

    def act_chunk(i, _):
        for t in range(1, NX):
            rs_img(i, t).wait_recv()
        pre = stg[i, x].astype(F32)
        for t in range(1, NX):
            pre = pre + rrs[i, t - 1].astype(F32)
        pre_c[pl.ds(pl.multiple_of(i * RI, 8), RI), :] = pre[0:RI]
        hid[i, x] = gelu_tanh(pre).astype(BF16)
        for t in range(1, NX):
            ag_img(i, t).start()
        return 0

    def act_text():
        for t in range(1, NX):
            rs_txt(t).wait_recv()
        pre = stgt[x].astype(F32)
        for t in range(1, NX):
            pre = pre + rrst[t - 1].astype(F32)
        for i in range(NZ):
            pre_c[IMG + i * RT : IMG + (i + 1) * RT, :] = pre[i * 16 : i * 16 + RT]
        hidt[x] = gelu_tanh(pre).astype(BF16)
        for t in range(1, NX):
            ag_txt(t).start()

    lax.fori_loop(0, 6, act_chunk, 0)
    act_text()
    lax.fori_loop(6, NZ, act_chunk, 0)

    w_step3(2)
    w_step3(3)

    def zslot(i):
        half = (i + 1) // 2
        return (NZ + half - 2 * half * (i % 2)) % NZ

    def mz_main(i):
        s = zslot(i)
        return remote(zst.at[i, 0:48], zr.at[s, 0:48], s_mzs.at[i], s_mzr.at[s], zdev(s))

    def mz_rest(i):
        s = zslot(i)
        return remote(zst.at[i, 48:64], zr.at[s, 48:64], s_mrs.at[i], s_mrr.at[s], zdev(s))

    def down_chunk(i, _):
        for t in range(1, NX):
            ag_img_in(i, t).wait_recv()
        out = dot_nt(hid[i, 0], W[2, :, 0:HQ])
        for q in range(1, NX):
            out = out + dot_nt(hid[i, q], W[2, :, q * HQ : (q + 1) * HQ])
        diff = mod[0, 2, 0:1, :] * out[0:RI] - mod[0, 2, 1:2, :] * out[RI : 2 * RI]
        zst[i, 0:48, :] = diff[0:48].astype(BF16)
        rem[i, 0:8, :] = diff[48:56]

        @pl.when(i > 0)
        def _():
            mz_main(i).start()

        for q in range(NX):
            h32[q, pl.ds(pl.multiple_of(i * RI, 8), RI), :] = hid[i, q].astype(F32)[0:RI]
        return 0

    def rest_chunk(i, _):
        zst[i, 48:64, :] = rem[i].astype(BF16)

        @pl.when(i > 0)
        def _():
            mz_rest(i).start()

        return 0

    def down_text():
        for t in range(1, NX):
            ag_txt_in(t).wait_recv()
        out = dot_nt(hidt[0], W[3, :, 0:HQ])
        for q in range(1, NX):
            out = out + dot_nt(hidt[q], W[3, :, q * HQ : (q + 1) * HQ])
        for i in range(NZ):
            rem[i, 8:16, :] = (
                mod[1, 2, 0:1, :] * out[i * 16 : i * 16 + RT] - mod[1, 2, 1:2, :] * out[i * 16 + RT : (i + 1) * 16]
            )
        for q in range(NX):
            full = hidt[q].astype(F32)
            for i in range(NZ):
                h32[q, IMG + i * RT : IMG + (i + 1) * RT, :] = full[i * 16 : i * 16 + RT]

    lax.fori_loop(0, 6, down_chunk, 0)
    down_text()
    lax.fori_loop(0, 6, rest_chunk, 0)
    lax.fori_loop(6, NZ, down_chunk, 0)
    lax.fori_loop(6, NZ, rest_chunk, 0)

    img_lane = lax.broadcasted_iota(jnp.int32, (CH, SEQ), 1) < IMG
    txt_lane = lax.broadcasted_iota(jnp.int32, (CH, 128), 1) >= 64
    turned = u32[...].T
    uT[...] = jnp.where(img_lane, turned, 0.0).astype(BF16)
    uTt[...] = jnp.where(txt_lane, turned[:, SEQ - 128 :], 0.0).astype(BF16)
    hc[...] = h32[...].astype(BF16)

    total = ndiff[...] + zst[0].astype(F32)
    for s in range(1, NZ):
        a = remote(zst.at[s, 0:48], zr.at[s, 0:48], s_mzs.at[s], s_mzr.at[s], zdev(s))
        b = remote(zst.at[s, 48:64], zr.at[s, 48:64], s_mrs.at[s], s_mrr.at[s], zdev(s))
        a.wait_recv()
        b.wait_recv()
        total = total + zr[s].astype(F32)
    total = total * coef[:, 0:1]
    err_i = mod[0, 2, 0:1, :] * total[0:RI]
    err_t = mod[1, 2, 0:1, :] * total[RI : RI + RT]
    errz[0] = jnp.concatenate([err_i, err_t], axis=0).astype(BF16)

    def send_e(i, to, who):
        return remote(errz.at[i], errz.at[to], s_ezs.at[to], s_ezr.at[to], who)

    send_e(0, 1, zdev(1)).start()
    send_e(0, 2, zdev(-1)).start()

    def err_chunk(i, _):
        @pl.when(i > 0)
        def _():
            send_e(i, i, zdev(1)).wait_recv()

        @pl.when(jnp.logical_and(i > 0, i < 6))
        def _():
            send_e(i, i + 2, zdev((i % 2) * 2 - 1)).start()

        full = errz[i].astype(F32)
        e32[pl.ds(pl.multiple_of(i * RI, 8), RI), :] = full[0:RI]
        e32[pl.ds(pl.multiple_of(IMG + i * RT, 8), RT), :] = full[RI : RI + RT]
        return 0

    lax.fori_loop(0, NZ, err_chunk, 0)
    ec[...] = e32[...].astype(BF16)

    def hg_block(q, _):
        lanes = pl.ds(pl.multiple_of(q * HQ, HQ), HQ)
        gi = dot(ec[0:IMG], W[2, :, lanes]).astype(BF16)
        gt = dot(ec[IMG:SEQ], W[3, :, lanes]).astype(BF16)
        for j in range(NJ):
            hgs[j, q, 0:IMG, :] = gi[:, j * HJ : (j + 1) * HJ]
            hgs[j, q, IMG:SEQ, :] = gt[:, j * HJ : (j + 1) * HJ]
        return 0

    lax.fori_loop(0, NX, hg_block, 0)

    def rs_hg(j, t):
        return remote(hgs.at[j, (x + t) % NX], hgr.at[j, t - 1], s_hgs.at[j, t - 1], s_hgr.at[j, t - 1], xdev(t))

    for j in range(NJ):
        for t in range(1, NX):
            rs_hg(j, t).start()

    turned = e32[...].T
    eT[...] = jnp.where(img_lane, turned, 0.0).astype(BF16)
    eTt[...] = jnp.where(txt_lane, turned[:, SEQ - 128 :], 0.0).astype(BF16)

    def gd_block(q, _):
        G[0, q] = dot(eT[...], hc[q]).astype(BF16)
        G[1, q] = dot(eTt[...], hc[q, SEQ - 128 :, :]).astype(BF16)
        return 0

    lax.fori_loop(0, NX, gd_block, 0)

    def cols(m, j):
        return pl.ds(0, HQ) if j is None else pl.ds(j * HJ, HJ)

    def core_cp(p, m, j, l):
        return remote(
            G.at[m, l * 2 + 1 - c, :, cols(m, j)], CR.at[m, l, :, cols(m, j)], s_cs.at[p, l], s_cr.at[p, l], core
        )

    def y_cp(p, m, j, t):
        yy = (y + t) % 4
        rows = pl.ds(pl.multiple_of((yy // 2) * ROWS, ROWS), ROWS)
        return remote(
            G.at[m, (yy % 2) * 2 + c, rows, cols(m, j)], YR.at[m, t - 1, :, cols(m, j)],
            s_ys.at[p, t - 1], s_yr.at[p, t - 1], ydev(t),
        )

    def after_core(p, m, j):
        for l in range(2):
            core_cp(p, m, j, l).wait_recv()
            G[m, l * 2 + c, :, cols(m, j)] = (
                G[m, l * 2 + c, :, cols(m, j)].astype(F32) + CR[m, l, :, cols(m, j)].astype(F32)
            ).astype(BF16)
        for t in range(1, 4):
            y_cp(p, m, j, t).start()

    for m in range(2):
        for l in range(2):
            core_cp(m, m, None, l).start()

    def pre_grad(j):
        for t in range(1, NX):
            rs_hg(j, t).wait_recv()
        g = hgs[j, x].astype(F32)
        for t in range(1, NX):
            g = g + hgr[j, t - 1].astype(F32)
        own = (g * gelu_slope(pre_c[:, j * HJ : (j + 1) * HJ])).astype(BF16)
        pg[j, x] = own
        for t in range(1, NX):
            ag_pg(j, t).start()

    def ag_pg(j, t):
        return remote(pg.at[j, x], pg.at[j, x], s_pgs.at[j, t - 1], s_pgr.at[j, t - 1], xdev(t))

    def ag_pg_in(j, t):
        f = (x + NX - t) % NX
        return remote(pg.at[j, f], pg.at[j, f], s_pgs.at[j, t - 1], s_pgr.at[j, t - 1], xdev(t))

    pre_grad(0)
    after_core(0, 0, None)
    after_core(1, 1, None)
    for j in range(1, NJ):
        pre_grad(j)

    for j in range(NJ):
        for t in range(1, NX):
            ag_pg_in(j, t).wait_recv()
        wide = jnp.concatenate([pg[j, q] for q in range(NX)], axis=1)
        gi = dot(uT[...], wide).astype(BF16)
        gt = dot(uTt[...], wide[SEQ - 128 :]).astype(BF16)
        for q in range(NX):
            G[2, q, :, j * HJ : (j + 1) * HJ] = gi[:, q * HJ : (q + 1) * HJ]
            G[3, q, :, j * HJ : (j + 1) * HJ] = gt[:, q * HJ : (q + 1) * HJ]
        for k in range(2):
            for l in range(2):
                core_cp(2 + 2 * j + k, 2 + k, j, l).start()
        for k in range(2):
            after_core(2 + 2 * j + k, 2 + k, j)

    mine = pl.ds(pl.multiple_of(hi * ROWS, ROWS), ROWS)

    def finish(p, m, j, out):
        for t in range(1, 4):
            y_cp(p, m, j, t).wait_recv()
        g = G[m, lo * 2 + c, mine, cols(m, j)].astype(F32)
        for t in range(3):
            g = g + YR[m, t, :, cols(m, j)].astype(F32)
        out[:, cols(m, j)] = g

    finish(0, 0, None, out_di)
    finish(1, 1, None, out_dt)
    for j in range(NJ):
        finish(2 + 2 * j, 2, j, out_ui)
        finish(3 + 2 * j, 3, j, out_ut)

    for m in range(4):
        w1[m].wait_send()
        w2[m].wait_send()
        w3a[m].wait_send()
        w3b[m].wait_send()

    def sent(i, _):
        @pl.when(i > 0)
        def _():
            a, b = send_z(i, i, zdev(1))
            a.wait_send()
            b.wait_send()
            send_e(i, i, zdev(1)).wait_send()
            mz_main(i).wait_send()
            mz_rest(i).wait_send()

        for t in range(1, NX):
            rs_img(i, t).wait_send()
            ag_img(i, t).wait_send()
        return 0

    lax.fori_loop(0, NZ, sent, 0)
    for t in range(1, NX):
        rs_txt(t).wait_send()
        ag_txt(t).wait_send()
        for j in range(NJ):
            rs_hg(j, t).wait_send()
            ag_pg(j, t).wait_send()
    parts = [(0, 0, None), (1, 1, None)] + [(2 + 2 * j + k, 2 + k, j) for j in range(NJ) for k in range(2)]
    for p, m, j in parts:
        for l in range(2):
            core_cp(p, m, j, l).wait_send()
        for t in range(1, 4):
            y_cp(p, m, j, t).wait_send()


def body(
    latent_image, latent_text, noise_image, noise_text, up_image, down_image, up_text, down_text,
    modulation, timesteps, skips, text_lengths,
):
    r = lax.axis_index("row")
    x, hi = r // 2, r % 2
    total_samples = timesteps.shape[0] * lax.axis_size("dp")
    t_s = lax.dynamic_index_in_dim(timesteps, hi, 0, False)
    t_g = t_s - lax.dynamic_index_in_dim(skips, hi, 0, False)
    length = lax.dynamic_index_in_dim(text_lengths, hi, 0, False)
    times = jnp.stack([t_s, t_g]).astype(F32)
    half = D // 2
    channel = x * CH + jnp.arange(CH)
    frequency = jnp.exp(-math.log(10000.0) * (channel % half).astype(F32) / half)
    angles = times[:, None] * frequency[None, :]
    features = jnp.where(x < NX // 2, jnp.cos(angles), jnp.sin(angles))
    table = lax.dynamic_slice_in_dim(modulation, x * CH, CH, 3)
    mod = table[:, :, 0][:, :, None, :] + table[:, :, 1][:, :, None, :] * features
    levels = times / STEPS
    weight = SEQ / math.sqrt(total_samples * SEQ) / (IMG + length).astype(F32)
    row = jnp.arange(RI + RT)
    position = lax.axis_index("col") * RT + row - RI
    coef = jnp.where(jnp.logical_or(row < RI, position < length), weight, 0.0)
    coef = jnp.broadcast_to(coef[:, None], (RI + RT, 128))

    any_ = pl.BlockSpec(memory_space=pl.ANY)
    vmem = pl.BlockSpec(memory_space=pltpu.VMEM)
    smem = pl.BlockSpec(memory_space=pltpu.SMEM)
    V = pltpu.VMEM
    dma = lambda *s: pltpu.SemaphoreType.DMA(s)
    np_ = 2 + 2 * NJ
    out = jax.ShapeDtypeStruct((ROWS, HQ), F32)
    gi, di, gt, dt = pl.pallas_call(
        kernel,
        out_shape=(out, out, out, out),
        in_specs=[any_] * 8 + [vmem, vmem, smem],
        out_specs=(vmem,) * 4,
        scratch_shapes=[
            V((RI, D), BF16), V((RT, D), BF16), V((RI, D), BF16), V((RT, D), BF16),
            V((4, CH, HB), BF16), V((NZ, 2 * RI, CH), BF16), V((NZ * 16, CH), BF16),
            V((RI + RT, CH), F32), V((SEQ, CH), F32),
            V((NZ, NX, 2 * RI, HQ), BF16), V((NX, 128, HQ), BF16),
            V((NZ, 3, 2 * RI, HQ), BF16), V((3, 128, HQ), BF16),
            V((NZ, NX, 2 * RI, HQ), BF16), V((NX, 128, HQ), BF16),
            V((SEQ, HQ), F32), V((NX, SEQ, HQ), F32), V((NX, SEQ, HQ), BF16),
            V((NZ, 64, CH), BF16), V((NZ, 16, CH), F32), V((NZ, 64, CH), BF16), V((NZ, 64, CH), BF16),
            V((SEQ, CH), F32), V((SEQ, CH), BF16),
            V((CH, SEQ), BF16), V((CH, SEQ), BF16), V((CH, 128), BF16), V((CH, 128), BF16),
            V((NJ, NX, SEQ, HJ), BF16), V((NJ, 3, SEQ, HJ), BF16), V((NJ, NX, SEQ, HJ), BF16),
            V((4, NX, CH, HQ), BF16), V((4, 2, CH, HQ), BF16), V((4, 3, ROWS, HQ), BF16),
            dma(4), dma(4), dma(4), dma(4), dma(4), dma(4), dma(4, 2), dma(4, 2),
            dma(NZ), dma(NZ), dma(NZ), dma(NZ),
            dma(9, 3), dma(9, 3), dma(9, 3), dma(9, 3), dma(NZ), dma(NZ), dma(NZ), dma(NZ), dma(NZ), dma(NZ),
            dma(NJ, 3), dma(NJ, 3), dma(NJ, 3), dma(NJ, 3), dma(np_, 2), dma(np_, 2), dma(np_, 3), dma(np_, 3),
        ],
        compiler_params=pltpu.CompilerParams(
            collective_id=0, has_side_effects=True, vmem_limit_bytes=60 * 1024 * 1024
        ),
    )(latent_image, latent_text, noise_image, noise_text, up_image, up_text, down_image, down_text, mod, coef, levels)
    return gi, di, gt, dt


def solution(mesh):
    placed = (
        P("dp", "col", None),
        P("dp", "col", None),
        P("dp", "col", None),
        P("dp", "col", None),
        P("row", "col"),
        P("row", "col"),
        P("row", "col"),
        P("row", "col"),
        P(),
        P("dp"),
        P("dp"),
        P("dp"),
    )
    grads = P("row", ("col", "dp"))
    return jax.shard_map(
        body, mesh=mesh, in_specs=placed, out_specs=(grads, grads, grads, grads), check_vma=False
    )
```

```python
import functools
import math

import jax
import jax.numpy as jnp
from jax import lax
from jax.experimental import pallas as pl
from jax.experimental.pallas import tpu as pltpu
from jax.sharding import PartitionSpec as P

D = 3072
FF = 12288
IMG = 448
TXT = 64
STEPS = 1000
SEQ = 512
SAMPLES = 8

NX = 4
NZ = 8
CH = D // NX
HB = FF // NZ
HQ = HB // NX
RI = IMG // NZ
RT = TXT // NZ
NJ = 3
HJ = HQ // NJ
ROWS = D // 8
QR = ROWS // 4
NP = 3
PR = QR // NP
HR = ROWS // 2

GELU_SCALE = 0.7978845608028654
GELU_CUBIC = 0.044715
NORM_EPS = 1e-06
MESH = pl.DeviceIdType.MESH
F32 = jnp.float32
BF16 = jnp.bfloat16


def gelu_tanh(values):
    inner = GELU_SCALE * (values + GELU_CUBIC * values * values * values)
    return 0.5 * values * (1.0 + jnp.tanh(inner))


def gelu_slope(values):
    inner = GELU_SCALE * (values + GELU_CUBIC * values * values * values)
    tangent = jnp.tanh(inner)
    return 0.5 * (1.0 + tangent) + 0.5 * values * (1.0 - tangent * tangent) * GELU_SCALE * (
        1.0 + 3.0 * GELU_CUBIC * values * values
    )


def dot(a, b):
    return jnp.dot(a, b, preferred_element_type=F32)


def dot_nt(a, b):
    return lax.dot_general(a, b, (((1,), (1,)), ((), ())), preferred_element_type=F32)


class Sum:
    def __init__(self, part, relay, got, ss, rs, pos, to, s):
        self.part, self.relay, self.got, self.ss, self.rs, self.pos, self.to, self.s = part, relay, got, ss, rs, pos, to, s

    @property
    def relayed(self):
        return remote(self.part((self.pos + 2) % 4), self.relay, self.ss(0), self.rs(0), self.to(self.s))

    @property
    def direct(self):
        return remote(self.part((self.pos - self.s + 4) % 4), self.got(0), self.ss(1), self.rs(1), self.to(-self.s))

    @property
    def joined(self):
        return remote(self.part((self.pos + self.s + 4) % 4), self.got(1), self.ss(2), self.rs(2), self.to(self.s))

    def join(self):
        self.relayed.wait_recv()
        joint = self.part((self.pos + self.s + 4) % 4)
        joint[...] = (joint[...].astype(F32) + self.relay[...].astype(F32)).astype(BF16)
        self.joined.start()

    def first(self):
        self.relayed.start()
        self.direct.start()

    def wait(self):
        self.direct.wait_recv()
        self.joined.wait_recv()

    def sent(self):
        self.relayed.wait_send()
        self.direct.wait_send()
        self.joined.wait_send()


class Gather:
    def __init__(self, slot, ss, rs, pos, to, s):
        self.slot, self.ss, self.rs, self.pos, self.to, self.s = slot, ss, rs, pos, to, s

    @property
    def plus(self):
        return remote(self.slot(self.pos), self.slot(self.pos), self.ss(0), self.rs(0), self.to(self.s))

    @property
    def minus(self):
        return remote(self.slot(self.pos), self.slot(self.pos), self.ss(1), self.rs(1), self.to(-self.s))

    @property
    def onward(self):
        back = self.slot((self.pos - self.s + 4) % 4)
        return remote(back, back, self.ss(2), self.rs(2), self.to(self.s))

    def first(self):
        self.plus.start()
        self.minus.start()

    def forward(self):
        self.plus.wait_recv()
        self.onward.start()

    def wait(self):
        self.minus.wait_recv()
        self.onward.wait_recv()

    def sent(self):
        self.plus.wait_send()
        self.minus.wait_send()
        self.onward.wait_send()


def remote(src, dst, ss, rs, who):
    return pltpu.make_async_remote_copy(
        src_ref=src, dst_ref=dst, send_sem=ss, recv_sem=rs, device_id=who, device_id_type=MESH
    )


def kernel(
    lat_i, lat_t, noi_i, noi_t, up_i, up_t, dn_i, dn_t, modulation, feats, timesteps, skips, lengths,
    out_ui, out_di, out_ut, out_dt,
    lbi, lbt, nbi, nbt, W, uimg, utxt, ndiff, mod, coef, u32,
    stg, stgt, rrs, rrst, hid, hidt, pre_c, h32, hc,
    zst, rem, zr, errz, e32, ec, uT, eT, uTt, eTt, hgs, hgr, pg, G, CR, YR,
    s_loc, s_wl, s_w1s, s_w1r, s_w2s, s_w2r, s_w3s, s_w3r,
    s_zis, s_zir, s_zts, s_ztr,
    s_rss, s_rsr, s_ags, s_agr, s_mzs, s_mzr, s_mrs, s_mrr, s_ezs, s_ezr,
    s_hgs, s_hgr, s_pgs, s_pgr, s_cs, s_cr, s_ys, s_yr,
):
    r = lax.axis_index("row")
    z = lax.axis_index("col")
    d = lax.axis_index("dp")
    x, hi, lo, c = r // 2, r % 2, d // 2, d % 2
    y = hi * 2 + lo

    def dev(x, hi, lo, c, z):
        return (x * 2 + hi, z, lo * 2 + c)

    def xdev(t):
        return dev((x + t + NX) % NX, hi, lo, c, z)

    def zdev(t):
        return dev(x, hi, lo, c, (z + t + NZ) % NZ)

    def ydev(t):
        yy = (y + t + 4) % 4
        return dev(x, yy // 2, yy % 2, c, z)

    core = dev(x, hi, lo, 1 - c, z)
    adj = dev(x, 1 - hi, 1 - lo, c, z)
    side = dev(x, hi, 1 - lo, c, z)

    bar = pltpu.get_barrier_semaphore()
    for t in range(1, NX):
        pl.semaphore_signal(bar, inc=1, device_id=xdev(t), device_id_type=MESH)
    for t in range(1, NZ):
        pl.semaphore_signal(bar, inc=1, device_id=zdev(t), device_id_type=MESH)
    for t in range(1, 4):
        pl.semaphore_signal(bar, inc=1, device_id=ydev(t), device_id_type=MESH)
    pl.semaphore_signal(bar, inc=1, device_id=core, device_id_type=MESH)

    reads = [
        pltpu.make_async_copy(lat_i.at[hi], lbi, s_loc.at[0]),
        pltpu.make_async_copy(lat_t.at[hi], lbt, s_loc.at[1]),
        pltpu.make_async_copy(noi_i.at[hi], nbi, s_loc.at[2]),
        pltpu.make_async_copy(noi_t.at[hi], nbt, s_loc.at[3]),
    ]
    for cp in reads:
        cp.start()
    weights = (up_i, up_t, dn_i, dn_t)
    wl = [
        pltpu.make_async_copy(
            weights[m], W.at[m, pl.ds(pl.multiple_of(hi * ROWS, ROWS), ROWS)], s_wl.at[m]
        )
        for m in range(4)
    ]

    def wrows(m, half, quarter, p):
        return W.at[m, pl.ds(pl.multiple_of(half * ROWS + quarter * QR + p * PR, PR), PR)]

    q_mine = lo * 2 + c
    q_side = (1 - lo) * 2 + c

    def w1(m, p):
        return remote(
            weights[m].at[pl.ds(pl.multiple_of(q_side * QR + p * PR, PR), PR)],
            wrows(m, hi, q_side, p), s_w1s.at[m, p], s_w1r.at[m, p], adj,
        )

    def w1in(m, p):
        rows = wrows(m, 1 - hi, q_mine, p)
        return remote(rows, rows, s_w1s.at[m, p], s_w1r.at[m, p], adj)

    def w2(m, p):
        rows = wrows(m, 1 - hi, q_mine, p)
        return remote(rows, rows, s_w2s.at[m, p], s_w2r.at[m, p], side)

    def w2in(m, p):
        rows = wrows(m, 1 - hi, q_side, p)
        return remote(rows, rows, s_w2s.at[m, p], s_w2r.at[m, p], side)

    def w3(m, p, k):
        rows = wrows(m, 1 - hi, q_side if k else q_mine, p)
        return remote(rows, rows, s_w3s.at[m, p, k], s_w3r.at[m, p, k], core)

    def w_step1(m):
        for p in range(NP):
            w1in(m, p).wait_recv()
            w2(m, p).start()
            w3(m, p, 0).start()

    def w_step2(m):
        for p in range(NP):
            w2in(m, p).wait_recv()
            w3(m, p, 1).start()

    def w_step3(m):
        wl[m].wait()
        for p in range(NP):
            w3(m, p, 0).wait_recv()
            w3(m, p, 1).wait_recv()

    for cp in wl:
        cp.start()
    lane0 = pl.multiple_of(x * CH, CH)
    own_lanes = pl.ds(lane0, CH)
    for k in range(2):
        for a in range(3):
            for b in range(2):
                mod[k, a, b : b + 1, :] = (
                    modulation[k, a, 0:1, own_lanes] + modulation[k, a, 1:2, own_lanes] * feats[b * 2 + hi, :, own_lanes]
                )
    t_s = timesteps[hi]
    t_g = t_s - skips[hi]
    levels = (t_s.astype(F32) * (1.0 / STEPS), t_g.astype(F32) * (1.0 / STEPS))
    length = lengths[hi]
    row = lax.broadcasted_iota(jnp.int32, (RI + RT, 128), 0)
    valid = jnp.logical_or(row < RI, row + (z * RT - RI) < length)
    count = jnp.full((RI + RT, 128), IMG, F32) + length.astype(F32)
    coef[...] = jnp.where(valid, SEQ / math.sqrt(SAMPLES * SEQ) / count, 0.0)
    for cp in reads:
        cp.wait()
    for latb, noib, rows, stream, base in ((lbi, nbi, RI, 0, 0), (lbt, nbt, RT, 1, RI)):
        lat_own = latb[:, own_lanes].astype(F32)
        noi_own = noib[:, own_lanes].astype(F32)
        owns = []
        us = []
        for b in range(2):
            level = levels[b]
            full = (1.0 - level) * latb[...].astype(F32) + level * noib[...].astype(F32)
            mean = jnp.mean(full, axis=-1, keepdims=True)
            cen = full - mean
            var = jnp.mean(cen * cen, axis=-1, keepdims=True)
            own = (1.0 - level) * lat_own + level * noi_own
            owns.append(own)
            normed = (own - mean) * lax.rsqrt(var + NORM_EPS)
            us.append(normed * (1.0 + mod[stream, 1, b : b + 1, :]) + mod[stream, 0, b : b + 1, :])
        ndiff[base : base + rows, :] = owns[0] - owns[1]
        both = jnp.concatenate(us, axis=0).astype(BF16)
        if stream == 0:
            uimg[0] = both
        else:
            utxt[0:16, :] = both

    pl.semaphore_wait(bar, 14)
    for m in range(4):
        for p in range(NP):
            w1(m, p).start()

    def send_z(i, to, who):
        a = remote(uimg.at[i], uimg.at[to], s_zis.at[to], s_zir.at[to], who)
        b = remote(
            utxt.at[pl.ds(pl.multiple_of(i * 16, 16), 16)],
            utxt.at[pl.ds(pl.multiple_of(to * 16, 16), 16)],
            s_zts.at[to], s_ztr.at[to], who,
        )
        return a, b

    for to, who in ((1, zdev(1)), (2, zdev(-1))):
        for cp in send_z(0, to, who):
            cp.start()

    w_step1(0)
    w_step2(0)
    w_step3(0)

    def sign(i):
        return 1 - 2 * (i % 2)

    def rs_img(i):
        return Sum(
            lambda q: stg.at[i, q], rrs.at[i, 2], lambda k: rrs.at[i, k],
            lambda k: s_rss.at[i, k], lambda k: s_rsr.at[i, k], x, xdev, sign(i),
        )

    def ag_img(i):
        return Gather(lambda q: hid.at[i, q], lambda k: s_ags.at[i, k], lambda k: s_agr.at[i, k], x, xdev, sign(i))

    def rs_txt(h):
        rows = pl.ds(h * 64, 64)
        return Sum(
            lambda q: stgt.at[q, rows], rrst.at[2, rows], lambda k: rrst.at[k, rows],
            lambda k: s_rss.at[8 + h, k], lambda k: s_rsr.at[8 + h, k], x, xdev, 1 - 2 * h,
        )

    def ag_txt(h):
        rows = pl.ds(h * 64, 64)
        return Gather(
            lambda q: hidt.at[q, rows], lambda k: s_ags.at[8 + h, k], lambda k: s_agr.at[8 + h, k], x, xdev, 1 - 2 * h
        )

    def up_chunk(i):
        @pl.when(i > 0)
        def _():
            a, b = send_z(i, i, zdev(1))
            a.wait_recv()
            b.wait_recv()

        @pl.when(jnp.logical_and(i > 0, i < 6))
        def _():
            for cp in send_z(i, i + 2, zdev((i % 2) * 2 - 1)):
                cp.start()

        u = uimg[i]
        for q in range(NX):
            stg[i, q] = dot(u, W[0, :, q * HQ : (q + 1) * HQ]).astype(BF16)
        rs_img(i).first()

    def at(k, step, do, *args):
        @pl.when(k == step)
        def _():
            do(*args)

    def up_step(k, _):
        @pl.when(k < NZ)
        def _():
            up_chunk(k)

        @pl.when(k >= 2)
        def _():
            rs_img(k - 2).join()

        at(k, 1, w_step1, 1)
        at(k, 3, w_step1, 2)
        at(k, 4, w_step2, 1)
        at(k, 6, w_step1, 3)
        at(k, 7, w_step2, 2)
        return 0

    lax.fori_loop(0, NZ + 2, up_step, 0)

    w_step3(1)
    for q in range(NX):
        stgt[q] = dot(utxt[...], W[1, :, q * HQ : (q + 1) * HQ]).astype(BF16)
    for h in range(2):
        rs_txt(h).first()
    w_step2(3)

    def pack_u(i, _):
        u32[pl.ds(pl.multiple_of(i * RI, 8), RI), :] = uimg[i].astype(F32)[0:RI]
        u32[pl.ds(pl.multiple_of(IMG + i * RT, 8), RT), :] = utxt[
            pl.ds(pl.multiple_of(i * 16, 16), 16), :
        ].astype(F32)[0:RT]
        return 0

    lax.fori_loop(0, NZ, pack_u, 0)

    def act_chunk(i):
        rs_img(i).wait()
        pre = stg[i, x].astype(F32) + rrs[i, 0].astype(F32) + rrs[i, 1].astype(F32)
        pre_c[pl.ds(pl.multiple_of(i * RI, 8), RI), :] = pre[0:RI]
        hid[i, x] = gelu_tanh(pre).astype(BF16)
        ag_img(i).first()

    def join_text():
        for h in range(2):
            rs_txt(h).join()

    def act_text():
        for h in range(2):
            rs_txt(h).wait()
        pre = stgt[x].astype(F32) + rrst[0].astype(F32) + rrst[1].astype(F32)
        for i in range(NZ):
            pre_c[IMG + i * RT : IMG + (i + 1) * RT, :] = pre[i * 16 : i * 16 + RT]
        hidt[x] = gelu_tanh(pre).astype(BF16)
        for h in range(2):
            ag_txt(h).first()

    def pass_text():
        for h in range(2):
            ag_txt(h).forward()

    def zslot(i):
        half = (i + 1) // 2
        return (NZ + half - 2 * half * (i % 2)) % NZ

    def mz_main(i):
        s = zslot(i)
        return remote(zst.at[i, 0:48], zr.at[s, 0:48], s_mzs.at[i], s_mzr.at[s], zdev(s))

    def mz_rest(i):
        s = zslot(i)
        return remote(zst.at[i, 48:64], zr.at[s, 48:64], s_mrs.at[i], s_mrr.at[s], zdev(s))

    def down_chunk(i):
        ag_img(i).wait()
        out = dot_nt(hid[i, 0], W[2, :, 0:HQ])
        for q in range(1, NX):
            out = out + dot_nt(hid[i, q], W[2, :, q * HQ : (q + 1) * HQ])
        diff = mod[0, 2, 0:1, :] * out[0:RI] - mod[0, 2, 1:2, :] * out[RI : 2 * RI]
        zst[i, 0:48, :] = diff[0:48].astype(BF16)
        rem[i, 0:8, :] = diff[48:56]

        @pl.when(i > 0)
        def _():
            mz_main(i).start()

        for q in range(NX):
            h32[q, pl.ds(pl.multiple_of(i * RI, 8), RI), :] = hid[i, q].astype(F32)[0:RI]

    def rest_chunk(i, _):
        zst[i, 48:64, :] = rem[i].astype(BF16)

        @pl.when(i > 0)
        def _():
            mz_rest(i).start()

        return 0

    def down_text():
        for h in range(2):
            ag_txt(h).wait()
        out = dot_nt(hidt[0], W[3, :, 0:HQ])
        for q in range(1, NX):
            out = out + dot_nt(hidt[q], W[3, :, q * HQ : (q + 1) * HQ])
        for i in range(NZ):
            rem[i, 8:16, :] = (
                mod[1, 2, 0:1, :] * out[i * 16 : i * 16 + RT] - mod[1, 2, 1:2, :] * out[i * 16 + RT : (i + 1) * 16]
            )
        for q in range(NX):
            full = hidt[q].astype(F32)
            for i in range(NZ):
                h32[q, IMG + i * RT : IMG + (i + 1) * RT, :] = full[i * 16 : i * 16 + RT]

    def down_rest():
        w_step3(3)
        down_text()
        lax.fori_loop(3, NZ, rest_chunk, 0)

    def order(k):
        return k + 3 + (k // 5) * (4 - 2 * k)

    def hidden_step(k, _):
        @pl.when(k < NZ)
        def _():
            act_chunk(order(k))

        at(k, 2, join_text)
        at(k, 4, act_text)

        @pl.when(jnp.logical_and(k >= 1, k <= NZ))
        def _():
            ag_img(order(k - 1)).forward()

        at(k, 6, pass_text)
        at(k, 3, w_step3, 2)

        @pl.when(k >= 3)
        def _():
            down_chunk(order(k - 3))

        at(k, 7, down_rest)

        @pl.when(k >= 8)
        def _():
            rest_chunk(order(k - 3), 0)

        return 0

    lax.fori_loop(0, NZ + 3, hidden_step, 0)

    img_lane = lax.broadcasted_iota(jnp.int32, (CH, SEQ), 1) < IMG
    txt_lane = lax.broadcasted_iota(jnp.int32, (CH, 128), 1) >= 64
    turned = u32[...].T
    uT[...] = jnp.where(img_lane, turned, 0.0).astype(BF16)
    uTt[...] = jnp.where(txt_lane, turned[:, SEQ - 128 :], 0.0).astype(BF16)
    hc[...] = h32[...].astype(BF16)

    total = ndiff[...] + zst[0].astype(F32)
    for s in range(1, NZ):
        a = remote(zst.at[s, 0:48], zr.at[s, 0:48], s_mzs.at[s], s_mzr.at[s], zdev(s))
        b = remote(zst.at[s, 48:64], zr.at[s, 48:64], s_mrs.at[s], s_mrr.at[s], zdev(s))
        a.wait_recv()
        b.wait_recv()
        total = total + zr[s].astype(F32)
    total = total * coef[:, 0:1]
    err_i = mod[0, 2, 0:1, :] * total[0:RI]
    err_t = mod[1, 2, 0:1, :] * total[RI : RI + RT]
    errz[0] = jnp.concatenate([err_i, err_t], axis=0).astype(BF16)

    def send_e(i, to, who):
        return remote(errz.at[i], errz.at[to], s_ezs.at[to], s_ezr.at[to], who)

    send_e(0, 1, zdev(1)).start()
    send_e(0, 2, zdev(-1)).start()

    def err_chunk(i, _):
        @pl.when(i > 0)
        def _():
            send_e(i, i, zdev(1)).wait_recv()

        @pl.when(jnp.logical_and(i > 0, i < 6))
        def _():
            send_e(i, i + 2, zdev((i % 2) * 2 - 1)).start()

        full = errz[i].astype(F32)
        e32[pl.ds(pl.multiple_of(i * RI, 8), RI), :] = full[0:RI]
        e32[pl.ds(pl.multiple_of(IMG + i * RT, 8), RT), :] = full[RI : RI + RT]
        return 0

    lax.fori_loop(0, NZ, err_chunk, 0)
    ec[...] = e32[...].astype(BF16)

    def hg_block(q, _):
        lanes = pl.ds(pl.multiple_of(q * HQ, HQ), HQ)
        gi = dot(ec[0:IMG], W[2, :, lanes]).astype(BF16)
        gt = dot(ec[IMG:SEQ], W[3, :, lanes]).astype(BF16)
        for j in range(NJ):
            hgs[j, q, 0:IMG, :] = gi[:, j * HJ : (j + 1) * HJ]
            hgs[j, q, IMG:SEQ, :] = gt[:, j * HJ : (j + 1) * HJ]
        return 0

    lax.fori_loop(0, NX, hg_block, 0)

    def rs_hg(j, h):
        rows = pl.ds(h * 256, 256)
        return Sum(
            lambda q: hgs.at[j, q, rows], hgr.at[j, 2, rows], lambda k: hgr.at[j, k, rows],
            lambda k: s_hgs.at[j, h, k], lambda k: s_hgr.at[j, h, k], x, xdev, 1 - 2 * h,
        )

    def ag_pg(j, h):
        rows = pl.ds(h * 256, 256)
        return Gather(
            lambda q: pg.at[j, q, rows], lambda k: s_pgs.at[j, h, k], lambda k: s_pgr.at[j, h, k], x, xdev, 1 - 2 * h
        )

    units = [(j, h) for j in range(NJ) for h in range(2)]
    for j, h in units:
        rs_hg(j, h).relayed.start()
    for j, h in units:
        rs_hg(j, h).direct.start()

    turned = e32[...].T
    eT[...] = jnp.where(img_lane, turned, 0.0).astype(BF16)
    eTt[...] = jnp.where(txt_lane, turned[:, SEQ - 128 :], 0.0).astype(BF16)

    def gd_block(q, _):
        G[0, q] = dot(eT[...], hc[q]).astype(BF16)
        G[1, q] = dot(eTt[...], hc[q, SEQ - 128 :, :]).astype(BF16)
        return 0

    lax.fori_loop(0, NX, gd_block, 0)

    def cols(m, j):
        return pl.ds(0, HQ) if j is None else pl.ds(j * HJ, HJ)

    def core_cp(p, m, j, l):
        return remote(
            G.at[m, l * 2 + 1 - c, :, cols(m, j)], CR.at[m, l, :, cols(m, j)], s_cs.at[p, l], s_cr.at[p, l], core
        )

    def rs_y(p, m, j, h):
        rows = pl.ds(h * HR, HR)
        return Sum(
            lambda yy: G.at[
                m, (yy % 2) * 2 + c, pl.ds(pl.multiple_of((yy // 2) * ROWS + h * HR, HR), HR), cols(m, j)
            ],
            YR.at[m, 2, rows, cols(m, j)], lambda k: YR.at[m, k, rows, cols(m, j)],
            lambda k: s_ys.at[p, h, k], lambda k: s_yr.at[p, h, k], y, ydev, 1 - 2 * h,
        )

    def join_y(p, m, j):
        for h in range(2):
            rs_y(p, m, j, h).join()

    def after_core(p, m, j):
        for l in range(2):
            core_cp(p, m, j, l).wait_recv()
            G[m, l * 2 + c, :, cols(m, j)] = (
                G[m, l * 2 + c, :, cols(m, j)].astype(F32) + CR[m, l, :, cols(m, j)].astype(F32)
            ).astype(BF16)
        for h in range(2):
            rs_y(p, m, j, h).relayed.start()
        for h in range(2):
            rs_y(p, m, j, h).direct.start()

    for m in range(2):
        for l in range(2):
            core_cp(m, m, None, l).start()

    def pre_grad(j):
        for h in range(2):
            rs_hg(j, h).wait()
        g = hgs[j, x].astype(F32) + hgr[j, 0].astype(F32) + hgr[j, 1].astype(F32)
        pg[j, x] = (g * gelu_slope(pre_c[:, j * HJ : (j + 1) * HJ])).astype(BF16)
        for h in range(2):
            ag_pg(j, h).first()

    def pass_pg(j):
        for h in range(2):
            ag_pg(j, h).forward()

    for j, h in units:
        rs_hg(j, h).join()
    after_core(0, 0, None)
    after_core(1, 1, None)
    pre_grad(0)
    pre_grad(1)
    pass_pg(0)
    join_y(0, 0, None)
    pre_grad(2)
    pass_pg(1)
    join_y(1, 1, None)
    pass_pg(2)

    for j in range(NJ):
        for h in range(2):
            ag_pg(j, h).wait()
        wide = jnp.concatenate([pg[j, q] for q in range(NX)], axis=1)
        gi = dot(uT[...], wide).astype(BF16)
        gt = dot(uTt[...], wide[SEQ - 128 :]).astype(BF16)
        for q in range(NX):
            G[2, q, :, j * HJ : (j + 1) * HJ] = gi[:, q * HJ : (q + 1) * HJ]
            G[3, q, :, j * HJ : (j + 1) * HJ] = gt[:, q * HJ : (q + 1) * HJ]
        for k in range(2):
            for l in range(2):
                core_cp(2 + 2 * j + k, 2 + k, j, l).start()
        for k in range(2):
            after_core(2 + 2 * j + k, 2 + k, j)
        if j > 0:
            for k in range(2):
                join_y(2 * j + k, 2 + k, j - 1)
    for k in range(2):
        join_y(2 * NJ + k, 2 + k, NJ - 1)

    mine = pl.ds(pl.multiple_of(hi * ROWS, ROWS), ROWS)

    def finish(p, m, j, out):
        for h in range(2):
            rs_y(p, m, j, h).wait()
        g = G[m, lo * 2 + c, mine, cols(m, j)].astype(F32)
        for k in range(2):
            g = g + YR[m, k, :, cols(m, j)].astype(F32)
        out[:, cols(m, j)] = g

    finish(0, 0, None, out_di)
    finish(1, 1, None, out_dt)
    for j in range(NJ):
        finish(2 + 2 * j, 2, j, out_ui)
        finish(3 + 2 * j, 3, j, out_ut)

    for m in range(4):
        for p in range(NP):
            w1(m, p).wait_send()
            w2(m, p).wait_send()
            w3(m, p, 0).wait_send()
            w3(m, p, 1).wait_send()

    def sent(i, _):
        @pl.when(i > 0)
        def _():
            a, b = send_z(i, i, zdev(1))
            a.wait_send()
            b.wait_send()
            send_e(i, i, zdev(1)).wait_send()
            mz_main(i).wait_send()
            mz_rest(i).wait_send()

        rs_img(i).sent()
        ag_img(i).sent()
        return 0

    lax.fori_loop(0, NZ, sent, 0)
    for h in range(2):
        rs_txt(h).sent()
        ag_txt(h).sent()
    for j, h in units:
        rs_hg(j, h).sent()
        ag_pg(j, h).sent()
    parts = [(0, 0, None), (1, 1, None)] + [(2 + 2 * j + k, 2 + k, j) for j in range(NJ) for k in range(2)]
    for p, m, j in parts:
        for l in range(2):
            core_cp(p, m, j, l).wait_send()
        for h in range(2):
            rs_y(p, m, j, h).sent()


def widen(a, b, c, d, oa, ob, oc, od):
    for src, dst in ((a, oa), (b, ob), (c, oc), (d, od)):
        dst[...] = src[...]


def body(
    latent_image, latent_text, noise_image, noise_text, up_image, down_image, up_text, down_text,
    modulation, timesteps, skips, text_lengths,
):
    half = D // 2
    frequency = jnp.exp(-math.log(10000.0) * jnp.arange(half).astype(F32) / half)
    times = jnp.concatenate([timesteps, timesteps - skips]).astype(F32)
    angles = times[:, None] * frequency[None, :]
    feats = jnp.concatenate([jnp.cos(angles), jnp.sin(angles)], axis=1)[:, None, :]

    any_ = pl.BlockSpec(memory_space=pl.ANY)
    vmem = pl.BlockSpec(memory_space=pltpu.VMEM)
    smem = pl.BlockSpec(memory_space=pltpu.SMEM)
    V = pltpu.VMEM
    dma = lambda *s: pltpu.SemaphoreType.DMA(s)
    parts = 2 + 2 * NJ
    out = jax.ShapeDtypeStruct((ROWS, HQ), F32)
    grads = pl.pallas_call(
        kernel,
        out_shape=(out, out, out, out),
        in_specs=[any_] * 8 + [vmem, vmem, smem, smem, smem],
        out_specs=(vmem,) * 4,
        scratch_shapes=[
            V((RI, D), BF16), V((RT, D), BF16), V((RI, D), BF16), V((RT, D), BF16),
            V((4, CH, HB), BF16), V((NZ, 2 * RI, CH), BF16), V((NZ * 16, CH), BF16),
            V((RI + RT, CH), F32), V((2, 3, 2, CH), F32), V((RI + RT, 128), F32), V((SEQ, CH), F32),
            V((NZ, NX, 2 * RI, HQ), BF16), V((NX, 128, HQ), BF16),
            V((NZ, 3, 2 * RI, HQ), BF16), V((3, 128, HQ), BF16),
            V((NZ, NX, 2 * RI, HQ), BF16), V((NX, 128, HQ), BF16),
            V((SEQ, HQ), F32), V((NX, SEQ, HQ), F32), V((NX, SEQ, HQ), BF16),
            V((NZ, 64, CH), BF16), V((NZ, 16, CH), F32), V((NZ, 64, CH), BF16), V((NZ, 64, CH), BF16),
            V((SEQ, CH), F32), V((SEQ, CH), BF16),
            V((CH, SEQ), BF16), V((CH, SEQ), BF16), V((CH, 128), BF16), V((CH, 128), BF16),
            V((NJ, NX, SEQ, HJ), BF16), V((NJ, 3, SEQ, HJ), BF16), V((NJ, NX, SEQ, HJ), BF16),
            V((4, NX, CH, HQ), BF16), V((4, 2, CH, HQ), BF16), V((4, 3, ROWS, HQ), BF16),
            dma(4), dma(4), dma(4, NP), dma(4, NP), dma(4, NP), dma(4, NP), dma(4, NP, 2), dma(4, NP, 2),
            dma(NZ), dma(NZ), dma(NZ), dma(NZ),
            dma(10, 3), dma(10, 3), dma(10, 3), dma(10, 3), dma(NZ), dma(NZ), dma(NZ), dma(NZ), dma(NZ), dma(NZ),
            dma(NJ, 2, 3), dma(NJ, 2, 3), dma(NJ, 2, 3), dma(NJ, 2, 3), dma(parts, 2), dma(parts, 2), dma(parts, 2, 3), dma(parts, 2, 3),
        ],
        compiler_params=pltpu.CompilerParams(
            collective_id=0, has_side_effects=True, vmem_limit_bytes=60 * 1024 * 1024
        ),
    )(
        latent_image, latent_text, noise_image, noise_text, up_image, up_text, down_image, down_text,
        modulation, feats, timesteps, skips, text_lengths,
    )
    return pl.pallas_call(
        widen, out_shape=(out, out, out, out), in_specs=[vmem] * 4, out_specs=(vmem,) * 4,
    )(*grads)


def solution(mesh):
    placed = (
        P("dp", "col", None),
        P("dp", "col", None),
        P("dp", "col", None),
        P("dp", "col", None),
        P("row", "col"),
        P("row", "col"),
        P("row", "col"),
        P("row", "col"),
        P(),
        P("dp"),
        P("dp"),
        P("dp"),
    )
    grads = P("row", ("col", "dp"))
    return jax.shard_map(
        body, mesh=mesh, in_specs=placed, out_specs=(grads, grads, grads, grads), check_vma=False
    )
```

```python
import functools
import math

import jax
import jax.numpy as jnp
from jax import lax
from jax.experimental import pallas as pl
from jax.experimental.pallas import tpu as pltpu
from jax.sharding import PartitionSpec as P

D = 3072
FF = 12288
IMG = 448
TXT = 64
STEPS = 1000
SEQ = 512
SAMPLES = 8

NX = 4
NZ = 8
CH = D // NX
HB = FF // NZ
HQ = HB // NX
RI = IMG // NZ
RT = TXT // NZ
RC = RI + RT
NJ = 3
HJ = HQ // NJ
ROWS = D // 8
QR = ROWS // 4
NP = 3
PR = QR // NP
HR = ROWS // 2

GELU_SCALE = 0.7978845608028654
GELU_CUBIC = 0.044715
NORM_EPS = 1e-06
MESH = pl.DeviceIdType.MESH
F32 = jnp.float32
BF16 = jnp.bfloat16


def gelu_tanh(values):
    inner = GELU_SCALE * (values + GELU_CUBIC * values * values * values)
    return 0.5 * values * (1.0 + jnp.tanh(inner))


def gelu_slope(values):
    inner = GELU_SCALE * (values + GELU_CUBIC * values * values * values)
    tangent = jnp.tanh(inner)
    return 0.5 * (1.0 + tangent) + 0.5 * values * (1.0 - tangent * tangent) * GELU_SCALE * (
        1.0 + 3.0 * GELU_CUBIC * values * values
    )


def dot(a, b):
    return jnp.dot(a, b, preferred_element_type=F32)


def dot_nt(a, b):
    return lax.dot_general(a, b, (((1,), (1,)), ((), ())), preferred_element_type=F32)


class Sum:
    def __init__(self, part, relay, got, ss, rs, pos, to, s):
        self.part, self.relay, self.got, self.ss, self.rs, self.pos, self.to, self.s = part, relay, got, ss, rs, pos, to, s

    @property
    def relayed(self):
        return remote(self.part((self.pos + 2) % 4), self.relay, self.ss(0), self.rs(0), self.to(self.s))

    @property
    def direct(self):
        return remote(self.part((self.pos - self.s + 4) % 4), self.got(0), self.ss(1), self.rs(1), self.to(-self.s))

    @property
    def joined(self):
        return remote(self.part((self.pos + self.s + 4) % 4), self.got(1), self.ss(2), self.rs(2), self.to(self.s))

    def join(self):
        self.relayed.wait_recv()
        joint = self.part((self.pos + self.s + 4) % 4)
        joint[...] = (joint[...].astype(F32) + self.relay[...].astype(F32)).astype(BF16)
        self.joined.start()

    def first(self):
        self.relayed.start()
        self.direct.start()

    def wait(self):
        self.direct.wait_recv()
        self.joined.wait_recv()

    def sent(self):
        self.relayed.wait_send()
        self.direct.wait_send()
        self.joined.wait_send()


class Gather:
    def __init__(self, slot, ss, rs, pos, to, s):
        self.slot, self.ss, self.rs, self.pos, self.to, self.s = slot, ss, rs, pos, to, s

    @property
    def plus(self):
        return remote(self.slot(self.pos), self.slot(self.pos), self.ss(0), self.rs(0), self.to(self.s))

    @property
    def minus(self):
        return remote(self.slot(self.pos), self.slot(self.pos), self.ss(1), self.rs(1), self.to(-self.s))

    @property
    def onward(self):
        back = self.slot((self.pos - self.s + 4) % 4)
        return remote(back, back, self.ss(2), self.rs(2), self.to(self.s))

    def first(self):
        self.plus.start()
        self.minus.start()

    def forward(self):
        self.plus.wait_recv()
        self.onward.start()

    def wait(self):
        self.minus.wait_recv()
        self.onward.wait_recv()

    def sent(self):
        self.plus.wait_send()
        self.minus.wait_send()
        self.onward.wait_send()


def remote(src, dst, ss, rs, who):
    return pltpu.make_async_remote_copy(
        src_ref=src, dst_ref=dst, send_sem=ss, recv_sem=rs, device_id=who, device_id_type=MESH
    )


def kernel(
    lat_i, lat_t, noi_i, noi_t, up_i, up_t, dn_i, dn_t, modulation, feats, timesteps, skips, lengths,
    out_ui, out_di, out_ut, out_dt,
    lbi, lbt, nbi, nbt, W, uimg, utxt, ndiff, mod, coef, u32,
    stg, stgt, rrs, rrst, hid, hidt, pre_c, h32, hc,
    zst, rem, zr, errz, t32, uT, eT, hgs, hgr, pg, G, CR, YR, TS, TA, OB,
    s_loc, s_wl, s_w1s, s_w1r, s_w2s, s_w2r, s_w3s, s_w3r,
    s_zis, s_zir, s_zts, s_ztr,
    s_rss, s_rsr, s_ags, s_agr, s_mzs, s_mzr, s_mrs, s_mrr, s_ezs, s_ezr,
    s_hgs, s_hgr, s_pgs, s_pgr, s_cs, s_cr, s_ys, s_yr, s_ts, s_tr, s_out,
):
    r = lax.axis_index("row")
    z = lax.axis_index("col")
    d = lax.axis_index("dp")
    x, hi, lo, c = r // 2, r % 2, d // 2, d % 2
    y = hi * 2 + lo

    def dev(x, hi, lo, c, z):
        return (x * 2 + hi, z, lo * 2 + c)

    def xdev(t):
        return dev((x + t + NX) % NX, hi, lo, c, z)

    def zdev(t):
        return dev(x, hi, lo, c, (z + t + NZ) % NZ)

    def ydev(t):
        yy = (y + t + 4) % 4
        return dev(x, yy // 2, yy % 2, c, z)

    def tdev(t, k):
        yy = (y + t) % 4
        return dev(x, yy // 2, yy % 2, c + k - 2 * c * k, z)

    core = dev(x, hi, lo, 1 - c, z)
    adj = dev(x, 1 - hi, 1 - lo, c, z)
    side = dev(x, hi, 1 - lo, c, z)

    bar = pltpu.get_barrier_semaphore()
    for t in range(1, NX):
        pl.semaphore_signal(bar, inc=1, device_id=xdev(t), device_id_type=MESH)
    for t in range(1, NZ):
        pl.semaphore_signal(bar, inc=1, device_id=zdev(t), device_id_type=MESH)
    others = [(t, k) for t in range(4) for k in range(2) if t or k]
    for t, k in others:
        pl.semaphore_signal(bar, inc=1, device_id=tdev(t, k), device_id_type=MESH)

    reads = [
        pltpu.make_async_copy(lat_i.at[hi], lbi, s_loc.at[0]),
        pltpu.make_async_copy(lat_t.at[hi], lbt, s_loc.at[1]),
        pltpu.make_async_copy(noi_i.at[hi], nbi, s_loc.at[2]),
        pltpu.make_async_copy(noi_t.at[hi], nbt, s_loc.at[3]),
    ]
    for cp in reads:
        cp.start()
    weights = (up_i, up_t, dn_i, dn_t)
    wl = [
        pltpu.make_async_copy(
            weights[m], W.at[m, pl.ds(pl.multiple_of(hi * ROWS, ROWS), ROWS)], s_wl.at[m]
        )
        for m in range(4)
    ]

    def wrows(m, half, quarter, p):
        return W.at[m, pl.ds(pl.multiple_of(half * ROWS + quarter * QR + p * PR, PR), PR)]

    q_mine = lo * 2 + c
    q_side = (1 - lo) * 2 + c

    def w1(m, p):
        return remote(
            weights[m].at[pl.ds(pl.multiple_of(q_side * QR + p * PR, PR), PR)],
            wrows(m, hi, q_side, p), s_w1s.at[m, p], s_w1r.at[m, p], adj,
        )

    def w1in(m, p):
        rows = wrows(m, 1 - hi, q_mine, p)
        return remote(rows, rows, s_w1s.at[m, p], s_w1r.at[m, p], adj)

    def w2(m, p):
        rows = wrows(m, 1 - hi, q_mine, p)
        return remote(rows, rows, s_w2s.at[m, p], s_w2r.at[m, p], side)

    def w2in(m, p):
        rows = wrows(m, 1 - hi, q_side, p)
        return remote(rows, rows, s_w2s.at[m, p], s_w2r.at[m, p], side)

    def w3(m, p, k):
        rows = wrows(m, 1 - hi, q_side if k else q_mine, p)
        return remote(rows, rows, s_w3s.at[m, p, k], s_w3r.at[m, p, k], core)

    def w_step1(m):
        for p in range(NP):
            w1in(m, p).wait_recv()
            w2(m, p).start()
            w3(m, p, 0).start()

    def w_step2(m):
        for p in range(NP):
            w2in(m, p).wait_recv()
            w3(m, p, 1).start()

    def w_step3(m):
        wl[m].wait()
        for p in range(NP):
            w3(m, p, 0).wait_recv()
            w3(m, p, 1).wait_recv()

    for cp in wl:
        cp.start()
    lane0 = pl.multiple_of(x * CH, CH)
    own_lanes = pl.ds(lane0, CH)
    for k in range(2):
        for a in range(3):
            for b in range(2):
                mod[k, a, b : b + 1, :] = (
                    modulation[k, a, 0:1, own_lanes] + modulation[k, a, 1:2, own_lanes] * feats[b * 2 + hi, :, own_lanes]
                )
    t_s = timesteps[hi]
    t_g = t_s - skips[hi]
    levels = (t_s.astype(F32) * (1.0 / STEPS), t_g.astype(F32) * (1.0 / STEPS))
    length = lengths[hi]
    row = lax.broadcasted_iota(jnp.int32, (RI + RT, 128), 0)
    valid = jnp.logical_or(row < RI, row + (z * RT - RI) < length)
    count = jnp.full((RI + RT, 128), IMG, F32) + length.astype(F32)
    coef[...] = jnp.where(valid, SEQ / math.sqrt(SAMPLES * SEQ) / count, 0.0)
    for cp in reads:
        cp.wait()
    for latb, noib, rows, stream, base in ((lbi, nbi, RI, 0, 0), (lbt, nbt, RT, 1, RI)):
        lat_own = latb[:, own_lanes].astype(F32)
        noi_own = noib[:, own_lanes].astype(F32)
        owns = []
        us = []
        for b in range(2):
            level = levels[b]
            full = (1.0 - level) * latb[...].astype(F32) + level * noib[...].astype(F32)
            mean = jnp.mean(full, axis=-1, keepdims=True)
            cen = full - mean
            var = jnp.mean(cen * cen, axis=-1, keepdims=True)
            own = (1.0 - level) * lat_own + level * noi_own
            owns.append(own)
            normed = (own - mean) * lax.rsqrt(var + NORM_EPS)
            us.append(normed * (1.0 + mod[stream, 1, b : b + 1, :]) + mod[stream, 0, b : b + 1, :])
        ndiff[base : base + rows, :] = owns[0] - owns[1]
        both = jnp.concatenate(us, axis=0).astype(BF16)
        if stream == 0:
            uimg[0] = both
        else:
            utxt[0:16, :] = both

    pl.semaphore_wait(bar, 17)
    for p in range(NP):
        w1(0, p).start()

    def send_z(i, to, who):
        a = remote(uimg.at[i], uimg.at[to], s_zis.at[to], s_zir.at[to], who)
        b = remote(
            utxt.at[pl.ds(pl.multiple_of(i * 16, 16), 16)],
            utxt.at[pl.ds(pl.multiple_of(to * 16, 16), 16)],
            s_zts.at[to], s_ztr.at[to], who,
        )
        return a, b

    for to, who in ((1, zdev(1)), (2, zdev(-1))):
        for cp in send_z(0, to, who):
            cp.start()

    def z_pass(i):
        a, b = send_z(i, i, zdev(1))
        a.wait_recv()
        b.wait_recv()
        if i < 6:
            for cp in send_z(i, i + 2, zdev((i % 2) * 2 - 1)):
                cp.start()

    w_step1(0)
    for m in range(1, 4):
        for p in range(NP):
            w1(m, p).start()
    z_pass(1)
    z_pass(2)
    w_step2(0)
    w_step3(0)

    def sign(i):
        return 1 - 2 * (i % 2)

    def rs_img(i):
        return Sum(
            lambda q: stg.at[i, q], rrs.at[i, 2], lambda k: rrs.at[i, k],
            lambda k: s_rss.at[i, k], lambda k: s_rsr.at[i, k], x, xdev, sign(i),
        )

    def ag_img(i):
        return Gather(lambda q: hid.at[i, q], lambda k: s_ags.at[i, k], lambda k: s_agr.at[i, k], x, xdev, sign(i))

    def rs_txt(h):
        rows = pl.ds(h * 64, 64)
        return Sum(
            lambda q: stgt.at[q, rows], rrst.at[2, rows], lambda k: rrst.at[k, rows],
            lambda k: s_rss.at[8 + h, k], lambda k: s_rsr.at[8 + h, k], x, xdev, 1 - 2 * h,
        )

    def ag_txt(h):
        rows = pl.ds(h * 64, 64)
        return Gather(
            lambda q: hidt.at[q, rows], lambda k: s_ags.at[8 + h, k], lambda k: s_agr.at[8 + h, k], x, xdev, 1 - 2 * h
        )

    def up_chunk(i):
        @pl.when(i > 2)
        def _():
            a, b = send_z(i, i, zdev(1))
            a.wait_recv()
            b.wait_recv()

        @pl.when(jnp.logical_and(i > 2, i < 6))
        def _():
            for cp in send_z(i, i + 2, zdev((i % 2) * 2 - 1)):
                cp.start()

        u = uimg[i]
        for q in range(NX):
            stg[i, q] = dot(u, W[0, :, q * HQ : (q + 1) * HQ]).astype(BF16)
        rs_img(i).first()

    def at(k, step, do, *args):
        @pl.when(k == step)
        def _():
            do(*args)

    def up_step(k, _):
        @pl.when(k < NZ)
        def _():
            up_chunk(k)

        @pl.when(k >= 2)
        def _():
            rs_img(k - 2).join()

        at(k, 1, w_step1, 1)
        at(k, 3, w_step1, 2)
        at(k, 4, w_step2, 1)
        at(k, 6, w_step1, 3)
        at(k, 7, w_step2, 2)
        return 0

    lax.fori_loop(0, NZ + 2, up_step, 0)

    w_step3(1)
    for q in range(NX):
        stgt[q] = dot(utxt[...], W[1, :, q * HQ : (q + 1) * HQ]).astype(BF16)
    for h in range(2):
        rs_txt(h).first()
    w_step2(3)

    def pack_u(i, _):
        u32[pl.ds(pl.multiple_of(i * RC, 8), RI), :] = uimg[i].astype(F32)[0:RI]
        text = utxt[pl.ds(pl.multiple_of(i * 16, 16), 16), :].astype(F32)[0:RT]
        u32[pl.ds(pl.multiple_of(i * RC + RI, 8), RT), :] = text
        t32[pl.ds(pl.multiple_of(i * RT, 8), RT), :] = text
        return 0

    lax.fori_loop(0, NZ, pack_u, 0)

    def text_cp(f, t, k):
        yy = (y + t) % 4
        src = TS.at[f, yy // 2] if f % 2 == 0 else TS.at[f, (yy % 2) * 2 + c + k - 2 * c * k]
        return remote(src, TA.at[f, k, t], s_ts.at[f, t, k], s_tr.at[f, t, k], tdev(t, k))

    def send_text(f):
        TA[f, 0, 0] = TS[f, hi] if f % 2 == 0 else TS[f, q_mine]
        for t, k in others:
            text_cp(f, t, k).start()

    def wait_text(f):
        for t, k in others:
            text_cp(f, t, k).wait_recv()

    def sent_text(f):
        for t, k in others:
            text_cp(f, t, k).wait_send()

    def halves(f):
        for h in range(2):
            TS[f, h] = t32[:, h * ROWS : (h + 1) * ROWS].astype(BF16)

    halves(0)
    send_text(0)

    def act_chunk(i):
        rs_img(i).wait()
        pre = stg[i, x].astype(F32) + rrs[i, 0].astype(F32) + rrs[i, 1].astype(F32)
        pre_c[pl.ds(pl.multiple_of(i * RC, 8), RI), :] = pre[0:RI]
        hid[i, x] = gelu_tanh(pre).astype(BF16)
        ag_img(i).first()

    def join_text():
        for h in range(2):
            rs_txt(h).join()

    def act_text():
        for h in range(2):
            rs_txt(h).wait()
        pre = stgt[x].astype(F32) + rrst[0].astype(F32) + rrst[1].astype(F32)
        for i in range(NZ):
            pre_c[i * RC + RI : (i + 1) * RC, :] = pre[i * 16 : i * 16 + RT]
        hidt[x] = gelu_tanh(pre).astype(BF16)
        for h in range(2):
            ag_txt(h).first()

    def pass_text():
        for h in range(2):
            ag_txt(h).forward()

    def zslot(i):
        half = (i + 1) // 2
        return (NZ + half - 2 * half * (i % 2)) % NZ

    def mz_main(i):
        s = zslot(i)
        return remote(zst.at[i, 0:48], zr.at[s, 0:48], s_mzs.at[i], s_mzr.at[s], zdev(s))

    def mz_rest(i):
        s = zslot(i)
        return remote(zst.at[i, 48:64], zr.at[s, 48:64], s_mrs.at[i], s_mrr.at[s], zdev(s))

    def down_chunk(i):
        ag_img(i).wait()
        out = dot_nt(hid[i, 0], W[2, :, 0:HQ])
        for q in range(1, NX):
            out = out + dot_nt(hid[i, q], W[2, :, q * HQ : (q + 1) * HQ])
        diff = mod[0, 2, 0:1, :] * out[0:RI] - mod[0, 2, 1:2, :] * out[RI : 2 * RI]
        zst[i, 0:48, :] = diff[0:48].astype(BF16)
        rem[i, 0:8, :] = diff[48:56]

        @pl.when(i > 0)
        def _():
            mz_main(i).start()

        for q in range(NX):
            h32[q, pl.ds(pl.multiple_of(i * RC, 8), RI), :] = hid[i, q].astype(F32)[0:RI]

    def rest_chunk(i, _):
        zst[i, 48:64, :] = rem[i].astype(BF16)

        @pl.when(i > 0)
        def _():
            mz_rest(i).start()

        return 0

    def down_text():
        for h in range(2):
            ag_txt(h).wait()
        out = dot_nt(hidt[0], W[3, :, 0:HQ])
        for q in range(1, NX):
            out = out + dot_nt(hidt[q], W[3, :, q * HQ : (q + 1) * HQ])
        for i in range(NZ):
            rem[i, 8:16, :] = (
                mod[1, 2, 0:1, :] * out[i * 16 : i * 16 + RT] - mod[1, 2, 1:2, :] * out[i * 16 + RT : (i + 1) * 16]
            )
        for q in range(NX):
            full = hidt[q].astype(F32)
            text = [full[i * 16 : i * 16 + RT] for i in range(NZ)]
            for i in range(NZ):
                h32[q, i * RC + RI : (i + 1) * RC, :] = text[i]
            TS[1, q] = jnp.concatenate(text, axis=0).astype(BF16)
        send_text(1)

    def down_rest():
        w_step3(3)
        down_text()
        lax.fori_loop(3, NZ, rest_chunk, 0)

    def order(k):
        return k + 3 + (k // 5) * (4 - 2 * k)

    def hidden_step(k, _):
        @pl.when(k < NZ)
        def _():
            act_chunk(order(k))

        at(k, 2, join_text)
        at(k, 4, act_text)

        @pl.when(jnp.logical_and(k >= 1, k <= NZ))
        def _():
            ag_img(order(k - 1)).forward()

        at(k, 6, pass_text)
        at(k, 3, w_step3, 2)

        @pl.when(k >= 3)
        def _():
            down_chunk(order(k - 3))

        at(k, 7, down_rest)

        @pl.when(k >= 8)
        def _():
            rest_chunk(order(k - 3), 0)

        return 0

    lax.fori_loop(0, NZ + 3, hidden_step, 0)

    lane = lax.broadcasted_iota(jnp.int32, (CH, SEQ), 1)
    img_lane = lane % RC < RI
    uT[...] = jnp.where(img_lane, u32[...].T, 0.0).astype(BF16)
    hc[...] = h32[...].astype(BF16)

    total = ndiff[...] + zst[0].astype(F32)
    for s in range(1, NZ):
        a = remote(zst.at[s, 0:48], zr.at[s, 0:48], s_mzs.at[s], s_mzr.at[s], zdev(s))
        b = remote(zst.at[s, 48:64], zr.at[s, 48:64], s_mrs.at[s], s_mrr.at[s], zdev(s))
        a.wait_recv()
        b.wait_recv()
        total = total + zr[s].astype(F32)
    total = total * coef[:, 0:1]
    err_i = mod[0, 2, 0:1, :] * total[0:RI]
    err_t = mod[1, 2, 0:1, :] * total[RI : RI + RT]
    errz[0] = jnp.concatenate([err_i, err_t], axis=0).astype(BF16)

    def send_e(i, to, who):
        return remote(errz.at[i], errz.at[to], s_ezs.at[to], s_ezr.at[to], who)

    send_e(0, 1, zdev(1)).start()
    send_e(0, 2, zdev(-1)).start()

    def rs_hg(i):
        return Sum(
            lambda q: hgs.at[i, q], hgr.at[i, 2], lambda k: hgr.at[i, k],
            lambda k: s_hgs.at[i, k], lambda k: s_hgr.at[i, k], x, xdev, sign(i),
        )

    def ag_pg(i):
        return Gather(lambda q: pg.at[i, q], lambda k: s_pgs.at[i, k], lambda k: s_pgr.at[i, k], x, xdev, sign(i))

    def pre_grad(i):
        rs_hg(i).wait()
        g = hgs[i, x].astype(F32) + hgr[i, 0].astype(F32) + hgr[i, 1].astype(F32)
        pg[i, x] = (g * gelu_slope(pre_c[pl.ds(pl.multiple_of(i * RC, 8), RC), :])).astype(BF16)
        ag_pg(i).first()

    def left_forward(i):
        @pl.when(i > 0)
        def _():
            a, b = send_z(i, i, zdev(1))
            a.wait_send()
            b.wait_send()
            mz_main(i).wait_send()
            mz_rest(i).wait_send()

        rs_img(i).sent()
        ag_img(i).sent()

        @pl.when(i < 4)
        def _():
            for p in range(NP):
                w1_sent(i, p)

    def w1_sent(m, p):
        rows = wrows(m, 1 - hi, q_mine, p)
        for ss, rs in (
            (s_w1s.at[m, p], s_w1r.at[m, p]), (s_w2s.at[m, p], s_w2r.at[m, p]),
            (s_w3s.at[m, p, 0], s_w3r.at[m, p, 0]), (s_w3s.at[m, p, 1], s_w3r.at[m, p, 1]),
        ):
            remote(rows, rows, ss, rs, core).wait_send()

    def err_chunk(i):
        left_forward(i)

        @pl.when(i > 0)
        def _():
            send_e(i, i, zdev(1)).wait_recv()

        @pl.when(jnp.logical_and(i > 0, i < 6))
        def _():
            send_e(i, i + 2, zdev((i % 2) * 2 - 1)).start()

        full = errz[i].astype(F32)
        image = full[0:RI].astype(BF16)
        text = full[RI:RC].astype(BF16)
        t32[pl.ds(pl.multiple_of(i * RT, 8), RT), :] = full[RI:RC]
        for q in range(NX):
            lanes = slice(q * HQ, (q + 1) * HQ)
            hgs[i, q] = jnp.concatenate([dot(image, W[2, :, lanes]), dot(text, W[3, :, lanes])], axis=0).astype(BF16)
        rs_hg(i).first()

    def err_step(k, _):
        err_chunk(k)

        @pl.when(k >= 2)
        def _():
            rs_hg(k - 2).join()

        @pl.when(k >= 4)
        def _():
            pre_grad(k - 4)

        @pl.when(k >= 6)
        def _():
            ag_pg(k - 6).forward()

        return 0

    lax.fori_loop(0, NZ, err_step, 0)

    def cols(j):
        return pl.ds(j * HJ, HJ)

    def core_cp(m, j, l):
        return remote(
            G.at[m, l * 2 + 1 - c, :, cols(j)], CR.at[m, l, :, cols(j)], s_cs.at[m, j, l], s_cr.at[m, j, l], core
        )

    def rs_y(m, j, h):
        rows = pl.ds(h * HR, HR)
        return Sum(
            lambda yy: G.at[m, (yy % 2) * 2 + c, pl.ds(pl.multiple_of((yy // 2) * ROWS + h * HR, HR), HR), cols(j)],
            YR.at[m, 2, rows, cols(j)], lambda k: YR.at[m, k, rows, cols(j)],
            lambda k: s_ys.at[m, j, h, k], lambda k: s_yr.at[m, j, h, k], y, ydev, 1 - 2 * h,
        )

    def grad(m, j, left, wide):
        g = dot(left, wide).astype(BF16)
        for q in range(NX):
            G[m, q, :, j * HJ : (j + 1) * HJ] = g[:, q * HJ : (q + 1) * HJ]
        for l in range(2):
            core_cp(m, j, l).start()

    def after_core(m, j):
        for l in range(2):
            core_cp(m, j, l).wait_recv()
            G[m, l * 2 + c, :, cols(j)] = (
                G[m, l * 2 + c, :, cols(j)].astype(F32) + CR[m, l, :, cols(j)].astype(F32)
            ).astype(BF16)
        for h in range(2):
            rs_y(m, j, h).relayed.start()
        for h in range(2):
            rs_y(m, j, h).direct.start()

    def join_y(m, j):
        for h in range(2):
            rs_y(m, j, h).join()

    mine = pl.ds(pl.multiple_of(hi * ROWS, ROWS), ROWS)
    outs = (out_ui, out_di, out_ut, out_dt)

    def out_cp(o, j):
        return pltpu.make_async_copy(OB.at[o, :, cols(j)], outs[o].at[:, cols(j)], s_out.at[o, j])

    def finish(m, j):
        for h in range(2):
            rs_y(m, j, h).wait()
        g = G[m, lo * 2 + c, mine, cols(j)].astype(F32)
        for k in range(2):
            g = g + YR[m, k, :, cols(j)].astype(F32)
        OB[1 - m, :, cols(j)] = g
        out_cp(1 - m, j).start()

    def text_grad(o, fl, fr):
        left = TA[fl].reshape(8 * TXT, ROWS).astype(F32).T.astype(BF16)
        OB[o] = dot(left, TA[fr].reshape(8 * TXT, HQ))
        for j in range(NJ):
            out_cp(o, j).start()

    eT[...] = jnp.where(img_lane, errz[...].reshape(SEQ, CH).astype(F32).T, 0.0).astype(BF16)
    for j in range(NJ):
        grad(0, j, eT[...], jnp.concatenate([hc[q, :, j * HJ : (j + 1) * HJ] for q in range(NX)], axis=1))
    rs_hg(6).join()
    rs_hg(7).join()
    after_core(0, 0)
    pre_grad(4)
    after_core(0, 1)
    pre_grad(5)
    after_core(0, 2)
    halves(2)
    send_text(2)
    ag_pg(2).forward()
    ag_pg(3).forward()
    pre_grad(6)
    ag_pg(4).forward()
    pre_grad(7)
    join_y(0, 0)
    ag_pg(5).forward()
    join_y(0, 1)
    ag_pg(6).forward()
    join_y(0, 2)
    ag_pg(7).forward()

    def pg_in(i, _):
        ag_pg(i).wait()
        for q in range(NX):
            h32[q, pl.ds(pl.multiple_of(i * RT, 8), RT), :] = pg[i, q].astype(F32)[RI:RC]
        return 0

    lax.fori_loop(0, NZ, pg_in, 0)
    for j in range(NJ):
        wide = jnp.concatenate([pg[:, q, :, j * HJ : (j + 1) * HJ].reshape(SEQ, HJ) for q in range(NX)], axis=1)
        grad(1, j, uT[...], wide)
        if j == 0:
            TS[3] = h32[:, 0:TXT, :].astype(BF16)
            send_text(3)
        if j > 0:
            after_core(1, j - 1)
    after_core(1, NJ - 1)

    def left_backward(i, _):
        @pl.when(i > 0)
        def _():
            send_e(i, i, zdev(1)).wait_send()

        rs_hg(i).sent()
        ag_pg(i).sent()
        return 0

    for h in range(2):
        rs_txt(h).sent()
        ag_txt(h).sent()
    join_y(1, 0)
    for j in range(NJ):
        finish(0, j)
    join_y(1, 1)
    wait_text(1)
    wait_text(2)
    text_grad(3, 2, 1)
    join_y(1, 2)
    wait_text(0)
    wait_text(3)
    text_grad(2, 0, 3)
    lax.fori_loop(0, NZ, left_backward, 0)
    for f in range(4):
        sent_text(f)
    for j in range(NJ):
        finish(1, j)

    for m in range(2):
        for j in range(NJ):
            for l in range(2):
                core_cp(m, j, l).wait_send()
            for h in range(2):
                rs_y(m, j, h).sent()
    for o in range(4):
        for j in range(NJ):
            out_cp(o, j).wait()


def hand_on(a, b, c, d, oa, ob, oc, od, buf, s_in, s_out):
    ins = [pltpu.make_async_copy(src, buf.at[i], s_in.at[i]) for i, src in enumerate((a, b, c, d))]
    outs = [pltpu.make_async_copy(buf.at[i], dst, s_out.at[i]) for i, dst in enumerate((oa, ob, oc, od))]
    for cp in ins:
        cp.start()
    for i in range(4):
        ins[i].wait()
        outs[i].start()
    for cp in outs:
        cp.wait()


def body(
    latent_image, latent_text, noise_image, noise_text, up_image, down_image, up_text, down_text,
    modulation, timesteps, skips, text_lengths,
):
    half = D // 2
    frequency = jnp.exp(-math.log(10000.0) * jnp.arange(half).astype(F32) / half)
    times = jnp.concatenate([timesteps, timesteps - skips]).astype(F32)
    angles = times[:, None] * frequency[None, :]
    feats = jnp.concatenate([jnp.cos(angles), jnp.sin(angles)], axis=1)[:, None, :]

    any_ = pl.BlockSpec(memory_space=pl.ANY)
    vmem = pl.BlockSpec(memory_space=pltpu.VMEM)
    smem = pl.BlockSpec(memory_space=pltpu.SMEM)
    V = pltpu.VMEM
    dma = lambda *s: pltpu.SemaphoreType.DMA(s)
    out = jax.ShapeDtypeStruct((ROWS, HQ), F32)
    grads = pl.pallas_call(
        kernel,
        out_shape=(out, out, out, out),
        in_specs=[any_] * 8 + [vmem, vmem, smem, smem, smem],
        out_specs=(any_,) * 4,
        scratch_shapes=[
            V((RI, D), BF16), V((RT, D), BF16), V((RI, D), BF16), V((RT, D), BF16),
            V((4, CH, HB), BF16), V((NZ, 2 * RI, CH), BF16), V((NZ * 16, CH), BF16),
            V((RI + RT, CH), F32), V((2, 3, 2, CH), F32), V((RI + RT, 128), F32), V((SEQ, CH), F32),
            V((NZ, NX, 2 * RI, HQ), BF16), V((NX, 128, HQ), BF16),
            V((NZ, 3, 2 * RI, HQ), BF16), V((3, 128, HQ), BF16),
            V((NZ, NX, 2 * RI, HQ), BF16), V((NX, 128, HQ), BF16),
            V((SEQ, HQ), F32), V((NX, SEQ, HQ), F32), V((NX, SEQ, HQ), BF16),
            V((NZ, 64, CH), BF16), V((NZ, 16, CH), F32), V((NZ, 64, CH), BF16), V((NZ, 64, CH), BF16),
            V((TXT, CH), F32), V((CH, SEQ), BF16), V((CH, SEQ), BF16),
            V((NZ, NX, RC, HQ), BF16), V((NZ, 3, RC, HQ), BF16), V((NZ, NX, RC, HQ), BF16),
            V((2, NX, CH, HQ), BF16), V((2, 2, CH, HQ), BF16), V((2, 3, ROWS, HQ), BF16),
            V((4, 4, TXT, HQ), BF16), V((4, 2, 4, TXT, HQ), BF16), V((4, ROWS, HQ), F32),
            dma(4), dma(4), dma(4, NP), dma(4, NP), dma(4, NP), dma(4, NP), dma(4, NP, 2), dma(4, NP, 2),
            dma(NZ), dma(NZ), dma(NZ), dma(NZ),
            dma(10, 3), dma(10, 3), dma(10, 3), dma(10, 3), dma(NZ), dma(NZ), dma(NZ), dma(NZ), dma(NZ), dma(NZ),
            dma(NZ, 3), dma(NZ, 3), dma(NZ, 3), dma(NZ, 3), dma(2, NJ, 2), dma(2, NJ, 2),
            dma(2, NJ, 2, 3), dma(2, NJ, 2, 3), dma(4, 4, 2), dma(4, 4, 2), dma(4, NJ),
        ],
        compiler_params=pltpu.CompilerParams(
            collective_id=0, has_side_effects=True, vmem_limit_bytes=60 * 1024 * 1024
        ),
    )(
        latent_image, latent_text, noise_image, noise_text, up_image, up_text, down_image, down_text,
        modulation, feats, timesteps, skips, text_lengths,
    )
    return pl.pallas_call(
        hand_on, out_shape=(out, out, out, out), in_specs=[any_] * 4, out_specs=(any_,) * 4,
        scratch_shapes=[V((4, ROWS, HQ), F32), dma(4), dma(4)],
    )(*grads)


def solution(mesh):
    placed = (
        P("dp", "col", None),
        P("dp", "col", None),
        P("dp", "col", None),
        P("dp", "col", None),
        P("row", "col"),
        P("row", "col"),
        P("row", "col"),
        P("row", "col"),
        P(),
        P("dp"),
        P("dp"),
        P("dp"),
    )
    grads = P("row", ("col", "dp"))
    return jax.shard_map(
        body, mesh=mesh, in_specs=placed, out_specs=(grads, grads, grads, grads), check_vma=False
    )
```

```python
import functools
import math

import jax
import jax.numpy as jnp
from jax import lax
from jax.experimental import pallas as pl
from jax.experimental.pallas import tpu as pltpu
from jax.sharding import PartitionSpec as P

D = 3072
FF = 12288
IMG = 448
TXT = 64
STEPS = 1000
SEQ = 512
SAMPLES = 8

NX = 4
NZ = 8
CH = D // NX
HB = FF // NZ
HQ = HB // NX
RI = IMG // NZ
RT = TXT // NZ
RC = RI + RT
NJ = 3
LAG = 2
HJ = HQ // NJ
ROWS = D // 8
QR = ROWS // 4
HR = ROWS // 2

GELU_SCALE = 0.7978845608028654
GELU_CUBIC = 0.044715
NORM_EPS = 1e-06
MESH = pl.DeviceIdType.MESH
F32 = jnp.float32
BF16 = jnp.bfloat16


def gelu_tanh(values):
    inner = GELU_SCALE * (values + GELU_CUBIC * values * values * values)
    return 0.5 * values * (1.0 + jnp.tanh(inner))


def gelu_slope(values):
    inner = GELU_SCALE * (values + GELU_CUBIC * values * values * values)
    tangent = jnp.tanh(inner)
    return 0.5 * (1.0 + tangent) + 0.5 * values * (1.0 - tangent * tangent) * GELU_SCALE * (
        1.0 + 3.0 * GELU_CUBIC * values * values
    )


def dot(a, b):
    return jnp.dot(a, b, preferred_element_type=F32)


def dot_nt(a, b):
    return lax.dot_general(a, b, (((1,), (1,)), ((), ())), preferred_element_type=F32)


class Sum:
    def __init__(self, part, relay, got, both, ss, rs, pos, to, s):
        self.part, self.relay, self.got, self.both = part, relay, got, both
        self.ss, self.rs, self.pos, self.to, self.s = ss, rs, pos, to, s

    @property
    def relayed(self):
        return remote(self.part((self.pos + 2) % 4), self.relay, self.ss, self.rs[0], self.to(self.s))

    @property
    def direct(self):
        return remote(self.part((self.pos - self.s + 4) % 4), self.got(0), self.ss, self.rs[1], self.to(-self.s))

    @property
    def joined(self):
        return remote(self.part((self.pos + self.s + 4) % 4), self.got(1), self.ss, self.rs[1], self.to(self.s))

    def add(self):
        joint = self.part((self.pos + self.s + 4) % 4)
        joint[...] = (joint[...].astype(F32) + self.relay[...].astype(F32)).astype(BF16)
        self.joined.start()

    def join(self):
        self.relayed.wait_recv()
        self.add()

    def first(self):
        self.relayed.start()
        self.direct.start()

    def wait(self):
        remote(self.both, self.both, self.ss, self.rs[1], self.to(1)).wait_recv()


class Gather:
    def __init__(self, slot, both, ss, rs, pos, to, s):
        self.slot, self.both, self.ss, self.rs, self.pos, self.to, self.s = slot, both, ss, rs, pos, to, s

    @property
    def plus(self):
        return remote(self.slot(self.pos), self.slot(self.pos), self.ss, self.rs[0], self.to(self.s))

    @property
    def minus(self):
        return remote(self.slot(self.pos), self.slot(self.pos), self.ss, self.rs[1], self.to(-self.s))

    @property
    def onward(self):
        back = self.slot((self.pos - self.s + 4) % 4)
        return remote(back, back, self.ss, self.rs[1], self.to(self.s))

    def first(self):
        self.plus.start()
        self.minus.start()

    def forward(self):
        self.plus.wait_recv()
        self.onward.start()

    def wait(self):
        remote(self.both, self.both, self.ss, self.rs[1], self.to(1)).wait_recv()


def remote(src, dst, ss, rs, who):
    return pltpu.make_async_remote_copy(
        src_ref=src, dst_ref=dst, send_sem=ss, recv_sem=rs, device_id=who, device_id_type=MESH
    )


def kernel(
    lat_i, lat_t, noi_i, noi_t, up_i, up_t, dn_i, dn_t, modulation, timesteps, skips, lengths,
    out_ui, out_di, out_ut, out_dt,
    lbi, lbt, nbi, nbt, W, uall, ndiff, mod, coef, u32,
    stg, stgt, rrs, rrst, hid, hidt, pre_c, h32, hc,
    zst, rem, zr, errz, t32, uT, eT, hgs, hgr, pg, G, CR, YR, TS, TA, OB,
    s_loc, s_wl, s_w1, s_w2, s_w3, s_z, s_rs, s_rst, s_ag, s_agt, s_mz, s_ez, s_hg, s_pge, s_pgeg, s_pg, s_pgg, s_core, s_y, s_t, s_out, s_sent,
):
    r = lax.axis_index("row")
    z = lax.axis_index("col")
    d = lax.axis_index("dp")
    x, hi, lo, c = r // 2, r % 2, d // 2, d % 2
    y = hi * 2 + lo

    def dev(x, hi, lo, c, z):
        return (x * 2 + hi, z, lo * 2 + c)

    def xdev(t):
        return dev((x + t + NX) % NX, hi, lo, c, z)

    def zdev(t):
        return dev(x, hi, lo, c, (z + t + NZ) % NZ)

    def ydev(t):
        yy = (y + t + 4) % 4
        return dev(x, yy // 2, yy % 2, c, z)

    def tdev(t, k):
        yy = (y + t) % 4
        return dev(x, yy // 2, yy % 2, c + k - 2 * c * k, z)

    core = dev(x, hi, lo, 1 - c, z)
    adj = dev(x, 1 - hi, 1 - lo, c, z)
    side = dev(x, hi, 1 - lo, c, z)

    bar = pltpu.get_barrier_semaphore()
    for t in range(1, NX):
        pl.semaphore_signal(bar, inc=1, device_id=xdev(t), device_id_type=MESH)
    for t in range(1, NZ):
        pl.semaphore_signal(bar, inc=1, device_id=zdev(t), device_id_type=MESH)
    others = [(t, k) for t in range(4) for k in range(2) if t or k]
    for t, k in others:
        pl.semaphore_signal(bar, inc=1, device_id=tdev(t, k), device_id_type=MESH)

    reads = [
        pltpu.make_async_copy(lat_i.at[hi], lbi, s_loc.at[0]),
        pltpu.make_async_copy(lat_t.at[hi], lbt, s_loc.at[1]),
        pltpu.make_async_copy(noi_i.at[hi], nbi, s_loc.at[2]),
        pltpu.make_async_copy(noi_t.at[hi], nbt, s_loc.at[3]),
    ]
    for cp in reads:
        cp.start()
    weights = (up_i, up_t, dn_i, dn_t)
    wl = [
        pltpu.make_async_copy(
            weights[m], W.at[m, pl.ds(pl.multiple_of(hi * ROWS, ROWS), ROWS)], s_wl.at[m]
        )
        for m in range(4)
    ]

    q_mine = lo * 2 + c
    q_side = (1 - lo) * 2 + c

    def wpiece(m, half, quarter, p):
        rows = pl.ds(pl.multiple_of(half * ROWS + quarter * QR, QR), QR)
        return W.at[m, rows, first_lanes(p)] if m == 0 else W.at[m, rows]

    def first_q(p):
        return (x + (2, 1, 3, 0)[p]) % NX

    def first_lanes(p):
        return pl.ds(pl.multiple_of(first_q(p) * HQ, HQ), HQ)

    def widx(m, p):
        return p if m == 0 else 3 + m

    def w1(m, p):
        rows = pl.ds(pl.multiple_of(q_side * QR, QR), QR)
        src = weights[m].at[rows, first_lanes(p)] if m == 0 else weights[m].at[rows]
        return remote(src, wpiece(m, hi, q_side, p), s_sent.at[0], s_w1.at[widx(m, p)], adj)

    def w2(m, p):
        piece = wpiece(m, 1 - hi, q_mine, p)
        return remote(piece, piece, s_sent.at[1], s_w2.at[widx(m, p)], side)

    def w3(m, p, k):
        piece = wpiece(m, 1 - hi, q_side if k else q_mine, p)
        return remote(piece, piece, s_sent.at[2], s_w3.at[widx(m, p)], core)

    def w_step1(m, p=0):
        w1(m, p).wait_recv()
        w2(m, p).start()
        w3(m, p, 0).start()

    def w_step2(m, p=0):
        w2(m, p).wait_recv()
        w3(m, p, 1).start()

    def w_step3(m, p=0):
        if p == 0:
            wl[m].wait()
        both = W.at[m, 0 : 2 * QR, 0:HQ] if m == 0 else W.at[m, 0 : 2 * QR]
        remote(both, both, s_sent.at[2], s_w3.at[widx(m, p)], core).wait_recv()

    for cp in wl:
        cp.start()
    lane0 = pl.multiple_of(x * CH, CH)
    own_lanes = pl.ds(lane0, CH)
    t_s = timesteps[hi]
    t_g = t_s - skips[hi]
    times = (t_s.astype(F32), t_g.astype(F32))
    lane = lax.broadcasted_iota(jnp.int32, (8, CH), 1) + (x * CH) % (D // 2)
    frequency = jnp.exp(-math.log(10000.0) * lane.astype(F32) / (D // 2))
    angles = frequency * jnp.where(lax.broadcasted_iota(jnp.int32, (8, CH), 0) == 0, times[0], times[1])
    feats = jnp.where(lane * 0 + x < NX // 2, jnp.cos(angles), jnp.sin(angles))
    for k in range(2):
        for a in range(3):
            for b in range(2):
                mod[k, a, b : b + 1, :] = (
                    modulation[k, a, 0:1, own_lanes] + modulation[k, a, 1:2, own_lanes] * feats[b : b + 1]
                )
    levels = (times[0] * (1.0 / STEPS), times[1] * (1.0 / STEPS))
    length = lengths[hi]
    row = lax.broadcasted_iota(jnp.int32, (RI + RT, 128), 0)
    valid = jnp.logical_or(row < RI, row + (z * RT - RI) < length)
    count = jnp.full((RI + RT, 128), IMG, F32) + length.astype(F32)
    coef[...] = jnp.where(valid, SEQ / math.sqrt(SAMPLES * SEQ) / count, 0.0)
    pl.semaphore_wait(bar, 17)
    for p in range(NX):
        w1(0, p).start()
    for cp in reads:
        cp.wait()
    for latb, noib, rows, stream, base in ((lbi, nbi, RI, 0, 0), (lbt, nbt, RT, 1, RI)):
        lat_own = latb[:, own_lanes].astype(F32)
        noi_own = noib[:, own_lanes].astype(F32)
        owns = []
        us = []
        for b in range(2):
            level = levels[b]
            full = (1.0 - level) * latb[...].astype(F32) + level * noib[...].astype(F32)
            mean = jnp.mean(full, axis=-1, keepdims=True)
            cen = full - mean
            var = jnp.mean(cen * cen, axis=-1, keepdims=True)
            own = (1.0 - level) * lat_own + level * noi_own
            owns.append(own)
            normed = (own - mean) * lax.rsqrt(var + NORM_EPS)
            us.append(normed * (1.0 + mod[stream, 1, b : b + 1, :]) + mod[stream, 0, b : b + 1, :])
        ndiff[base : base + rows, :] = owns[0] - owns[1]
        both = jnp.concatenate(us, axis=0).astype(BF16)
        uall[0, 2 * base : 2 * (base + rows), :] = both

    def send_z(i, to, p, who):
        rows = pl.ds(p * RC, RC)
        return remote(uall.at[i, rows], uall.at[to, rows], s_sent.at[3], s_z.at[to, p], who)

    for p in range(2):
        send_z(0, 1, p, zdev(1)).start()
        send_z(0, 2, p, zdev(-1)).start()

    def z_pass(*chunks):
        for p in range(2):
            for i in chunks:
                send_z(i, i, p, zdev(1)).wait_recv()
                if i < 6:
                    send_z(i, i + 2, p, zdev((i % 2) * 2 - 1)).start()

    def sign(i):
        return 1 - 2 * (i % 2)

    def rs_img(i):
        return Sum(
            lambda q: stg.at[i, q], rrs.at[i, 2], lambda k: rrs.at[i, k], rrs.at[i, 0:2],
            s_sent.at[4], (s_rs.at[i, 0], s_rs.at[i, 1]), x, xdev, sign(i),
        )

    def ag_img(i):
        return Gather(
            lambda q: hid.at[i, q], rrs.at[i, 0:2], s_sent.at[5], (s_ag.at[i, 0], s_ag.at[i, 1]), x, xdev, sign(i)
        )

    def rs_txt(h):
        rows = pl.ds(h * 64, 64)
        return Sum(
            lambda q: stgt.at[q, rows], rrst.at[2, rows], lambda k: rrst.at[k, rows], rrst.at[0:2, rows],
            s_sent.at[6], (s_rst.at[h, 0], s_rst.at[h, 1]), x, xdev, 1 - 2 * h,
        )

    def ag_txt(h):
        rows = pl.ds(h * 64, 64)
        return Gather(
            lambda q: hidt.at[q, rows], rrst.at[0:2, rows], s_sent.at[7], (s_agt.at[h, 0], s_agt.at[h, 1]),
            x, xdev, 1 - 2 * h,
        )

    def up_first(p):
        w_step3(0, p)
        for i in range(3):
            stg[i, first_q(p)] = dot(uall[i, 0 : 2 * RI], W[0, :, first_lanes(p)]).astype(BF16)
        if p == 0:
            for i in range(3):
                rs_img(i).relayed.start()
        elif p == 1:
            rs_img(1).direct.start()
        elif p == 2:
            rs_img(0).direct.start()
            rs_img(2).direct.start()

    w_step1(0, 0)
    w_step1(0, 1)
    z_pass(1, 2)
    w_step2(0, 0)
    w_step1(0, 2)
    w_step2(0, 1)
    up_first(0)
    w_step1(0, 3)
    for m in range(1, 4):
        w1(m, 0).start()
    z_pass(3, 4)
    w_step2(0, 2)
    up_first(1)
    w_step2(0, 3)
    up_first(2)
    up_first(3)
    for i in range(3):
        rs_img(i).join()

    def up_chunk(i):
        u = uall[i, 0 : 2 * RI]
        for q in range(NX):
            stg[i, q] = dot(u, W[0, :, q * HQ : (q + 1) * HQ]).astype(BF16)
        rs_img(i).first()

    def at(k, step, do, *args):
        @pl.when(k == step)
        def _():
            do(*args)

    def up_step(k, _):
        at(k, 4, z_pass, 5, 6)
        at(k, 6, z_pass, 7)

        @pl.when(k < NZ)
        def _():
            up_chunk(k)

        at(k, 4, w_step1, 1)
        at(k, 5, w_step1, 2)
        at(k, 6, w_step2, 1)
        at(k, 7, w_step1, 3)

        @pl.when(k > 3)
        def _():
            rs_img(k - 1).join()

        return 0

    lax.fori_loop(3, NZ + 1, up_step, 0)
    w_step2(2)

    w_step3(1)
    utxt = uall[:, 2 * RI :].reshape(NZ * 16, CH)
    for q in range(NX):
        stgt[q] = dot(utxt, W[1, :, q * HQ : (q + 1) * HQ]).astype(BF16)
    for h in range(2):
        rs_txt(h).first()

    def pack_u(i, _):
        u32[pl.ds(pl.multiple_of(i * RC, 8), RI), :] = uall[i, 0 : 2 * RI].astype(F32)[0:RI]
        text = uall[i, 2 * RI :].astype(F32)[0:RT]
        u32[pl.ds(pl.multiple_of(i * RC + RI, 8), RT), :] = text
        t32[pl.ds(pl.multiple_of(i * RT, 8), RT), :] = text
        return 0

    lax.fori_loop(0, NZ, pack_u, 0)

    def text_cp(f, t, k, rows, lanes):
        yy = (y + t) % 4
        b = yy // 2 if f % 2 == 0 else (yy % 2) * 2 + c + k - 2 * c * k
        return remote(TS.at[f, b, rows, lanes], TA.at[f, k, t, rows, lanes], s_sent.at[8], s_t.at[f], tdev(t, k))

    def send_text(f, rows=slice(0, TXT), lanes=slice(0, HQ)):
        TA[f, 0, 0, rows, lanes] = TS[f, hi if f % 2 == 0 else q_mine, rows, lanes]
        for t, k in others:
            text_cp(f, t, k, rows, lanes).start()

    def wait_text(f):
        seven = TA.at[f].reshape(8, TXT, HQ).at[0:7]
        remote(seven, seven, s_sent.at[8], s_t.at[f], core).wait_recv()

    def halves(f, rows=slice(0, TXT)):
        for h in range(2):
            TS[f, h, rows] = t32[rows, h * ROWS : (h + 1) * ROWS].astype(BF16)

    halves(0)

    def act_chunk(i):
        rs_img(i).wait()
        pre = stg[i, x].astype(F32) + rrs[i, 0].astype(F32) + rrs[i, 1].astype(F32)
        pre_c[pl.ds(pl.multiple_of(i * RC, 8), RI), :] = pre[0:RI]
        hid[i, x] = gelu_tanh(pre).astype(BF16)
        ag_img(i).first()

    def join_text():
        for h in range(2):
            rs_txt(h).join()

    def act_text():
        for h in range(2):
            rs_txt(h).wait()
        pre = stgt[x].astype(F32) + rrst[0].astype(F32) + rrst[1].astype(F32)
        for i in range(NZ):
            pre_c[i * RC + RI : (i + 1) * RC, :] = pre[i * 16 : i * 16 + RT]
        hidt[x] = gelu_tanh(pre).astype(BF16)
        for h in range(2):
            ag_txt(h).first()

    def pass_text():
        for h in range(2):
            ag_txt(h).forward()

    def zslot(i):
        half = (i + 1) // 2
        return (NZ + half - 2 * half * (i % 2)) % NZ

    def mz(i, rows):
        return remote(zst.at[i, rows], zr.at[zslot(i), rows], s_sent.at[9], s_mz, zdev(zslot(i)))

    def mz_main(i):
        return mz(i, pl.ds(0, 48))

    def mz_rest(i):
        return mz(i, pl.ds(48, 16))

    def down_chunk(i):
        ag_img(i).wait()
        out = dot_nt(hid[i, 0], W[2, :, 0:HQ])
        for q in range(1, NX):
            out = out + dot_nt(hid[i, q], W[2, :, q * HQ : (q + 1) * HQ])
        diff = mod[0, 2, 0:1, :] * out[0:RI] - mod[0, 2, 1:2, :] * out[RI : 2 * RI]
        zst[i, 0:48, :] = diff[0:48].astype(BF16)
        rem[i, 0:8, :] = diff[48:56]

        @pl.when(i > 0)
        def _():
            mz_main(i).start()

        for q in range(NX):
            h32[q, pl.ds(pl.multiple_of(i * RC, 8), RI), :] = hid[i, q].astype(F32)[0:RI]

    def rest_chunk(i, _):
        zst[i, 48:64, :] = rem[i].astype(BF16)

        @pl.when(i > 0)
        def _():
            mz_rest(i).start()

        return 0

    def down_text():
        for h in range(2):
            ag_txt(h).wait()
        out = dot_nt(hidt[0], W[3, :, 0:HQ])
        for q in range(1, NX):
            out = out + dot_nt(hidt[q], W[3, :, q * HQ : (q + 1) * HQ])
        for i in range(NZ):
            rem[i, 8:16, :] = (
                mod[1, 2, 0:1, :] * out[i * 16 : i * 16 + RT] - mod[1, 2, 1:2, :] * out[i * 16 + RT : (i + 1) * 16]
            )
        for q in range(NX):
            full = hidt[q].astype(F32)
            text = [full[i * 16 : i * 16 + RT] for i in range(NZ)]
            for i in range(NZ):
                h32[q, i * RC + RI : (i + 1) * RC, :] = text[i]
            TS[1, q] = jnp.concatenate(text, axis=0).astype(BF16)
        send_text(1)

    def down_rest():
        w_step3(3)
        down_text()
        lax.fori_loop(5, NZ, rest_chunk, 0)

    def order(k):
        return k + 5 * (1 - (k + 5) // 8) + (k // 5) * (7 - 2 * k)

    def hidden_step(k, _):
        @pl.when(k < NZ)
        def _():
            act_chunk(order(k))

        at(k, 1, join_text)
        at(k, 3, act_text)

        @pl.when(jnp.logical_and(k >= LAG, k < NZ + LAG))
        def _():
            ag_img(order(k - LAG)).forward()

        at(k, LAG + 1, w_step2, 3)
        at(k, LAG + 1, w_step3, 2)
        at(k, LAG + 3, pass_text)

        @pl.when(k >= LAG + 2)
        def _():
            down_chunk(order(k - LAG - 2))

        at(k, LAG + 4, down_rest)
        at(k, LAG + 5, send_text, 0)

        @pl.when(k >= LAG + 5)
        def _():
            rest_chunk(order(k - LAG - 2), 0)

        return 0

    lax.fori_loop(0, NZ + LAG + 2, hidden_step, 0)

    lane = lax.broadcasted_iota(jnp.int32, (CH, SEQ), 1)
    img_lane = lane % RC < RI
    uT[...] = jnp.where(img_lane, u32[...].T, 0.0).astype(BF16)
    hc[...] = h32[...].astype(BF16)
    pre_c[...] = gelu_slope(pre_c[...])

    total = ndiff[...] + zst[0].astype(F32)
    remote(zr.at[1:NZ], zr.at[1:NZ], s_sent.at[9], s_mz, core).wait_recv()
    for s in range(1, NZ):
        total = total + zr[s].astype(F32)
    total = total * coef[:, 0:1]
    err_i = mod[0, 2, 0:1, :] * total[0:RI]
    err_t = mod[1, 2, 0:1, :] * total[RI : RI + RT]
    errz[0] = jnp.concatenate([err_i, err_t], axis=0).astype(BF16)

    def send_e(i, to, p, who):
        rows = pl.ds(p * 32, 32)
        return remote(errz.at[i, rows], errz.at[to, rows], s_sent.at[10], s_ez.at[to, p], who)

    for p in range(2):
        send_e(0, 1, p, zdev(1)).start()
        send_e(0, 2, p, zdev(-1)).start()

    def rs_hg(i):
        return Sum(
            lambda q: hgs.at[i, q], hgr.at[2, i], lambda k: hgr.at[k, i], hgr.at[0:2, i],
            s_sent.at[11], (s_hg.at[i, 0], s_hg.at[i, 1]), x, xdev, sign(i),
        )

    def ag_early(i):
        rows = pl.ds(pl.multiple_of(i * RC, RC), RC)
        return Gather(
            lambda q: pg.at[:, q, rows], None, s_sent.at[12], (s_pge.at[i], s_pgeg), x, xdev, sign(i)
        )

    def ag_late(j, h):
        rows = pl.ds(SEQ // 2 + h * (SEQ // 4), SEQ // 4)
        return Gather(
            lambda q: pg.at[j, q, rows], pg.at[j, 0:2, rows], s_sent.at[12], (s_pg.at[j, h], s_pgg.at[j, h]),
            x, xdev, 1 - 2 * h,
        )

    def pre_early(i):
        rs_hg(i).wait()
        g = hgs[i, x].astype(F32) + hgr[0, i].astype(F32) + hgr[1, i].astype(F32)
        rows = pl.ds(pl.multiple_of(i * RC, RC), RC)
        g = (g * pre_c[rows, :]).astype(BF16)
        for j in range(NJ):
            pg[j, x, rows, :] = g[:, j * HJ : (j + 1) * HJ]
        ag_early(i).first()

    def pre_late(j):
        lanes = slice(j * HJ, (j + 1) * HJ)
        late = slice(NZ // 2, NZ)
        g = hgs[late, x, :, lanes].astype(F32) + hgr[0, late, :, lanes].astype(F32) + hgr[1, late, :, lanes].astype(F32)
        pg[j, x, SEQ // 2 :, :] = (g.reshape(SEQ // 2, HJ) * pre_c[SEQ // 2 :, lanes]).astype(BF16)
        for h in range(2):
            ag_late(j, h).first()

    def pass_late(j):
        for h in range(2):
            ag_late(j, h).forward()

    def err_pass(i, p):
        send_e(i, i, p, zdev(1)).wait_recv()

        @pl.when(i < 6)
        def _():
            send_e(i, i + 2, p, zdev((i % 2) * 2 - 1)).start()

    def err_chunk(i):
        full = errz[i].astype(F32)
        image = full[0:RI].astype(BF16)
        text = full[RI:RC].astype(BF16)
        t32[pl.ds(pl.multiple_of(i * RT, 8), RT), :] = full[RI:RC]
        for q in range(NX):
            lanes = slice(q * HQ, (q + 1) * HQ)
            hgs[i, q] = jnp.concatenate([dot(image, W[2, :, lanes]), dot(text, W[3, :, lanes])], axis=0).astype(BF16)
        rs_hg(i).first()

    err_chunk(0)

    def err_step(k, _):
        for p in range(2):
            err_pass(2 * k - 1, p)

            @pl.when(k < 4)
            def _():
                err_pass(2 * k, p)

        err_chunk(2 * k - 1)

        @pl.when(k < 4)
        def _():
            err_chunk(2 * k)

        for i in (3, 2):

            @pl.when(2 * k - i >= 0)
            def _():
                rs_hg(2 * k - i).join()

        at(k, 2, pre_early, 0)
        at(k, 3, pre_early, 1)
        at(k, 3, pre_early, 2)
        at(k, 4, pre_early, 3)

        @pl.when(k >= 3)
        def _():
            ag_early(k - 3).forward()

        @pl.when(k == 3)
        def _():
            halves(2, slice(0, 32))
            send_text(2, slice(0, 32))

        return 0

    lax.fori_loop(1, 5, err_step, 0)
    halves(2, slice(32, TXT))
    send_text(2, slice(32, TXT))

    def cols(j):
        return pl.ds(j * HJ, HJ)

    def core_cp(m, j, l):
        return remote(G.at[m, l * 2 + 1 - c, :, cols(j)], CR.at[m, l, :, cols(j)], s_sent.at[13], s_core.at[m, j], core)

    def rs_y(m, j, h):
        rows = pl.ds(h * HR, HR)
        return Sum(
            lambda yy: G.at[m, (yy % 2) * 2 + c, pl.ds(pl.multiple_of((yy // 2) * ROWS + h * HR, HR), HR), cols(j)],
            YR.at[m, 2, rows, cols(j)], lambda k: YR.at[m, k, rows, cols(j)], None,
            s_sent.at[14], (s_y.at[m, j, 0], s_y.at[m, j, 1]), y, ydev, 1 - 2 * h,
        )

    def grad(m, j, left, wide):
        g = dot(left, wide).astype(BF16)
        for q in range(NX):
            G[m, q, :, j * HJ : (j + 1) * HJ] = g[:, q * HJ : (q + 1) * HJ]
        for l in range(2):
            core_cp(m, j, l).start()

    def after_core(m, j):
        both = CR.at[m, :, :, cols(j)]
        remote(both, both, s_sent.at[13], s_core.at[m, j], core).wait_recv()
        for l in range(2):
            G[m, l * 2 + c, :, cols(j)] = (
                G[m, l * 2 + c, :, cols(j)].astype(F32) + CR[m, l, :, cols(j)].astype(F32)
            ).astype(BF16)
        for h in range(2):
            rs_y(m, j, h).relayed.start()
        for h in range(2):
            rs_y(m, j, h).direct.start()

    def join_y(m, j):
        both = YR.at[m, 2, :, cols(j)]
        remote(both, both, s_sent.at[14], s_y.at[m, j, 0], core).wait_recv()
        for h in range(2):
            rs_y(m, j, h).add()

    mine = pl.ds(pl.multiple_of(hi * ROWS, ROWS), ROWS)
    outs = (out_ui, out_di, out_ut, out_dt)

    def out_cp(o, j):
        return pltpu.make_async_copy(OB.at[o, :, cols(j)], outs[o].at[:, cols(j)], s_out.at[o])

    def finish(m, j):
        both = YR.at[m, 0:2, :, cols(j)]
        remote(both, both, s_sent.at[14], s_y.at[m, j, 1], core).wait_recv()
        g = G[m, lo * 2 + c, mine, cols(j)].astype(F32)
        for k in range(2):
            g = g + YR[m, k, :, cols(j)].astype(F32)
        OB[1 - m, :, cols(j)] = g
        out_cp(1 - m, j).start()

    def text_grad(o, fl, fr):
        left = TA[fl].reshape(8 * TXT, ROWS).astype(F32).T.astype(BF16)
        OB[o] = dot(left, TA[fr].reshape(8 * TXT, HQ))
        for j in range(NJ):
            out_cp(o, j).start()

    eT[...] = jnp.where(img_lane, errz[...].reshape(SEQ, CH).astype(F32).T, 0.0).astype(BF16)
    for j in range(NJ):
        grad(0, j, eT[...], jnp.concatenate([hc[q, :, j * HJ : (j + 1) * HJ] for q in range(NX)], axis=1))
    rs_hg(7).join()
    ag_early(2).forward()
    for j in range(NJ):
        after_core(0, j)
    ag_early(3).forward()
    for i in range(NZ // 2, NZ):
        rs_hg(i).wait()
    for j in range(NJ):
        pre_late(j)
    early = pg.at[:, 0:2, 0 : SEQ // 2]
    remote(early, early, s_sent.at[12], s_pgeg, core).wait_recv()
    for j in range(NJ):
        pass_late(j)
        join_y(0, j)

    def pg_in(j):
        for h in range(2):
            ag_late(j, h).wait()
        lanes = slice(j * HJ, (j + 1) * HJ)
        for q in range(NX):
            text = pg[j, q].astype(F32).reshape(NZ, RC, HJ)[:, RI:RC]
            TS[3, q, :, lanes] = text.reshape(TXT, HJ).astype(BF16)
        return lanes

    for j in range(NJ):
        lanes = pg_in(j)
        grad(1, j, uT[...], jnp.concatenate([pg[j, q] for q in range(NX)], axis=1))
        after_core(1, j)
        send_text(3, lanes=lanes)

    join_y(1, 0)
    for j in range(NJ):
        finish(0, j)
    join_y(1, 1)
    wait_text(1)
    wait_text(2)
    text_grad(3, 2, 1)
    join_y(1, 2)
    wait_text(0)
    wait_text(3)
    text_grad(2, 0, 3)
    for j in range(NJ):
        finish(1, j)

    sent = (
        W.at[:, 0:QR], W.at[:, 0:QR], W.at[:, 0 : 2 * QR], uall.at[0:7], rrs, rrs, rrst, rrst,
        hgs.at[0:7], zst.at[0:7], errz.at[0:7], hgr, hgr, CR, YR,
    )
    for k, whole in enumerate(sent):
        remote(whole, whole, s_sent.at[k], s_sent.at[k], core).wait_send()
    for o in range(4):
        pltpu.make_async_copy(OB.at[o], outs[o], s_out.at[o]).wait()


def hand_on(a, b, c, d, oa, ob, oc, od, buf, s_in, s_out):
    ins = [pltpu.make_async_copy(src, buf.at[i], s_in.at[i]) for i, src in enumerate((a, b, c, d))]
    outs = [pltpu.make_async_copy(buf.at[i], dst, s_out.at[i]) for i, dst in enumerate((oa, ob, oc, od))]
    for cp in ins:
        cp.start()
    for i in range(4):
        ins[i].wait()
        outs[i].start()
    for cp in outs:
        cp.wait()


def body(
    latent_image, latent_text, noise_image, noise_text, up_image, down_image, up_text, down_text,
    modulation, timesteps, skips, text_lengths,
):
    any_ = pl.BlockSpec(memory_space=pl.ANY)
    vmem = pl.BlockSpec(memory_space=pltpu.VMEM)
    smem = pl.BlockSpec(memory_space=pltpu.SMEM)
    V = pltpu.VMEM
    dma = lambda *s: pltpu.SemaphoreType.DMA(s)
    out = jax.ShapeDtypeStruct((ROWS, HQ), F32)
    grads = pl.pallas_call(
        kernel,
        out_shape=(out, out, out, out),
        in_specs=[any_] * 8 + [vmem, smem, smem, smem],
        out_specs=(any_,) * 4,
        scratch_shapes=[
            V((RI, D), BF16), V((RT, D), BF16), V((RI, D), BF16), V((RT, D), BF16),
            V((4, CH, HB), BF16), V((NZ, 2 * RC, CH), BF16),
            V((RI + RT, CH), F32), V((2, 3, 2, CH), F32), V((RI + RT, 128), F32), V((SEQ, CH), F32),
            V((NZ, NX, 2 * RI, HQ), BF16), V((NX, 128, HQ), BF16),
            V((NZ, 3, 2 * RI, HQ), BF16), V((3, 128, HQ), BF16),
            V((NZ, NX, 2 * RI, HQ), BF16), V((NX, 128, HQ), BF16),
            V((SEQ, HQ), F32), V((NX, SEQ, HQ), F32), V((NX, SEQ, HQ), BF16),
            V((NZ, 64, CH), BF16), V((NZ, 16, CH), F32), V((NZ, 64, CH), BF16), V((NZ, 64, CH), BF16),
            V((TXT, CH), F32), V((CH, SEQ), BF16), V((CH, SEQ), BF16),
            V((NZ, NX, RC, HQ), BF16), V((3, NZ, RC, HQ), BF16), V((NJ, NX, SEQ, HJ), BF16),
            V((2, NX, CH, HQ), BF16), V((2, 2, CH, HQ), BF16), V((2, 3, ROWS, HQ), BF16),
            V((4, 4, TXT, HQ), BF16), V((4, 2, 4, TXT, HQ), BF16), V((4, ROWS, HQ), F32),
            dma(4), dma(4), dma(7), dma(7), dma(7), dma(NZ, 2), dma(NZ, 2), dma(2, 2), dma(NZ, 2), dma(2, 2),
            pltpu.SemaphoreType.DMA, dma(NZ, 2), dma(NZ, 2), dma(4), pltpu.SemaphoreType.DMA, dma(NJ, 2), dma(NJ, 2), dma(2, NJ), dma(2, NJ, 2), dma(4), dma(4), dma(15),
        ],
        compiler_params=pltpu.CompilerParams(
            collective_id=0, has_side_effects=True, vmem_limit_bytes=60 * 1024 * 1024
        ),
    )(
        latent_image, latent_text, noise_image, noise_text, up_image, up_text, down_image, down_text,
        modulation, timesteps, skips, text_lengths,
    )
    return pl.pallas_call(
        hand_on, out_shape=(out, out, out, out), in_specs=[any_] * 4, out_specs=(any_,) * 4,
        scratch_shapes=[V((4, ROWS, HQ), F32), dma(4), dma(4)],
    )(*grads)


def solution(mesh):
    placed = (
        P("dp", "col", None),
        P("dp", "col", None),
        P("dp", "col", None),
        P("dp", "col", None),
        P("row", "col"),
        P("row", "col"),
        P("row", "col"),
        P("row", "col"),
        P(),
        P("dp"),
        P("dp"),
        P("dp"),
    )
    grads = P("row", ("col", "dp"))
    return jax.shard_map(
        body, mesh=mesh, in_specs=placed, out_specs=(grads, grads, grads, grads), check_vma=False
    )
```

```python
import functools
import math

import jax
import jax.numpy as jnp
from jax import lax
from jax.experimental import pallas as pl
from jax.experimental.pallas import tpu as pltpu
from jax.sharding import PartitionSpec as P

D = 3072
FF = 12288
IMG = 448
TXT = 64
STEPS = 1000
SEQ = 512
SAMPLES = 8

NX = 4
NZ = 8
CH = D // NX
HB = FF // NZ
HQ = HB // NX
RI = IMG // NZ
RT = TXT // NZ
RC = RI + RT
NJ = 3
LAG = 2
HJ = HQ // NJ
ROWS = D // 8
QR = ROWS // 4
HR = ROWS // 2

GELU_SCALE = 0.7978845608028654
GELU_CUBIC = 0.044715
NORM_EPS = 1e-06
MESH = pl.DeviceIdType.MESH
F32 = jnp.float32
BF16 = jnp.bfloat16


def gelu_tanh(values):
    inner = GELU_SCALE * (values + GELU_CUBIC * values * values * values)
    return 0.5 * values * (1.0 + jnp.tanh(inner))


def gelu_slope(values):
    inner = GELU_SCALE * (values + GELU_CUBIC * values * values * values)
    tangent = jnp.tanh(inner)
    return 0.5 * (1.0 + tangent) + 0.5 * values * (1.0 - tangent * tangent) * GELU_SCALE * (
        1.0 + 3.0 * GELU_CUBIC * values * values
    )


def dot(a, b):
    return jnp.dot(a, b, preferred_element_type=F32)


def dot_nt(a, b):
    return lax.dot_general(a, b, (((1,), (1,)), ((), ())), preferred_element_type=F32)


class Sum:
    def __init__(self, part, relay, got, both, ss, rs, pos, to, s):
        self.part, self.relay, self.got, self.both = part, relay, got, both
        self.ss, self.rs, self.pos, self.to, self.s = ss, rs, pos, to, s

    @property
    def relayed(self):
        return remote(self.part((self.pos + 2) % 4), self.relay, self.ss, self.rs[0], self.to(self.s))

    @property
    def direct(self):
        return remote(self.part((self.pos - self.s + 4) % 4), self.got(0), self.ss, self.rs[1], self.to(-self.s))

    @property
    def joined(self):
        return remote(self.part((self.pos + self.s + 4) % 4), self.got(1), self.ss, self.rs[1], self.to(self.s))

    def add(self):
        joint = self.part((self.pos + self.s + 4) % 4)
        joint[...] = (joint[...].astype(F32) + self.relay[...].astype(F32)).astype(BF16)
        self.joined.start()

    def join(self):
        self.relayed.wait_recv()
        self.add()

    def first(self):
        self.relayed.start()
        self.direct.start()

    def wait(self):
        remote(self.both, self.both, self.ss, self.rs[1], self.to(1)).wait_recv()


class Gather:
    def __init__(self, slot, both, ss, rs, pos, to, s):
        self.slot, self.both, self.ss, self.rs, self.pos, self.to, self.s = slot, both, ss, rs, pos, to, s

    @property
    def plus(self):
        return remote(self.slot(self.pos), self.slot(self.pos), self.ss, self.rs[0], self.to(self.s))

    @property
    def minus(self):
        return remote(self.slot(self.pos), self.slot(self.pos), self.ss, self.rs[1], self.to(-self.s))

    @property
    def onward(self):
        back = self.slot((self.pos - self.s + 4) % 4)
        return remote(back, back, self.ss, self.rs[1], self.to(self.s))

    def first(self):
        self.plus.start()
        self.minus.start()

    def forward(self):
        self.plus.wait_recv()
        self.onward.start()

    def wait(self):
        remote(self.both, self.both, self.ss, self.rs[1], self.to(1)).wait_recv()


def remote(src, dst, ss, rs, who):
    return pltpu.make_async_remote_copy(
        src_ref=src, dst_ref=dst, send_sem=ss, recv_sem=rs, device_id=who, device_id_type=MESH
    )


def kernel(
    lat_i, lat_t, noi_i, noi_t, up_i, up_t, dn_i, dn_t, modulation, timesteps, skips, lengths,
    out_ui, out_di, out_ut, out_dt,
    lbi, lbt, nbi, nbt, W, uall, ndiff, mod, coef, u32,
    stg, stgt, rrs, rrst, hid, hidt, pre_c, h32, hc,
    zst, rem, zr, errz, t32, uT, eT, hgs, hgr, pg, G, CR, YR, TS, TA, OB,
    s_loc, s_wl, s_w1, s_w2, s_w3, s_z, s_rs, s_rst, s_ag, s_agt, s_mz, s_ez, s_hg, s_pge, s_pgeg, s_pg, s_pgg, s_core, s_y, s_t, s_out, s_sent,
):
    r = lax.axis_index("row")
    z = lax.axis_index("col")
    d = lax.axis_index("dp")
    x, hi, lo, c = r // 2, r % 2, d // 2, d % 2
    y = hi * 2 + lo

    def dev(x, hi, lo, c, z):
        return (x * 2 + hi, z, lo * 2 + c)

    def xdev(t):
        return dev((x + t + NX) % NX, hi, lo, c, z)

    def zdev(t):
        return dev(x, hi, lo, c, (z + t + NZ) % NZ)

    def ydev(t):
        yy = (y + t + 4) % 4
        return dev(x, yy // 2, yy % 2, c, z)

    def tdev(t, k):
        yy = (y + t) % 4
        return dev(x, yy // 2, yy % 2, c + k - 2 * c * k, z)

    core = dev(x, hi, lo, 1 - c, z)
    adj = dev(x, 1 - hi, 1 - lo, c, z)
    side = dev(x, hi, 1 - lo, c, z)

    bar = pltpu.get_barrier_semaphore()
    for t in range(1, NX):
        pl.semaphore_signal(bar, inc=1, device_id=xdev(t), device_id_type=MESH)
    for t in range(1, NZ):
        pl.semaphore_signal(bar, inc=1, device_id=zdev(t), device_id_type=MESH)
    others = [(t, k) for t in range(4) for k in range(2) if t or k]
    for t, k in others:
        pl.semaphore_signal(bar, inc=1, device_id=tdev(t, k), device_id_type=MESH)

    reads = [
        pltpu.make_async_copy(lat_i.at[hi], lbi, s_loc.at[0]),
        pltpu.make_async_copy(lat_t.at[hi], lbt, s_loc.at[1]),
        pltpu.make_async_copy(noi_i.at[hi], nbi, s_loc.at[2]),
        pltpu.make_async_copy(noi_t.at[hi], nbt, s_loc.at[3]),
    ]
    for cp in reads:
        cp.start()
    weights = (up_i, up_t, dn_i, dn_t)
    wl = [
        pltpu.make_async_copy(
            weights[m], W.at[m, pl.ds(pl.multiple_of(hi * ROWS, ROWS), ROWS)], s_wl.at[m]
        )
        for m in range(4)
    ]

    q_mine = lo * 2 + c
    q_side = (1 - lo) * 2 + c

    def wpiece(m, half, quarter, p):
        rows = pl.ds(pl.multiple_of(half * ROWS + quarter * QR, QR), QR)
        return W.at[m, rows, first_lanes(p)] if m == 0 else W.at[m, rows]

    def first_q(p):
        return (x + (2, 1, 3, 0)[p]) % NX

    def first_lanes(p):
        return pl.ds(pl.multiple_of(first_q(p) * HQ, HQ), HQ)

    def widx(m, p):
        return p if m == 0 else 3 + m

    def w1(m, p):
        rows = pl.ds(pl.multiple_of(q_side * QR, QR), QR)
        src = weights[m].at[rows, first_lanes(p)] if m == 0 else weights[m].at[rows]
        return remote(src, wpiece(m, hi, q_side, p), s_sent.at[0], s_w1.at[widx(m, p)], adj)

    def w2(m, p):
        piece = wpiece(m, 1 - hi, q_mine, p)
        return remote(piece, piece, s_sent.at[1], s_w2.at[widx(m, p)], side)

    def w3(m, p, k):
        piece = wpiece(m, 1 - hi, q_side if k else q_mine, p)
        return remote(piece, piece, s_sent.at[2], s_w3.at[widx(m, p)], core)

    def w_step1(m, p=0):
        w1(m, p).wait_recv()
        w2(m, p).start()
        w3(m, p, 0).start()

    def w_step2(m, p=0):
        w2(m, p).wait_recv()
        w3(m, p, 1).start()

    def w_step3(m, p=0):
        if p == 0:
            wl[m].wait()
        both = W.at[m, 0 : 2 * QR, 0:HQ] if m == 0 else W.at[m, 0 : 2 * QR]
        remote(both, both, s_sent.at[2], s_w3.at[widx(m, p)], core).wait_recv()

    for cp in wl:
        cp.start()
    lane0 = pl.multiple_of(x * CH, CH)
    own_lanes = pl.ds(lane0, CH)
    t_s = timesteps[hi]
    t_g = t_s - skips[hi]
    times = (t_s.astype(F32), t_g.astype(F32))
    lane = lax.broadcasted_iota(jnp.int32, (8, CH), 1) + (x * CH) % (D // 2)
    frequency = jnp.exp(-math.log(10000.0) * lane.astype(F32) / (D // 2))
    angles = frequency * jnp.where(lax.broadcasted_iota(jnp.int32, (8, CH), 0) == 0, times[0], times[1])
    feats = jnp.where(lane * 0 + x < NX // 2, jnp.cos(angles), jnp.sin(angles))
    for k in range(2):
        for a in range(3):
            for b in range(2):
                mod[k, a, b : b + 1, :] = (
                    modulation[k, a, 0:1, own_lanes] + modulation[k, a, 1:2, own_lanes] * feats[b : b + 1]
                )
    levels = (times[0] * (1.0 / STEPS), times[1] * (1.0 / STEPS))
    length = lengths[hi]
    row = lax.broadcasted_iota(jnp.int32, (RI + RT, 128), 0)
    valid = jnp.logical_or(row < RI, row + (z * RT - RI) < length)
    count = jnp.full((RI + RT, 128), IMG, F32) + length.astype(F32)
    coef[...] = jnp.where(valid, SEQ / math.sqrt(SAMPLES * SEQ) / count, 0.0)
    pl.semaphore_wait(bar, 17)
    for p in range(NX):
        w1(0, p).start()
    for cp in reads:
        cp.wait()
    for latb, noib, rows, stream, base in ((lbi, nbi, RI, 0, 0), (lbt, nbt, RT, 1, RI)):
        lat_own = latb[:, own_lanes].astype(F32)
        noi_own = noib[:, own_lanes].astype(F32)
        owns = []
        us = []
        for b in range(2):
            level = levels[b]
            full = (1.0 - level) * latb[...].astype(F32) + level * noib[...].astype(F32)
            mean = jnp.mean(full, axis=-1, keepdims=True)
            cen = full - mean
            var = jnp.mean(cen * cen, axis=-1, keepdims=True)
            own = (1.0 - level) * lat_own + level * noi_own
            owns.append(own)
            normed = (own - mean) * lax.rsqrt(var + NORM_EPS)
            us.append(normed * (1.0 + mod[stream, 1, b : b + 1, :]) + mod[stream, 0, b : b + 1, :])
        ndiff[base : base + rows, :] = owns[0] - owns[1]
        both = jnp.concatenate(us, axis=0).astype(BF16)
        uall[0, 2 * base : 2 * (base + rows), :] = both

    def send_z(i, to, p, who):
        rows = pl.ds(p * RC, RC)
        return remote(uall.at[i, rows], uall.at[to, rows], s_sent.at[3], s_z.at[to, p], who)

    for p in range(2):
        send_z(0, 1, p, zdev(1)).start()
        send_z(0, 2, p, zdev(-1)).start()

    def z_pass(*chunks):
        for p in range(2):
            for i in chunks:
                send_z(i, i, p, zdev(1)).wait_recv()
                if i < 6:
                    send_z(i, i + 2, p, zdev((i % 2) * 2 - 1)).start()

    def sign(i):
        return 1 - 2 * (i % 2)

    def rs_img(i):
        return Sum(
            lambda q: stg.at[i, q], rrs.at[i, 2], lambda k: rrs.at[i, k], rrs.at[i, 0:2],
            s_sent.at[4], (s_rs.at[i, 0], s_rs.at[i, 1]), x, xdev, sign(i),
        )

    def ag_img(i):
        return Gather(
            lambda q: hid.at[i, q], rrs.at[i, 0:2], s_sent.at[5], (s_ag.at[i, 0], s_ag.at[i, 1]), x, xdev, sign(i)
        )

    def rs_txt(h):
        rows = pl.ds(h * 64, 64)
        return Sum(
            lambda q: stgt.at[q, rows], rrst.at[2, rows], lambda k: rrst.at[k, rows], rrst.at[0:2, rows],
            s_sent.at[6], (s_rst.at[h, 0], s_rst.at[h, 1]), x, xdev, 1 - 2 * h,
        )

    def ag_txt(h):
        rows = pl.ds(h * 64, 64)
        return Gather(
            lambda q: hidt.at[q, rows], rrst.at[0:2, rows], s_sent.at[7], (s_agt.at[h, 0], s_agt.at[h, 1]),
            x, xdev, 1 - 2 * h,
        )

    def up_first(p):
        w_step3(0, p)
        for i in range(3):
            stg[i, first_q(p)] = dot(uall[i, 0 : 2 * RI], W[0, :, first_lanes(p)]).astype(BF16)
        if p == 0:
            for i in range(3):
                rs_img(i).relayed.start()
        elif p == 1:
            rs_img(1).direct.start()
        elif p == 2:
            rs_img(0).direct.start()
            rs_img(2).direct.start()

    w_step1(0, 0)
    w_step1(0, 1)
    z_pass(1, 2)
    w_step2(0, 0)
    w_step1(0, 2)
    w_step2(0, 1)
    up_first(0)
    w_step1(0, 3)
    for m in range(1, 4):
        w1(m, 0).start()
    z_pass(3, 4)
    w_step2(0, 2)
    up_first(1)
    w_step2(0, 3)
    up_first(2)
    up_first(3)
    for i in range(3):
        rs_img(i).join()

    def up_chunk(i):
        u = uall[i, 0 : 2 * RI]
        for q in range(NX):
            stg[i, q] = dot(u, W[0, :, q * HQ : (q + 1) * HQ]).astype(BF16)
        rs_img(i).first()

    def at(k, step, do, *args):
        @pl.when(k == step)
        def _():
            do(*args)

    def up_step(k, _):
        at(k, 4, z_pass, 5, 6)
        at(k, 6, z_pass, 7)

        @pl.when(k < NZ)
        def _():
            up_chunk(k)

        at(k, 4, w_step1, 1)
        at(k, 5, w_step1, 2)
        at(k, 6, w_step2, 1)
        at(k, 7, w_step1, 3)

        @pl.when(k > 3)
        def _():
            rs_img(k - 1).join()

        return 0

    lax.fori_loop(3, NZ + 1, up_step, 0)
    w_step2(2)

    w_step3(1)
    utxt = uall[:, 2 * RI :].reshape(NZ * 16, CH)
    for q in range(NX):
        stgt[q] = dot(utxt, W[1, :, q * HQ : (q + 1) * HQ]).astype(BF16)
    for h in range(2):
        rs_txt(h).first()

    def pack_u(i, _):
        u32[pl.ds(pl.multiple_of(i * RC, 8), RI), :] = uall[i, 0 : 2 * RI].astype(F32)[0:RI]
        text = uall[i, 2 * RI :].astype(F32)[0:RT]
        u32[pl.ds(pl.multiple_of(i * RC + RI, 8), RT), :] = text
        t32[pl.ds(pl.multiple_of(i * RT, 8), RT), :] = text
        return 0

    lax.fori_loop(0, NZ, pack_u, 0)

    def text_cp(f, t, k, rows, lanes):
        yy = (y + t) % 4
        b = yy // 2 if f % 2 == 0 else (yy % 2) * 2 + c + k - 2 * c * k
        return remote(TS.at[f, b, rows, lanes], TA.at[f, k, t, rows, lanes], s_sent.at[8], s_t.at[f], tdev(t, k))

    def send_text(f, rows=slice(0, TXT), lanes=slice(0, HQ)):
        TA[f, 0, 0, rows, lanes] = TS[f, hi if f % 2 == 0 else q_mine, rows, lanes]
        for t, k in others:
            text_cp(f, t, k, rows, lanes).start()

    def wait_text(f):
        seven = TA.at[f].reshape(8, TXT, HQ).at[0:7]
        remote(seven, seven, s_sent.at[8], s_t.at[f], core).wait_recv()

    def halves(f, rows=slice(0, TXT)):
        for h in range(2):
            TS[f, h, rows] = t32[rows, h * ROWS : (h + 1) * ROWS].astype(BF16)

    halves(0)

    def act_chunk(i):
        rs_img(i).wait()
        pre = stg[i, x].astype(F32) + rrs[i, 0].astype(F32) + rrs[i, 1].astype(F32)
        pre_c[pl.ds(pl.multiple_of(i * RC, 8), RI), :] = pre[0:RI]
        hid[i, x] = gelu_tanh(pre).astype(BF16)
        ag_img(i).first()

    def join_text():
        for h in range(2):
            rs_txt(h).join()

    def act_text():
        for h in range(2):
            rs_txt(h).wait()
        pre = stgt[x].astype(F32) + rrst[0].astype(F32) + rrst[1].astype(F32)
        for i in range(NZ):
            pre_c[i * RC + RI : (i + 1) * RC, :] = pre[i * 16 : i * 16 + RT]
        hidt[x] = gelu_tanh(pre).astype(BF16)
        for h in range(2):
            ag_txt(h).first()

    def pass_text():
        for h in range(2):
            ag_txt(h).forward()

    def zslot(i):
        half = (i + 1) // 2
        return (NZ + half - 2 * half * (i % 2)) % NZ

    def mz(i, rows):
        return remote(zst.at[i, rows], zr.at[zslot(i), rows], s_sent.at[9], s_mz, zdev(zslot(i)))

    def mz_main(i):
        return mz(i, pl.ds(0, 48))

    def mz_rest(i):
        return mz(i, pl.ds(48, 16))

    def down_chunk(i):
        ag_img(i).wait()
        out = dot_nt(hid[i, 0], W[2, :, 0:HQ])
        for q in range(1, NX):
            out = out + dot_nt(hid[i, q], W[2, :, q * HQ : (q + 1) * HQ])
        diff = mod[0, 2, 0:1, :] * out[0:RI] - mod[0, 2, 1:2, :] * out[RI : 2 * RI]
        zst[i, 0:48, :] = diff[0:48].astype(BF16)
        rem[i, 0:8, :] = diff[48:56]

        @pl.when(i > 0)
        def _():
            mz_main(i).start()

        for q in range(NX):
            h32[q, pl.ds(pl.multiple_of(i * RC, 8), RI), :] = hid[i, q].astype(F32)[0:RI]

    def rest_chunk(i, _):
        zst[i, 48:64, :] = rem[i].astype(BF16)

        @pl.when(i > 0)
        def _():
            mz_rest(i).start()

        return 0

    def down_text():
        for h in range(2):
            ag_txt(h).wait()
        out = dot_nt(hidt[0], W[3, :, 0:HQ])
        for q in range(1, NX):
            out = out + dot_nt(hidt[q], W[3, :, q * HQ : (q + 1) * HQ])
        for i in range(NZ):
            rem[i, 8:16, :] = (
                mod[1, 2, 0:1, :] * out[i * 16 : i * 16 + RT] - mod[1, 2, 1:2, :] * out[i * 16 + RT : (i + 1) * 16]
            )
        for q in range(NX):
            full = hidt[q].astype(F32)
            text = [full[i * 16 : i * 16 + RT] for i in range(NZ)]
            for i in range(NZ):
                h32[q, i * RC + RI : (i + 1) * RC, :] = text[i]
            TS[1, q] = jnp.concatenate(text, axis=0).astype(BF16)
        send_text(1)

    def down_rest():
        w_step3(3)
        down_text()
        lax.fori_loop(5, NZ, rest_chunk, 0)

    def order(k):
        return k + 5 * (1 - (k + 5) // 8) + (k // 5) * (7 - 2 * k)

    def hidden_step(k, _):
        @pl.when(k < NZ)
        def _():
            act_chunk(order(k))

        at(k, 1, join_text)
        at(k, 3, act_text)

        @pl.when(jnp.logical_and(k >= LAG, k < NZ + LAG))
        def _():
            ag_img(order(k - LAG)).forward()

        at(k, LAG + 1, w_step2, 3)
        at(k, LAG + 1, w_step3, 2)
        at(k, LAG + 3, pass_text)

        @pl.when(k >= LAG + 2)
        def _():
            down_chunk(order(k - LAG - 2))

        at(k, LAG + 4, down_rest)
        at(k, LAG + 5, send_text, 0)

        @pl.when(k >= LAG + 5)
        def _():
            rest_chunk(order(k - LAG - 2), 0)

        return 0

    lax.fori_loop(0, NZ + LAG + 2, hidden_step, 0)

    lane = lax.broadcasted_iota(jnp.int32, (CH, SEQ), 1)
    img_lane = lane % RC < RI
    uT[...] = jnp.where(img_lane, u32[...].T, 0.0).astype(BF16)
    hc[...] = h32[...].astype(BF16)
    pre_c[...] = gelu_slope(pre_c[...])

    total = ndiff[...] + zst[0].astype(F32)
    remote(zr.at[1:NZ], zr.at[1:NZ], s_sent.at[9], s_mz, core).wait_recv()
    for s in range(1, NZ):
        total = total + zr[s].astype(F32)
    total = total * coef[:, 0:1]
    err_i = mod[0, 2, 0:1, :] * total[0:RI]
    err_t = mod[1, 2, 0:1, :] * total[RI : RI + RT]
    errz[0] = jnp.concatenate([err_i, err_t], axis=0).astype(BF16)

    def send_e(i, to, p, who):
        rows = pl.ds(p * 32, 32)
        return remote(errz.at[i, rows], errz.at[to, rows], s_sent.at[10], s_ez.at[to, p], who)

    for p in range(2):
        send_e(0, 1, p, zdev(1)).start()
        send_e(0, 2, p, zdev(-1)).start()

    def rs_hg(i):
        return Sum(
            lambda q: hgs.at[i, q], hgr.at[2, i], lambda k: hgr.at[k, i], hgr.at[0:2, i],
            s_sent.at[11], (s_hg.at[i, 0], s_hg.at[i, 1]), x, xdev, sign(i),
        )

    def ag_early(i):
        rows = pl.ds(pl.multiple_of(i * RC, RC), RC)
        return Gather(
            lambda q: pg.at[:, q, rows], None, s_sent.at[12], (s_pge.at[i], s_pgeg), x, xdev, sign(i)
        )

    def ag_late(j, h):
        rows = pl.ds(SEQ // 2 + h * (SEQ // 4), SEQ // 4)
        return Gather(
            lambda q: pg.at[j, q, rows], pg.at[j, 0:2, rows], s_sent.at[12], (s_pg.at[j, h], s_pgg.at[j, h]),
            x, xdev, 1 - 2 * h,
        )

    def pre_early(i):
        rs_hg(i).wait()
        g = hgs[i, x].astype(F32) + hgr[0, i].astype(F32) + hgr[1, i].astype(F32)
        rows = pl.ds(pl.multiple_of(i * RC, RC), RC)
        g = (g * pre_c[rows, :]).astype(BF16)
        for j in range(NJ):
            pg[j, x, rows, :] = g[:, j * HJ : (j + 1) * HJ]
        ag_early(i).first()

    def pre_late(j):
        lanes = slice(j * HJ, (j + 1) * HJ)
        late = slice(NZ // 2, NZ)
        g = hgs[late, x, :, lanes].astype(F32) + hgr[0, late, :, lanes].astype(F32) + hgr[1, late, :, lanes].astype(F32)
        pg[j, x, SEQ // 2 :, :] = (g.reshape(SEQ // 2, HJ) * pre_c[SEQ // 2 :, lanes]).astype(BF16)
        for h in range(2):
            ag_late(j, h).first()

    def pass_late(j):
        for h in range(2):
            ag_late(j, h).forward()

    def err_pass(i, p):
        send_e(i, i, p, zdev(1)).wait_recv()

        @pl.when(i < 6)
        def _():
            send_e(i, i + 2, p, zdev((i % 2) * 2 - 1)).start()

    def err_chunk(i):
        full = errz[i].astype(F32)
        image = full[0:RI].astype(BF16)
        text = full[RI:RC].astype(BF16)
        t32[pl.ds(pl.multiple_of(i * RT, 8), RT), :] = full[RI:RC]
        for q in range(NX):
            lanes = slice(q * HQ, (q + 1) * HQ)
            hgs[i, q] = jnp.concatenate([dot(image, W[2, :, lanes]), dot(text, W[3, :, lanes])], axis=0).astype(BF16)
        rs_hg(i).first()

    err_chunk(0)

    def err_step(k, _):
        for p in range(2):
            err_pass(2 * k - 1, p)

            @pl.when(k < 4)
            def _():
                err_pass(2 * k, p)

        err_chunk(2 * k - 1)

        @pl.when(k < 4)
        def _():
            err_chunk(2 * k)

        for i in (3, 2):

            @pl.when(2 * k - i >= 0)
            def _():
                rs_hg(2 * k - i).join()

        at(k, 2, pre_early, 0)
        at(k, 3, pre_early, 1)
        at(k, 3, pre_early, 2)
        at(k, 4, pre_early, 3)

        @pl.when(k >= 3)
        def _():
            ag_early(k - 3).forward()

        @pl.when(k == 3)
        def _():
            halves(2, slice(0, 32))
            send_text(2, slice(0, 32))

        return 0

    lax.fori_loop(1, 5, err_step, 0)
    halves(2, slice(32, TXT))
    send_text(2, slice(32, TXT))

    def cols(j):
        return pl.ds(j * HJ, HJ)

    def core_cp(m, j, l):
        return remote(G.at[m, l * 2 + 1 - c, :, cols(j)], CR.at[m, l, :, cols(j)], s_sent.at[13], s_core.at[m, j], core)

    def rs_y(m, j, h):
        rows = pl.ds(h * HR, HR)
        return Sum(
            lambda yy: G.at[m, (yy % 2) * 2 + c, pl.ds(pl.multiple_of((yy // 2) * ROWS + h * HR, HR), HR), cols(j)],
            YR.at[m, 2, rows, cols(j)], lambda k: YR.at[m, k, rows, cols(j)], None,
            s_sent.at[14], (s_y.at[m, j, 0], s_y.at[m, j, 1]), y, ydev, 1 - 2 * h,
        )

    def grad(m, j, left, wide):
        g = dot(left, wide).astype(BF16)
        for q in range(NX):
            G[m, q, :, j * HJ : (j + 1) * HJ] = g[:, q * HJ : (q + 1) * HJ]
        for l in range(2):
            core_cp(m, j, l).start()

    def after_core(m, j):
        both = CR.at[m, :, :, cols(j)]
        remote(both, both, s_sent.at[13], s_core.at[m, j], core).wait_recv()
        for l in range(2):
            G[m, l * 2 + c, :, cols(j)] = (
                G[m, l * 2 + c, :, cols(j)].astype(F32) + CR[m, l, :, cols(j)].astype(F32)
            ).astype(BF16)
        for h in range(2):
            rs_y(m, j, h).relayed.start()
        for h in range(2):
            rs_y(m, j, h).direct.start()

    def join_y(m, j):
        both = YR.at[m, 2, :, cols(j)]
        remote(both, both, s_sent.at[14], s_y.at[m, j, 0], core).wait_recv()
        for h in range(2):
            rs_y(m, j, h).add()

    mine = pl.ds(pl.multiple_of(hi * ROWS, ROWS), ROWS)
    outs = (out_ui, out_di, out_ut, out_dt)

    def out_cp(o, j):
        return pltpu.make_async_copy(OB.at[o, :, cols(j)], outs[o].at[:, cols(j)], s_out.at[o])

    def finish(m, j):
        both = YR.at[m, 0:2, :, cols(j)]
        remote(both, both, s_sent.at[14], s_y.at[m, j, 1], core).wait_recv()
        g = G[m, lo * 2 + c, mine, cols(j)].astype(F32)
        for k in range(2):
            g = g + YR[m, k, :, cols(j)].astype(F32)
        OB[1 - m, :, cols(j)] = g
        out_cp(1 - m, j).start()

    def text_grad(o, fl, fr):
        left = TA[fl].reshape(8 * TXT, ROWS).astype(F32).T.astype(BF16)
        OB[o] = dot(left, TA[fr].reshape(8 * TXT, HQ))
        for j in range(NJ):
            out_cp(o, j).start()

    eT[...] = jnp.where(img_lane, errz[...].reshape(SEQ, CH).astype(F32).T, 0.0).astype(BF16)
    for j in range(NJ):
        grad(0, j, eT[...], jnp.concatenate([hc[q, :, j * HJ : (j + 1) * HJ] for q in range(NX)], axis=1))
    rs_hg(7).join()
    ag_early(2).forward()
    for j in range(NJ):
        after_core(0, j)
    ag_early(3).forward()
    for i in range(NZ // 2, NZ):
        rs_hg(i).wait()
    for j in range(NJ):
        pre_late(j)
    early = pg.at[:, 0:2, 0 : SEQ // 2]
    remote(early, early, s_sent.at[12], s_pgeg, core).wait_recv()
    for j in range(NJ):
        pass_late(j)
        join_y(0, j)

    def pg_in(j):
        for h in range(2):
            ag_late(j, h).wait()
        lanes = slice(j * HJ, (j + 1) * HJ)
        for q in range(NX):
            text = pg[j, q].astype(F32).reshape(NZ, RC, HJ)[:, RI:RC]
            TS[3, q, :, lanes] = text.reshape(TXT, HJ).astype(BF16)
        return lanes

    def up_grad(j):
        lanes = pg_in(j)
        grad(1, j, uT[...], jnp.concatenate([pg[j, q] for q in range(NX)], axis=1))
        return lanes

    parts = [up_grad(j) for j in range(NJ - 1)]
    after_core(1, 0)
    send_text(3, lanes=parts[0])
    parts.append(up_grad(NJ - 1))
    for j in range(1, NJ):
        after_core(1, j)
    for j in range(1, NJ):
        send_text(3, lanes=parts[j])

    join_y(1, 0)
    for j in range(NJ):
        finish(0, j)
    join_y(1, 1)
    wait_text(1)
    wait_text(2)
    text_grad(3, 2, 1)
    join_y(1, 2)
    wait_text(0)
    wait_text(3)
    text_grad(2, 0, 3)
    for j in range(NJ):
        finish(1, j)

    sent = (
        W.at[:, 0:QR], W.at[:, 0:QR], W.at[:, 0 : 2 * QR], uall.at[0:7], rrs, rrs, rrst, rrst,
        hgs.at[0:7], zst.at[0:7], errz.at[0:7], hgr, hgr, CR, YR,
    )
    for k, whole in enumerate(sent):
        remote(whole, whole, s_sent.at[k], s_sent.at[k], core).wait_send()
    for o in range(4):
        pltpu.make_async_copy(OB.at[o], outs[o], s_out.at[o]).wait()


def hand_on(a, b, c, d, oa, ob, oc, od, buf, s_in, s_out):
    ins = [pltpu.make_async_copy(src, buf.at[i], s_in.at[i]) for i, src in enumerate((a, b, c, d))]
    outs = [pltpu.make_async_copy(buf.at[i], dst, s_out.at[i]) for i, dst in enumerate((oa, ob, oc, od))]
    for cp in ins:
        cp.start()
    for i in range(4):
        ins[i].wait()
        outs[i].start()
    for cp in outs:
        cp.wait()


def body(
    latent_image, latent_text, noise_image, noise_text, up_image, down_image, up_text, down_text,
    modulation, timesteps, skips, text_lengths,
):
    any_ = pl.BlockSpec(memory_space=pl.ANY)
    vmem = pl.BlockSpec(memory_space=pltpu.VMEM)
    smem = pl.BlockSpec(memory_space=pltpu.SMEM)
    V = pltpu.VMEM
    dma = lambda *s: pltpu.SemaphoreType.DMA(s)
    out = jax.ShapeDtypeStruct((ROWS, HQ), F32)
    grads = pl.pallas_call(
        kernel,
        out_shape=(out, out, out, out),
        in_specs=[any_] * 8 + [vmem, smem, smem, smem],
        out_specs=(any_,) * 4,
        scratch_shapes=[
            V((RI, D), BF16), V((RT, D), BF16), V((RI, D), BF16), V((RT, D), BF16),
            V((4, CH, HB), BF16), V((NZ, 2 * RC, CH), BF16),
            V((RI + RT, CH), F32), V((2, 3, 2, CH), F32), V((RI + RT, 128), F32), V((SEQ, CH), F32),
            V((NZ, NX, 2 * RI, HQ), BF16), V((NX, 128, HQ), BF16),
            V((NZ, 3, 2 * RI, HQ), BF16), V((3, 128, HQ), BF16),
            V((NZ, NX, 2 * RI, HQ), BF16), V((NX, 128, HQ), BF16),
            V((SEQ, HQ), F32), V((NX, SEQ, HQ), F32), V((NX, SEQ, HQ), BF16),
            V((NZ, 64, CH), BF16), V((NZ, 16, CH), F32), V((NZ, 64, CH), BF16), V((NZ, 64, CH), BF16),
            V((TXT, CH), F32), V((CH, SEQ), BF16), V((CH, SEQ), BF16),
            V((NZ, NX, RC, HQ), BF16), V((3, NZ, RC, HQ), BF16), V((NJ, NX, SEQ, HJ), BF16),
            V((2, NX, CH, HQ), BF16), V((2, 2, CH, HQ), BF16), V((2, 3, ROWS, HQ), BF16),
            V((4, 4, TXT, HQ), BF16), V((4, 2, 4, TXT, HQ), BF16), V((4, ROWS, HQ), F32),
            dma(4), dma(4), dma(7), dma(7), dma(7), dma(NZ, 2), dma(NZ, 2), dma(2, 2), dma(NZ, 2), dma(2, 2),
            pltpu.SemaphoreType.DMA, dma(NZ, 2), dma(NZ, 2), dma(4), pltpu.SemaphoreType.DMA, dma(NJ, 2), dma(NJ, 2), dma(2, NJ), dma(2, NJ, 2), dma(4), dma(4), dma(15),
        ],
        compiler_params=pltpu.CompilerParams(
            collective_id=0, has_side_effects=True, vmem_limit_bytes=60 * 1024 * 1024
        ),
    )(
        latent_image, latent_text, noise_image, noise_text, up_image, up_text, down_image, down_text,
        modulation, timesteps, skips, text_lengths,
    )
    return pl.pallas_call(
        hand_on, out_shape=(out, out, out, out), in_specs=[any_] * 4, out_specs=(any_,) * 4,
        scratch_shapes=[V((4, ROWS, HQ), F32), dma(4), dma(4)],
    )(*grads)


def solution(mesh):
    placed = (
        P("dp", "col", None),
        P("dp", "col", None),
        P("dp", "col", None),
        P("dp", "col", None),
        P("row", "col"),
        P("row", "col"),
        P("row", "col"),
        P("row", "col"),
        P(),
        P("dp"),
        P("dp"),
        P("dp"),
    )
    grads = P("row", ("col", "dp"))
    return jax.shard_map(
        body, mesh=mesh, in_specs=placed, out_specs=(grads, grads, grads, grads), check_vma=False
    )
```

```python
import functools
import math

import jax
import jax.numpy as jnp
from jax import lax
from jax.experimental import pallas as pl
from jax.experimental.pallas import tpu as pltpu
from jax.sharding import PartitionSpec as P

D = 3072
FF = 12288
IMG = 448
TXT = 64
STEPS = 1000
SEQ = 512
SAMPLES = 8

NX = 4
NZ = 8
CH = D // NX
HB = FF // NZ
HQ = HB // NX
RI = IMG // NZ
RT = TXT // NZ
RC = RI + RT
NJ = 3
LAG = 2
HJ = HQ // NJ
ROWS = D // 8
QR = ROWS // 4
HR = ROWS // 2

GELU_SCALE = 0.7978845608028654
GELU_CUBIC = 0.044715
NORM_EPS = 1e-06
MESH = pl.DeviceIdType.MESH
F32 = jnp.float32
BF16 = jnp.bfloat16


def gelu_tanh(values):
    inner = GELU_SCALE * (values + GELU_CUBIC * values * values * values)
    return 0.5 * values * (1.0 + jnp.tanh(inner))


def gelu_slope(values):
    inner = GELU_SCALE * (values + GELU_CUBIC * values * values * values)
    tangent = jnp.tanh(inner)
    return 0.5 * (1.0 + tangent) + 0.5 * values * (1.0 - tangent * tangent) * GELU_SCALE * (
        1.0 + 3.0 * GELU_CUBIC * values * values
    )


def dot(a, b):
    return jnp.dot(a, b, preferred_element_type=F32)


def dot_nt(a, b):
    return lax.dot_general(a, b, (((1,), (1,)), ((), ())), preferred_element_type=F32)


class Sum:
    def __init__(self, part, relay, got, both, ss, rs, pos, to, s):
        self.part, self.relay, self.got, self.both = part, relay, got, both
        self.ss, self.rs, self.pos, self.to, self.s = ss, rs, pos, to, s

    @property
    def relayed(self):
        return remote(self.part((self.pos + 2) % 4), self.relay, self.ss, self.rs[0], self.to(self.s))

    @property
    def direct(self):
        return remote(self.part((self.pos - self.s + 4) % 4), self.got(0), self.ss, self.rs[1], self.to(-self.s))

    @property
    def joined(self):
        return remote(self.part((self.pos + self.s + 4) % 4), self.got(1), self.ss, self.rs[1], self.to(self.s))

    def add(self):
        joint = self.part((self.pos + self.s + 4) % 4)
        joint[...] = (joint[...].astype(F32) + self.relay[...].astype(F32)).astype(BF16)
        self.joined.start()

    def join(self):
        self.relayed.wait_recv()
        self.add()

    def first(self):
        self.relayed.start()
        self.direct.start()

    def wait(self):
        remote(self.both, self.both, self.ss, self.rs[1], self.to(1)).wait_recv()


class Gather:
    def __init__(self, slot, both, ss, rs, pos, to, s):
        self.slot, self.both, self.ss, self.rs, self.pos, self.to, self.s = slot, both, ss, rs, pos, to, s

    @property
    def plus(self):
        return remote(self.slot(self.pos), self.slot(self.pos), self.ss, self.rs[0], self.to(self.s))

    @property
    def minus(self):
        return remote(self.slot(self.pos), self.slot(self.pos), self.ss, self.rs[1], self.to(-self.s))

    @property
    def onward(self):
        back = self.slot((self.pos - self.s + 4) % 4)
        return remote(back, back, self.ss, self.rs[1], self.to(self.s))

    def first(self):
        self.plus.start()
        self.minus.start()

    def forward(self):
        self.plus.wait_recv()
        self.onward.start()

    def wait(self):
        remote(self.both, self.both, self.ss, self.rs[1], self.to(1)).wait_recv()


def remote(src, dst, ss, rs, who):
    return pltpu.make_async_remote_copy(
        src_ref=src, dst_ref=dst, send_sem=ss, recv_sem=rs, device_id=who, device_id_type=MESH
    )


def kernel(
    lat_i, lat_t, noi_i, noi_t, up_i, up_t, dn_i, dn_t, modulation, timesteps, skips, lengths,
    out_ui, out_di, out_ut, out_dt,
    lbi, lbt, nbi, nbt, W, uall, ndiff, mod, coef, u32,
    stg, stgt, rrs, rrst, hid, hidt, pre_c, h32, hc,
    zst, rem, zr, errz, t32, uT, eT, hgs, hgr, pg, G, CR, YR, TS, TA, OB,
    s_loc, s_wl, s_w1, s_w2, s_w3, s_z, s_rs, s_rst, s_ag, s_agt, s_mz, s_ez, s_hg, s_pge, s_pgeg, s_pg, s_pgg, s_core, s_y, s_t, s_out, s_sent,
):
    r = lax.axis_index("row")
    z = lax.axis_index("col")
    d = lax.axis_index("dp")
    x, hi, lo, c = r // 2, r % 2, d // 2, d % 2
    y = hi * 2 + lo

    def dev(x, hi, lo, c, z):
        return (x * 2 + hi, z, lo * 2 + c)

    def xdev(t):
        return dev((x + t + NX) % NX, hi, lo, c, z)

    def zdev(t):
        return dev(x, hi, lo, c, (z + t + NZ) % NZ)

    def ydev(t):
        yy = (y + t + 4) % 4
        return dev(x, yy // 2, yy % 2, c, z)

    def tdev(t, k):
        yy = (y + t) % 4
        return dev(x, yy // 2, yy % 2, c + k - 2 * c * k, z)

    core = dev(x, hi, lo, 1 - c, z)
    adj = dev(x, 1 - hi, 1 - lo, c, z)
    side = dev(x, hi, 1 - lo, c, z)

    bar = pltpu.get_barrier_semaphore()
    for t in range(1, NX):
        pl.semaphore_signal(bar, inc=1, device_id=xdev(t), device_id_type=MESH)
    for t in range(1, NZ):
        pl.semaphore_signal(bar, inc=1, device_id=zdev(t), device_id_type=MESH)
    others = [(t, k) for t in range(4) for k in range(2) if t or k]
    for t, k in others:
        pl.semaphore_signal(bar, inc=1, device_id=tdev(t, k), device_id_type=MESH)

    reads = [
        pltpu.make_async_copy(lat_i.at[hi], lbi, s_loc.at[0]),
        pltpu.make_async_copy(lat_t.at[hi], lbt, s_loc.at[1]),
        pltpu.make_async_copy(noi_i.at[hi], nbi, s_loc.at[2]),
        pltpu.make_async_copy(noi_t.at[hi], nbt, s_loc.at[3]),
    ]
    for cp in reads:
        cp.start()
    weights = (up_i, up_t, dn_i, dn_t)
    wl = [
        pltpu.make_async_copy(
            weights[m], W.at[m, pl.ds(pl.multiple_of(hi * ROWS, ROWS), ROWS)], s_wl.at[m]
        )
        for m in range(4)
    ]

    q_mine = lo * 2 + c
    q_side = (1 - lo) * 2 + c

    def wpiece(m, half, quarter, p):
        rows = pl.ds(pl.multiple_of(half * ROWS + quarter * QR, QR), QR)
        return W.at[m, rows, first_lanes(p)] if m == 0 else W.at[m, rows]

    def first_q(p):
        return (x + (2, 1, 3, 0)[p]) % NX

    def first_lanes(p):
        return pl.ds(pl.multiple_of(first_q(p) * HQ, HQ), HQ)

    def widx(m, p):
        return p if m == 0 else 3 + m

    def w1(m, p):
        rows = pl.ds(pl.multiple_of(q_side * QR, QR), QR)
        src = weights[m].at[rows, first_lanes(p)] if m == 0 else weights[m].at[rows]
        return remote(src, wpiece(m, hi, q_side, p), s_sent.at[0], s_w1.at[widx(m, p)], adj)

    def w2(m, p):
        piece = wpiece(m, 1 - hi, q_mine, p)
        return remote(piece, piece, s_sent.at[1], s_w2.at[widx(m, p)], side)

    def w3(m, p, k):
        piece = wpiece(m, 1 - hi, q_side if k else q_mine, p)
        return remote(piece, piece, s_sent.at[2], s_w3.at[widx(m, p)], core)

    def w_step1(m, p=0):
        w1(m, p).wait_recv()
        w2(m, p).start()
        w3(m, p, 0).start()

    def w_step2(m, p=0):
        w2(m, p).wait_recv()
        w3(m, p, 1).start()

    def w_step3(m, p=0):
        if p == 0:
            wl[m].wait()
        both = W.at[m, 0 : 2 * QR, 0:HQ] if m == 0 else W.at[m, 0 : 2 * QR]
        remote(both, both, s_sent.at[2], s_w3.at[widx(m, p)], core).wait_recv()

    for cp in wl:
        cp.start()
    lane0 = pl.multiple_of(x * CH, CH)
    own_lanes = pl.ds(lane0, CH)
    t_s = timesteps[hi]
    t_g = t_s - skips[hi]
    times = (t_s.astype(F32), t_g.astype(F32))
    lane = lax.broadcasted_iota(jnp.int32, (8, CH), 1) + (x * CH) % (D // 2)
    frequency = jnp.exp(-math.log(10000.0) * lane.astype(F32) / (D // 2))
    angles = frequency * jnp.where(lax.broadcasted_iota(jnp.int32, (8, CH), 0) == 0, times[0], times[1])
    feats = jnp.where(lane * 0 + x < NX // 2, jnp.cos(angles), jnp.sin(angles))
    for k in range(2):
        for a in range(3):
            for b in range(2):
                mod[k, a, b : b + 1, :] = (
                    modulation[k, a, 0:1, own_lanes] + modulation[k, a, 1:2, own_lanes] * feats[b : b + 1]
                )
    levels = (times[0] * (1.0 / STEPS), times[1] * (1.0 / STEPS))
    length = lengths[hi]
    row = lax.broadcasted_iota(jnp.int32, (RI + RT, 128), 0)
    valid = jnp.logical_or(row < RI, row + (z * RT - RI) < length)
    count = jnp.full((RI + RT, 128), IMG, F32) + length.astype(F32)
    coef[...] = jnp.where(valid, SEQ / math.sqrt(SAMPLES * SEQ) / count, 0.0)
    pl.semaphore_wait(bar, 17)
    for p in range(NX):
        w1(0, p).start()
    for cp in reads:
        cp.wait()
    for latb, noib, rows, stream, base in ((lbi, nbi, RI, 0, 0), (lbt, nbt, RT, 1, RI)):
        lat_own = latb[:, own_lanes].astype(F32)
        noi_own = noib[:, own_lanes].astype(F32)
        owns = []
        us = []
        for b in range(2):
            level = levels[b]
            full = (1.0 - level) * latb[...].astype(F32) + level * noib[...].astype(F32)
            mean = jnp.mean(full, axis=-1, keepdims=True)
            cen = full - mean
            var = jnp.mean(cen * cen, axis=-1, keepdims=True)
            own = (1.0 - level) * lat_own + level * noi_own
            owns.append(own)
            normed = (own - mean) * lax.rsqrt(var + NORM_EPS)
            us.append(normed * (1.0 + mod[stream, 1, b : b + 1, :]) + mod[stream, 0, b : b + 1, :])
        ndiff[base : base + rows, :] = owns[0] - owns[1]
        both = jnp.concatenate(us, axis=0).astype(BF16)
        uall[0, 2 * base : 2 * (base + rows), :] = both

    def send_z(i, to, p, who):
        rows = pl.ds(p * RC, RC)
        return remote(uall.at[i, rows], uall.at[to, rows], s_sent.at[3], s_z.at[to, p], who)

    for p in range(2):
        send_z(0, 1, p, zdev(1)).start()
        send_z(0, 2, p, zdev(-1)).start()

    def z_pass(*chunks):
        for p in range(2):
            for i in chunks:
                send_z(i, i, p, zdev(1)).wait_recv()
                if i < 6:
                    send_z(i, i + 2, p, zdev((i % 2) * 2 - 1)).start()

    def sign(i):
        return 1 - 2 * (i % 2)

    def rs_img(i):
        return Sum(
            lambda q: stg.at[i, q], rrs.at[i, 2], lambda k: rrs.at[i, k], rrs.at[i, 0:2],
            s_sent.at[4], (s_rs.at[i, 0], s_rs.at[i, 1]), x, xdev, sign(i),
        )

    def ag_img(i):
        return Gather(
            lambda q: hid.at[i, q], rrs.at[i, 0:2], s_sent.at[5], (s_ag.at[i, 0], s_ag.at[i, 1]), x, xdev, sign(i)
        )

    def rs_txt(h):
        rows = pl.ds(h * 64, 64)
        return Sum(
            lambda q: stgt.at[q, rows], rrst.at[2, rows], lambda k: rrst.at[k, rows], rrst.at[0:2, rows],
            s_sent.at[6], (s_rst.at[h, 0], s_rst.at[h, 1]), x, xdev, 1 - 2 * h,
        )

    def ag_txt(h):
        rows = pl.ds(h * 64, 64)
        return Gather(
            lambda q: hidt.at[q, rows], rrst.at[0:2, rows], s_sent.at[7], (s_agt.at[h, 0], s_agt.at[h, 1]),
            x, xdev, 1 - 2 * h,
        )

    def up_first(p):
        w_step3(0, p)
        for i in range(3):
            stg[i, first_q(p)] = dot(uall[i, 0 : 2 * RI], W[0, :, first_lanes(p)]).astype(BF16)
        if p == 0:
            for i in range(3):
                rs_img(i).relayed.start()
        elif p == 1:
            rs_img(1).direct.start()
        elif p == 2:
            rs_img(0).direct.start()
            rs_img(2).direct.start()

    w_step1(0, 0)
    w_step1(0, 1)
    z_pass(1, 2)
    w_step2(0, 0)
    w_step1(0, 2)
    w_step2(0, 1)
    up_first(0)
    w_step1(0, 3)
    for m in range(1, 4):
        w1(m, 0).start()
    z_pass(3, 4)
    w_step2(0, 2)
    up_first(1)
    w_step2(0, 3)
    up_first(2)
    up_first(3)
    for i in range(3):
        rs_img(i).join()

    def up_chunk(i):
        u = uall[i, 0 : 2 * RI]
        for q in range(NX):
            stg[i, q] = dot(u, W[0, :, q * HQ : (q + 1) * HQ]).astype(BF16)
        rs_img(i).first()

    def at(k, step, do, *args):
        @pl.when(k == step)
        def _():
            do(*args)

    def up_step(k, _):
        at(k, 4, z_pass, 5, 6)
        at(k, 6, z_pass, 7)

        @pl.when(k < NZ)
        def _():
            up_chunk(k)

        at(k, 4, w_step1, 1)
        at(k, 5, w_step1, 2)
        at(k, 6, w_step2, 1)
        at(k, 7, w_step1, 3)

        @pl.when(k > 3)
        def _():
            rs_img(k - 1).join()

        return 0

    lax.fori_loop(3, NZ + 1, up_step, 0)
    w_step2(2)

    w_step3(1)
    utxt = uall[:, 2 * RI :].reshape(NZ * 16, CH)
    for q in range(NX):
        stgt[q] = dot(utxt, W[1, :, q * HQ : (q + 1) * HQ]).astype(BF16)
    for h in range(2):
        rs_txt(h).first()

    def pack_u(i, _):
        u32[pl.ds(pl.multiple_of(i * RC, 8), RI), :] = uall[i, 0 : 2 * RI].astype(F32)[0:RI]
        text = uall[i, 2 * RI :].astype(F32)[0:RT]
        u32[pl.ds(pl.multiple_of(i * RC + RI, 8), RT), :] = text
        t32[pl.ds(pl.multiple_of(i * RT, 8), RT), :] = text
        return 0

    lax.fori_loop(0, NZ, pack_u, 0)

    def text_cp(f, t, k, rows, lanes):
        yy = (y + t) % 4
        b = yy // 2 if f % 2 == 0 else (yy % 2) * 2 + c + k - 2 * c * k
        return remote(TS.at[f, b, rows, lanes], TA.at[f, k, t, rows, lanes], s_sent.at[8], s_t.at[f], tdev(t, k))

    def send_text(f, rows=slice(0, TXT), lanes=slice(0, HQ)):
        TA[f, 0, 0, rows, lanes] = TS[f, hi if f % 2 == 0 else q_mine, rows, lanes]
        for t, k in others:
            text_cp(f, t, k, rows, lanes).start()

    def wait_text(f):
        seven = TA.at[f].reshape(8, TXT, HQ).at[0:7]
        remote(seven, seven, s_sent.at[8], s_t.at[f], core).wait_recv()

    def halves(f, rows=slice(0, TXT)):
        for h in range(2):
            TS[f, h, rows] = t32[rows, h * ROWS : (h + 1) * ROWS].astype(BF16)

    halves(0)

    def act_chunk(i):
        rs_img(i).wait()
        pre = stg[i, x].astype(F32) + rrs[i, 0].astype(F32) + rrs[i, 1].astype(F32)
        pre_c[pl.ds(pl.multiple_of(i * RC, 8), RI), :] = pre[0:RI]
        hid[i, x] = gelu_tanh(pre).astype(BF16)
        ag_img(i).first()

    def join_text():
        for h in range(2):
            rs_txt(h).join()

    def act_text():
        for h in range(2):
            rs_txt(h).wait()
        pre = stgt[x].astype(F32) + rrst[0].astype(F32) + rrst[1].astype(F32)
        for i in range(NZ):
            pre_c[i * RC + RI : (i + 1) * RC, :] = pre[i * 16 : i * 16 + RT]
        hidt[x] = gelu_tanh(pre).astype(BF16)
        for h in range(2):
            ag_txt(h).first()

    def pass_text():
        for h in range(2):
            ag_txt(h).forward()

    def zslot(i):
        half = (i + 1) // 2
        return (NZ + half - 2 * half * (i % 2)) % NZ

    def mz(i, rows):
        return remote(zst.at[i, rows], zr.at[zslot(i), rows], s_sent.at[9], s_mz, zdev(zslot(i)))

    def mz_main(i):
        return mz(i, pl.ds(0, 48))

    def mz_rest(i):
        return mz(i, pl.ds(48, 16))

    def down_chunk(i):
        ag_img(i).wait()
        out = dot_nt(hid[i, 0], W[2, :, 0:HQ])
        for q in range(1, NX):
            out = out + dot_nt(hid[i, q], W[2, :, q * HQ : (q + 1) * HQ])
        diff = mod[0, 2, 0:1, :] * out[0:RI] - mod[0, 2, 1:2, :] * out[RI : 2 * RI]
        zst[i, 0:48, :] = diff[0:48].astype(BF16)
        rem[i, 0:8, :] = diff[48:56]

        @pl.when(i > 0)
        def _():
            mz_main(i).start()

        for q in range(NX):
            h32[q, pl.ds(pl.multiple_of(i * RC, 8), RI), :] = hid[i, q].astype(F32)[0:RI]

    def rest_chunk(i, _):
        zst[i, 48:64, :] = rem[i].astype(BF16)

        @pl.when(i > 0)
        def _():
            mz_rest(i).start()

        return 0

    def down_text():
        for h in range(2):
            ag_txt(h).wait()
        out = dot_nt(hidt[0], W[3, :, 0:HQ])
        for q in range(1, NX):
            out = out + dot_nt(hidt[q], W[3, :, q * HQ : (q + 1) * HQ])
        for i in range(NZ):
            rem[i, 8:16, :] = (
                mod[1, 2, 0:1, :] * out[i * 16 : i * 16 + RT] - mod[1, 2, 1:2, :] * out[i * 16 + RT : (i + 1) * 16]
            )
        for q in range(NX):
            full = hidt[q].astype(F32)
            text = [full[i * 16 : i * 16 + RT] for i in range(NZ)]
            for i in range(NZ):
                h32[q, i * RC + RI : (i + 1) * RC, :] = text[i]
            TS[1, q] = jnp.concatenate(text, axis=0).astype(BF16)
        send_text(1)

    def down_rest():
        w_step3(3)
        down_text()
        lax.fori_loop(5, NZ, rest_chunk, 0)

    def order(k):
        return k + 5 * (1 - (k + 5) // 8) + (k // 5) * (7 - 2 * k)

    def hidden_step(k, _):
        @pl.when(k < NZ)
        def _():
            act_chunk(order(k))

        at(k, 1, join_text)
        at(k, 3, act_text)

        @pl.when(jnp.logical_and(k >= LAG, k < NZ + LAG))
        def _():
            ag_img(order(k - LAG)).forward()

        at(k, LAG + 1, w_step2, 3)
        at(k, LAG + 1, w_step3, 2)
        at(k, LAG + 3, pass_text)

        @pl.when(k >= LAG + 2)
        def _():
            down_chunk(order(k - LAG - 2))

        at(k, LAG + 4, down_rest)
        at(k, LAG + 5, send_text, 0)

        @pl.when(k >= LAG + 5)
        def _():
            rest_chunk(order(k - LAG - 2), 0)

        return 0

    lax.fori_loop(0, NZ + LAG + 2, hidden_step, 0)

    lane = lax.broadcasted_iota(jnp.int32, (CH, SEQ), 1)
    img_lane = lane % RC < RI
    uT[...] = jnp.where(img_lane, u32[...].T, 0.0).astype(BF16)
    hc[...] = h32[...].astype(BF16)
    pre_c[...] = gelu_slope(pre_c[...])

    total = ndiff[...] + zst[0].astype(F32)
    remote(zr.at[1:NZ], zr.at[1:NZ], s_sent.at[9], s_mz, core).wait_recv()
    for s in range(1, NZ):
        total = total + zr[s].astype(F32)
    total = total * coef[:, 0:1]
    err_i = mod[0, 2, 0:1, :] * total[0:RI]
    err_t = mod[1, 2, 0:1, :] * total[RI : RI + RT]
    errz[0] = jnp.concatenate([err_i, err_t], axis=0).astype(BF16)

    def send_e(i, to, p, who):
        rows = pl.ds(p * 32, 32)
        return remote(errz.at[i, rows], errz.at[to, rows], s_sent.at[10], s_ez.at[to, p], who)

    for p in range(2):
        send_e(0, 1, p, zdev(1)).start()
        send_e(0, 2, p, zdev(-1)).start()

    def rs_hg(i):
        return Sum(
            lambda q: hgs.at[i, q], hgr.at[2, i], lambda k: hgr.at[k, i], hgr.at[0:2, i],
            s_sent.at[11], (s_hg.at[i, 0], s_hg.at[i, 1]), x, xdev, sign(i),
        )

    def ag_early(i):
        rows = pl.ds(pl.multiple_of(i * RC, RC), RC)
        return Gather(
            lambda q: pg.at[:, q, rows], None, s_sent.at[12], (s_pge.at[i], s_pgeg), x, xdev, sign(i)
        )

    def ag_late(j, h):
        rows = pl.ds(SEQ // 2 + h * (SEQ // 4), SEQ // 4)
        return Gather(
            lambda q: pg.at[j, q, rows], pg.at[j, 0:2, rows], s_sent.at[12], (s_pg.at[j, h], s_pgg.at[j, h]),
            x, xdev, 1 - 2 * h,
        )

    def pre_early(i):
        rs_hg(i).wait()
        g = hgs[i, x].astype(F32) + hgr[0, i].astype(F32) + hgr[1, i].astype(F32)
        rows = pl.ds(pl.multiple_of(i * RC, RC), RC)
        g = (g * pre_c[rows, :]).astype(BF16)
        for j in range(NJ):
            pg[j, x, rows, :] = g[:, j * HJ : (j + 1) * HJ]
        ag_early(i).first()

    def pre_late(j):
        lanes = slice(j * HJ, (j + 1) * HJ)
        late = slice(NZ // 2, NZ)
        g = hgs[late, x, :, lanes].astype(F32) + hgr[0, late, :, lanes].astype(F32) + hgr[1, late, :, lanes].astype(F32)
        pg[j, x, SEQ // 2 :, :] = (g.reshape(SEQ // 2, HJ) * pre_c[SEQ // 2 :, lanes]).astype(BF16)
        for h in range(2):
            ag_late(j, h).first()

    def pass_late(j):
        for h in range(2):
            ag_late(j, h).forward()

    def err_pass(i, p):
        send_e(i, i, p, zdev(1)).wait_recv()

        @pl.when(i < 6)
        def _():
            send_e(i, i + 2, p, zdev((i % 2) * 2 - 1)).start()

    def err_chunk(i):
        full = errz[i].astype(F32)
        image = full[0:RI].astype(BF16)
        text = full[RI:RC].astype(BF16)
        t32[pl.ds(pl.multiple_of(i * RT, 8), RT), :] = full[RI:RC]
        for q in range(NX):
            lanes = slice(q * HQ, (q + 1) * HQ)
            hgs[i, q] = jnp.concatenate([dot(image, W[2, :, lanes]), dot(text, W[3, :, lanes])], axis=0).astype(BF16)
        rs_hg(i).first()

    err_chunk(0)

    def err_step(k, _):
        for p in range(2):
            err_pass(2 * k - 1, p)

            @pl.when(k < 4)
            def _():
                err_pass(2 * k, p)

        err_chunk(2 * k - 1)

        @pl.when(k < 4)
        def _():
            err_chunk(2 * k)

        for i in (3, 2):

            @pl.when(2 * k - i >= 0)
            def _():
                rs_hg(2 * k - i).join()

        at(k, 2, pre_early, 0)
        at(k, 3, pre_early, 1)
        at(k, 3, pre_early, 2)
        at(k, 4, pre_early, 3)

        @pl.when(k >= 3)
        def _():
            ag_early(k - 3).forward()

        @pl.when(k == 3)
        def _():
            halves(2, slice(0, 32))
            send_text(2, slice(0, 32))

        return 0

    lax.fori_loop(1, 5, err_step, 0)
    halves(2, slice(32, TXT))
    send_text(2, slice(32, TXT))

    def cols(j):
        return pl.ds(j * HJ, HJ)

    def core_cp(m, j, l):
        return remote(G.at[m, l * 2 + 1 - c, :, cols(j)], CR.at[m, l, :, cols(j)], s_sent.at[13], s_core.at[m, j], core)

    def rs_y(m, j, h):
        rows = pl.ds(h * HR, HR)
        return Sum(
            lambda yy: G.at[m, (yy % 2) * 2 + c, pl.ds(pl.multiple_of((yy // 2) * ROWS + h * HR, HR), HR), cols(j)],
            YR.at[m, 2, rows, cols(j)], lambda k: YR.at[m, k, rows, cols(j)], None,
            s_sent.at[14], (s_y.at[m, j, 0], s_y.at[m, j, 1]), y, ydev, 1 - 2 * h,
        )

    def grad(m, j, left, wide):
        g = dot(left, wide).astype(BF16)
        for q in range(NX):
            G[m, q, :, j * HJ : (j + 1) * HJ] = g[:, q * HJ : (q + 1) * HJ]
        for l in range(2):
            core_cp(m, j, l).start()

    def after_core(m, j):
        both = CR.at[m, :, :, cols(j)]
        remote(both, both, s_sent.at[13], s_core.at[m, j], core).wait_recv()
        for l in range(2):
            G[m, l * 2 + c, :, cols(j)] = (
                G[m, l * 2 + c, :, cols(j)].astype(F32) + CR[m, l, :, cols(j)].astype(F32)
            ).astype(BF16)
        for h in range(2):
            rs_y(m, j, h).relayed.start()
        for h in range(2):
            rs_y(m, j, h).direct.start()

    def join_y(m, j):
        both = YR.at[m, 2, :, cols(j)]
        remote(both, both, s_sent.at[14], s_y.at[m, j, 0], core).wait_recv()
        for h in range(2):
            rs_y(m, j, h).add()

    mine = pl.ds(pl.multiple_of(hi * ROWS, ROWS), ROWS)
    outs = (out_ui, out_di, out_ut, out_dt)

    def out_cp(o, j):
        return pltpu.make_async_copy(OB.at[o, :, cols(j)], outs[o].at[:, cols(j)], s_out.at[o])

    def finish(m, j):
        both = YR.at[m, 0:2, :, cols(j)]
        remote(both, both, s_sent.at[14], s_y.at[m, j, 1], core).wait_recv()
        g = G[m, lo * 2 + c, mine, cols(j)].astype(F32)
        for k in range(2):
            g = g + YR[m, k, :, cols(j)].astype(F32)
        OB[1 - m, :, cols(j)] = g
        out_cp(1 - m, j).start()

    def text_grad(o, fl, fr):
        left = TA[fl].reshape(8 * TXT, ROWS).astype(F32).T.astype(BF16)
        OB[o] = dot(left, TA[fr].reshape(8 * TXT, HQ))
        for j in range(NJ):
            out_cp(o, j).start()

    eT[...] = jnp.where(img_lane, errz[...].reshape(SEQ, CH).astype(F32).T, 0.0).astype(BF16)
    for j in range(NJ):
        grad(0, j, eT[...], jnp.concatenate([hc[q, :, j * HJ : (j + 1) * HJ] for q in range(NX)], axis=1))
    rs_hg(7).join()
    ag_early(2).forward()
    for j in range(NJ):
        after_core(0, j)
    ag_early(3).forward()
    for i in range(NZ // 2, NZ):
        rs_hg(i).wait()
    for j in range(NJ):
        pre_late(j)
    def pg_text(part):
        rows = slice(part * 32, part * 32 + 32)
        tokens = slice(part * (SEQ // 2), (part + 1) * (SEQ // 2))
        for q in range(NX):
            for j in range(NJ):
                text = pg[j, q, tokens, :].astype(F32).reshape(NZ // 2, RC, HJ)[:, RI:RC]
                TS[3, q, rows, j * HJ : (j + 1) * HJ] = text.reshape(32, HJ).astype(BF16)
        send_text(3, rows)

    pass_late(0)
    join_y(0, 0)
    early = pg.at[:, 0:2, 0 : SEQ // 2]
    remote(early, early, s_sent.at[12], s_pgeg, core).wait_recv()
    pass_late(1)
    pg_text(0)
    join_y(0, 1)
    pass_late(2)
    join_y(0, 2)

    def up_grad(j):
        for h in range(2):
            ag_late(j, h).wait()
        grad(1, j, uT[...], jnp.concatenate([pg[j, q] for q in range(NX)], axis=1))

    for j in range(NJ - 1):
        up_grad(j)
    after_core(1, 0)
    up_grad(NJ - 1)
    for j in range(1, NJ):
        after_core(1, j)
    pg_text(1)

    join_y(1, 0)
    for j in range(NJ):
        finish(0, j)
    join_y(1, 1)
    wait_text(1)
    wait_text(2)
    text_grad(3, 2, 1)
    join_y(1, 2)
    wait_text(0)
    wait_text(3)
    text_grad(2, 0, 3)
    for j in range(NJ):
        finish(1, j)

    sent = (
        W.at[:, 0:QR], W.at[:, 0:QR], W.at[:, 0 : 2 * QR], uall.at[0:7], rrs, rrs, rrst, rrst,
        hgs.at[0:7], zst.at[0:7], errz.at[0:7], hgr, hgr, CR, YR,
    )
    for k, whole in enumerate(sent):
        remote(whole, whole, s_sent.at[k], s_sent.at[k], core).wait_send()
    for o in range(4):
        pltpu.make_async_copy(OB.at[o], outs[o], s_out.at[o]).wait()


def hand_on(a, b, c, d, oa, ob, oc, od, buf, s_in, s_out):
    ins = [pltpu.make_async_copy(src, buf.at[i], s_in.at[i]) for i, src in enumerate((a, b, c, d))]
    outs = [pltpu.make_async_copy(buf.at[i], dst, s_out.at[i]) for i, dst in enumerate((oa, ob, oc, od))]
    for cp in ins:
        cp.start()
    for i in range(4):
        ins[i].wait()
        outs[i].start()
    for cp in outs:
        cp.wait()


def body(
    latent_image, latent_text, noise_image, noise_text, up_image, down_image, up_text, down_text,
    modulation, timesteps, skips, text_lengths,
):
    any_ = pl.BlockSpec(memory_space=pl.ANY)
    vmem = pl.BlockSpec(memory_space=pltpu.VMEM)
    smem = pl.BlockSpec(memory_space=pltpu.SMEM)
    V = pltpu.VMEM
    dma = lambda *s: pltpu.SemaphoreType.DMA(s)
    out = jax.ShapeDtypeStruct((ROWS, HQ), F32)
    grads = pl.pallas_call(
        kernel,
        out_shape=(out, out, out, out),
        in_specs=[any_] * 8 + [vmem, smem, smem, smem],
        out_specs=(any_,) * 4,
        scratch_shapes=[
            V((RI, D), BF16), V((RT, D), BF16), V((RI, D), BF16), V((RT, D), BF16),
            V((4, CH, HB), BF16), V((NZ, 2 * RC, CH), BF16),
            V((RI + RT, CH), F32), V((2, 3, 2, CH), F32), V((RI + RT, 128), F32), V((SEQ, CH), F32),
            V((NZ, NX, 2 * RI, HQ), BF16), V((NX, 128, HQ), BF16),
            V((NZ, 3, 2 * RI, HQ), BF16), V((3, 128, HQ), BF16),
            V((NZ, NX, 2 * RI, HQ), BF16), V((NX, 128, HQ), BF16),
            V((SEQ, HQ), F32), V((NX, SEQ, HQ), F32), V((NX, SEQ, HQ), BF16),
            V((NZ, 64, CH), BF16), V((NZ, 16, CH), F32), V((NZ, 64, CH), BF16), V((NZ, 64, CH), BF16),
            V((TXT, CH), F32), V((CH, SEQ), BF16), V((CH, SEQ), BF16),
            V((NZ, NX, RC, HQ), BF16), V((3, NZ, RC, HQ), BF16), V((NJ, NX, SEQ, HJ), BF16),
            V((2, NX, CH, HQ), BF16), V((2, 2, CH, HQ), BF16), V((2, 3, ROWS, HQ), BF16),
            V((4, 4, TXT, HQ), BF16), V((4, 2, 4, TXT, HQ), BF16), V((4, ROWS, HQ), F32),
            dma(4), dma(4), dma(7), dma(7), dma(7), dma(NZ, 2), dma(NZ, 2), dma(2, 2), dma(NZ, 2), dma(2, 2),
            pltpu.SemaphoreType.DMA, dma(NZ, 2), dma(NZ, 2), dma(4), pltpu.SemaphoreType.DMA, dma(NJ, 2), dma(NJ, 2), dma(2, NJ), dma(2, NJ, 2), dma(4), dma(4), dma(15),
        ],
        compiler_params=pltpu.CompilerParams(
            collective_id=0, has_side_effects=True, vmem_limit_bytes=60 * 1024 * 1024
        ),
    )(
        latent_image, latent_text, noise_image, noise_text, up_image, up_text, down_image, down_text,
        modulation, timesteps, skips, text_lengths,
    )
    return pl.pallas_call(
        hand_on, out_shape=(out, out, out, out), in_specs=[any_] * 4, out_specs=(any_,) * 4,
        scratch_shapes=[V((4, ROWS, HQ), F32), dma(4), dma(4)],
    )(*grads)


def solution(mesh):
    placed = (
        P("dp", "col", None),
        P("dp", "col", None),
        P("dp", "col", None),
        P("dp", "col", None),
        P("row", "col"),
        P("row", "col"),
        P("row", "col"),
        P("row", "col"),
        P(),
        P("dp"),
        P("dp"),
        P("dp"),
    )
    grads = P("row", ("col", "dp"))
    return jax.shard_map(
        body, mesh=mesh, in_specs=placed, out_specs=(grads, grads, grads, grads), check_vma=False
    )
```

```python
import functools
import math

import jax
import jax.numpy as jnp
from jax import lax
from jax.experimental import pallas as pl
from jax.experimental.pallas import tpu as pltpu
from jax.sharding import PartitionSpec as P

D = 3072
FF = 12288
IMG = 448
TXT = 64
STEPS = 1000
SEQ = 512
SAMPLES = 8

NX = 4
NZ = 8
CH = D // NX
HB = FF // NZ
HQ = HB // NX
RI = IMG // NZ
RT = TXT // NZ
RC = RI + RT
NJ = 3
LAG = 2
HJ = HQ // NJ
ROWS = D // 8
QR = ROWS // 4
HR = ROWS // 2

GELU_SCALE = 0.7978845608028654
GELU_CUBIC = 0.044715
NORM_EPS = 1e-06
MESH = pl.DeviceIdType.MESH
F32 = jnp.float32
BF16 = jnp.bfloat16


def gelu_tanh(values):
    inner = GELU_SCALE * (values + GELU_CUBIC * values * values * values)
    return 0.5 * values * (1.0 + jnp.tanh(inner))


def gelu_slope(values):
    inner = GELU_SCALE * (values + GELU_CUBIC * values * values * values)
    tangent = jnp.tanh(inner)
    return 0.5 * (1.0 + tangent) + 0.5 * values * (1.0 - tangent * tangent) * GELU_SCALE * (
        1.0 + 3.0 * GELU_CUBIC * values * values
    )


def dot(a, b):
    return jnp.dot(a, b, preferred_element_type=F32)


def dot_nt(a, b):
    return lax.dot_general(a, b, (((1,), (1,)), ((), ())), preferred_element_type=F32)


class Sum:
    def __init__(self, part, relay, got, both, ss, rs, pos, to, s):
        self.part, self.relay, self.got, self.both = part, relay, got, both
        self.ss, self.rs, self.pos, self.to, self.s = ss, rs, pos, to, s

    @property
    def relayed(self):
        return remote(self.part((self.pos + 2) % 4), self.relay, self.ss, self.rs[0], self.to(self.s))

    @property
    def direct(self):
        return remote(self.part((self.pos - self.s + 4) % 4), self.got(0), self.ss, self.rs[1], self.to(-self.s))

    @property
    def joined(self):
        return remote(self.part((self.pos + self.s + 4) % 4), self.got(1), self.ss, self.rs[1], self.to(self.s))

    def add(self):
        joint = self.part((self.pos + self.s + 4) % 4)
        joint[...] = (joint[...].astype(F32) + self.relay[...].astype(F32)).astype(BF16)
        self.joined.start()

    def join(self):
        self.relayed.wait_recv()
        self.add()

    def first(self):
        self.relayed.start()
        self.direct.start()

    def wait(self):
        remote(self.both, self.both, self.ss, self.rs[1], self.to(1)).wait_recv()


class Gather:
    def __init__(self, slot, both, ss, rs, pos, to, s):
        self.slot, self.both, self.ss, self.rs, self.pos, self.to, self.s = slot, both, ss, rs, pos, to, s

    @property
    def plus(self):
        return remote(self.slot(self.pos), self.slot(self.pos), self.ss, self.rs[0], self.to(self.s))

    @property
    def minus(self):
        return remote(self.slot(self.pos), self.slot(self.pos), self.ss, self.rs[1], self.to(-self.s))

    @property
    def onward(self):
        back = self.slot((self.pos - self.s + 4) % 4)
        return remote(back, back, self.ss, self.rs[1], self.to(self.s))

    def first(self):
        self.plus.start()
        self.minus.start()

    def forward(self):
        self.plus.wait_recv()
        self.onward.start()

    def wait(self):
        remote(self.both, self.both, self.ss, self.rs[1], self.to(1)).wait_recv()


def remote(src, dst, ss, rs, who):
    return pltpu.make_async_remote_copy(
        src_ref=src, dst_ref=dst, send_sem=ss, recv_sem=rs, device_id=who, device_id_type=MESH
    )


def kernel(
    lat_i, lat_t, noi_i, noi_t, up_i, up_t, dn_i, dn_t, modulation, timesteps, skips, lengths,
    out_ui, out_di, out_ut, out_dt,
    lbi, lbt, nbi, nbt, W, uall, ndiff, mod, coef, u32,
    stg, stgt, rrs, rrst, hid, hidt, pre_c, h32, hc,
    zst, rem, zr, errz, t32, uT, eT, hgs, hgr, pg, G, CR, YR, TS, TA, OB,
    s_loc, s_wl, s_w1, s_w2, s_w3, s_z, s_rs, s_rst, s_ag, s_agt, s_mz, s_ez, s_hg, s_pge, s_pgeg, s_pg, s_pgg, s_core, s_y, s_t, s_out, s_sent,
):
    r = lax.axis_index("row")
    z = lax.axis_index("col")
    d = lax.axis_index("dp")
    x, hi, lo, c = r // 2, r % 2, d // 2, d % 2
    y = hi * 2 + lo

    def dev(x, hi, lo, c, z):
        return (x * 2 + hi, z, lo * 2 + c)

    def xdev(t):
        return dev((x + t + NX) % NX, hi, lo, c, z)

    def zdev(t):
        return dev(x, hi, lo, c, (z + t + NZ) % NZ)

    def ydev(t):
        yy = (y + t + 4) % 4
        return dev(x, yy // 2, yy % 2, c, z)

    def tdev(t, k):
        yy = (y + t) % 4
        return dev(x, yy // 2, yy % 2, c + k - 2 * c * k, z)

    core = dev(x, hi, lo, 1 - c, z)
    adj = dev(x, 1 - hi, 1 - lo, c, z)
    side = dev(x, hi, 1 - lo, c, z)

    bar = pltpu.get_barrier_semaphore()
    for t in range(1, NX):
        pl.semaphore_signal(bar, inc=1, device_id=xdev(t), device_id_type=MESH)
    for t in range(1, NZ):
        pl.semaphore_signal(bar, inc=1, device_id=zdev(t), device_id_type=MESH)
    others = [(t, k) for t in range(4) for k in range(2) if t or k]
    for t, k in others:
        pl.semaphore_signal(bar, inc=1, device_id=tdev(t, k), device_id_type=MESH)

    reads = [
        pltpu.make_async_copy(lat_i.at[hi], lbi, s_loc.at[0]),
        pltpu.make_async_copy(lat_t.at[hi], lbt, s_loc.at[1]),
        pltpu.make_async_copy(noi_i.at[hi], nbi, s_loc.at[2]),
        pltpu.make_async_copy(noi_t.at[hi], nbt, s_loc.at[3]),
    ]
    for cp in reads:
        cp.start()
    weights = (up_i, up_t, dn_i, dn_t)
    wl = [
        pltpu.make_async_copy(
            weights[m], W.at[m, pl.ds(pl.multiple_of(hi * ROWS, ROWS), ROWS)], s_wl.at[m]
        )
        for m in range(4)
    ]

    q_mine = lo * 2 + c
    q_side = (1 - lo) * 2 + c

    def wpiece(m, half, quarter, p):
        rows = pl.ds(pl.multiple_of(half * ROWS + quarter * QR, QR), QR)
        return W.at[m, rows, first_lanes(p)] if m == 0 else W.at[m, rows]

    def first_q(p):
        return (x + (2, 1, 3, 0)[p]) % NX

    def first_lanes(p):
        return pl.ds(pl.multiple_of(first_q(p) * HQ, HQ), HQ)

    def widx(m, p):
        return p if m == 0 else 3 + m

    def w1(m, p):
        rows = pl.ds(pl.multiple_of(q_side * QR, QR), QR)
        src = weights[m].at[rows, first_lanes(p)] if m == 0 else weights[m].at[rows]
        return remote(src, wpiece(m, hi, q_side, p), s_sent.at[0], s_w1.at[widx(m, p)], adj)

    def w2(m, p):
        piece = wpiece(m, 1 - hi, q_mine, p)
        return remote(piece, piece, s_sent.at[1], s_w2.at[widx(m, p)], side)

    def w3(m, p, k):
        piece = wpiece(m, 1 - hi, q_side if k else q_mine, p)
        return remote(piece, piece, s_sent.at[2], s_w3.at[widx(m, p)], core)

    def w_step1(m, p=0):
        w1(m, p).wait_recv()
        w2(m, p).start()
        w3(m, p, 0).start()

    def w_step2(m, p=0):
        w2(m, p).wait_recv()
        w3(m, p, 1).start()

    def w_step3(m, p=0):
        if p == 0:
            wl[m].wait()
        both = W.at[m, 0 : 2 * QR, 0:HQ] if m == 0 else W.at[m, 0 : 2 * QR]
        remote(both, both, s_sent.at[2], s_w3.at[widx(m, p)], core).wait_recv()

    for cp in wl:
        cp.start()
    lane0 = pl.multiple_of(x * CH, CH)
    own_lanes = pl.ds(lane0, CH)
    t_s = timesteps[hi]
    t_g = t_s - skips[hi]
    times = (t_s.astype(F32), t_g.astype(F32))
    lane = lax.broadcasted_iota(jnp.int32, (8, CH), 1) + (x * CH) % (D // 2)
    frequency = jnp.exp(-math.log(10000.0) * lane.astype(F32) / (D // 2))
    angles = frequency * jnp.where(lax.broadcasted_iota(jnp.int32, (8, CH), 0) == 0, times[0], times[1])
    feats = jnp.where(lane * 0 + x < NX // 2, jnp.cos(angles), jnp.sin(angles))
    for k in range(2):
        for a in range(3):
            for b in range(2):
                mod[k, a, b : b + 1, :] = (
                    modulation[k, a, 0:1, own_lanes] + modulation[k, a, 1:2, own_lanes] * feats[b : b + 1]
                )
    levels = (times[0] * (1.0 / STEPS), times[1] * (1.0 / STEPS))
    length = lengths[hi]
    row = lax.broadcasted_iota(jnp.int32, (RI + RT, 128), 0)
    valid = jnp.logical_or(row < RI, row + (z * RT - RI) < length)
    count = jnp.full((RI + RT, 128), IMG, F32) + length.astype(F32)
    coef[...] = jnp.where(valid, SEQ / math.sqrt(SAMPLES * SEQ) / count, 0.0)
    pl.semaphore_wait(bar, 17)
    for p in range(NX):
        w1(0, p).start()
    for cp in reads:
        cp.wait()
    for latb, noib, rows, stream, base in ((lbi, nbi, RI, 0, 0), (lbt, nbt, RT, 1, RI)):
        lat_own = latb[:, own_lanes].astype(F32)
        noi_own = noib[:, own_lanes].astype(F32)
        owns = []
        us = []
        for b in range(2):
            level = levels[b]
            full = (1.0 - level) * latb[...].astype(F32) + level * noib[...].astype(F32)
            mean = jnp.mean(full, axis=-1, keepdims=True)
            cen = full - mean
            var = jnp.mean(cen * cen, axis=-1, keepdims=True)
            own = (1.0 - level) * lat_own + level * noi_own
            owns.append(own)
            normed = (own - mean) * lax.rsqrt(var + NORM_EPS)
            us.append(normed * (1.0 + mod[stream, 1, b : b + 1, :]) + mod[stream, 0, b : b + 1, :])
        ndiff[base : base + rows, :] = owns[0] - owns[1]
        both = jnp.concatenate(us, axis=0).astype(BF16)
        uall[0, 2 * base : 2 * (base + rows), :] = both

    def send_z(i, to, p, who):
        rows = pl.ds(p * RC, RC)
        return remote(uall.at[i, rows], uall.at[to, rows], s_sent.at[3], s_z.at[to, p], who)

    for p in range(2):
        send_z(0, 1, p, zdev(1)).start()
        send_z(0, 2, p, zdev(-1)).start()

    def z_pass(*chunks):
        for p in range(2):
            for i in chunks:
                send_z(i, i, p, zdev(1)).wait_recv()
                if i < 6:
                    send_z(i, i + 2, p, zdev((i % 2) * 2 - 1)).start()

    def sign(i):
        return 1 - 2 * (i % 2)

    def rs_img(i):
        return Sum(
            lambda q: stg.at[i, q], rrs.at[i, 2], lambda k: rrs.at[i, k], rrs.at[i, 0:2],
            s_sent.at[4], (s_rs.at[i, 0], s_rs.at[i, 1]), x, xdev, sign(i),
        )

    def ag_img(i):
        return Gather(
            lambda q: hid.at[i, q], rrs.at[i, 0:2], s_sent.at[5], (s_ag.at[i, 0], s_ag.at[i, 1]), x, xdev, sign(i)
        )

    def rs_txt(h):
        rows = pl.ds(h * 64, 64)
        return Sum(
            lambda q: stgt.at[q, rows], rrst.at[2, rows], lambda k: rrst.at[k, rows], rrst.at[0:2, rows],
            s_sent.at[6], (s_rst.at[h, 0], s_rst.at[h, 1]), x, xdev, 1 - 2 * h,
        )

    def ag_txt(h):
        rows = pl.ds(h * 64, 64)
        return Gather(
            lambda q: hidt.at[q, rows], rrst.at[0:2, rows], s_sent.at[7], (s_agt.at[h, 0], s_agt.at[h, 1]),
            x, xdev, 1 - 2 * h,
        )

    def up_first(p):
        w_step3(0, p)
        for i in range(3):
            stg[i, first_q(p)] = dot(uall[i, 0 : 2 * RI], W[0, :, first_lanes(p)]).astype(BF16)
        if p == 0:
            for i in range(3):
                rs_img(i).relayed.start()
        elif p == 1:
            rs_img(1).direct.start()
        elif p == 2:
            rs_img(0).direct.start()
            rs_img(2).direct.start()

    w_step1(0, 0)
    w_step1(0, 1)
    z_pass(1, 2)
    w_step2(0, 0)
    w_step1(0, 2)
    w_step2(0, 1)
    up_first(0)
    w_step1(0, 3)
    for m in range(1, 4):
        w1(m, 0).start()
    z_pass(3, 4)
    w_step2(0, 2)
    up_first(1)
    w_step2(0, 3)
    up_first(2)
    up_first(3)
    for i in range(3):
        rs_img(i).join()

    def up_chunk(i):
        u = uall[i, 0 : 2 * RI]
        for q in range(NX):
            stg[i, q] = dot(u, W[0, :, q * HQ : (q + 1) * HQ]).astype(BF16)
        rs_img(i).first()

    def at(k, step, do, *args):
        @pl.when(k == step)
        def _():
            do(*args)

    def up_step(k, _):
        at(k, 4, z_pass, 5, 6)
        at(k, 6, z_pass, 7)

        @pl.when(k < NZ)
        def _():
            up_chunk(k)

        at(k, 4, w_step1, 1)
        at(k, 5, w_step1, 2)
        at(k, 6, w_step2, 1)
        at(k, 7, w_step1, 3)

        @pl.when(k > 3)
        def _():
            rs_img(k - 1).join()

        return 0

    lax.fori_loop(3, NZ + 1, up_step, 0)
    w_step2(2)

    w_step3(1)
    utxt = uall[:, 2 * RI :].reshape(NZ * 16, CH)
    for q in range(NX):
        stgt[q] = dot(utxt, W[1, :, q * HQ : (q + 1) * HQ]).astype(BF16)
    for h in range(2):
        rs_txt(h).first()

    def pack_u(i, _):
        u32[pl.ds(pl.multiple_of(i * RC, 8), RI), :] = uall[i, 0 : 2 * RI].astype(F32)[0:RI]
        text = uall[i, 2 * RI :].astype(F32)[0:RT]
        u32[pl.ds(pl.multiple_of(i * RC + RI, 8), RT), :] = text
        t32[pl.ds(pl.multiple_of(i * RT, 8), RT), :] = text
        return 0

    lax.fori_loop(0, NZ, pack_u, 0)

    def text_cp(f, t, k, rows, lanes):
        yy = (y + t) % 4
        b = yy // 2 if f % 2 == 0 else (yy % 2) * 2 + c + k - 2 * c * k
        return remote(TS.at[f, b, rows, lanes], TA.at[f, k, t, rows, lanes], s_sent.at[8], s_t.at[f], tdev(t, k))

    def send_text(f, rows=slice(0, TXT), lanes=slice(0, HQ)):
        TA[f, 0, 0, rows, lanes] = TS[f, hi if f % 2 == 0 else q_mine, rows, lanes]
        for t, k in others:
            text_cp(f, t, k, rows, lanes).start()

    def wait_text(f):
        seven = TA.at[f].reshape(8, TXT, HQ).at[0:7]
        remote(seven, seven, s_sent.at[8], s_t.at[f], core).wait_recv()

    def halves(f, rows=slice(0, TXT)):
        for h in range(2):
            TS[f, h, rows] = t32[rows, h * ROWS : (h + 1) * ROWS].astype(BF16)

    halves(0)

    def act_chunk(i):
        rs_img(i).wait()
        pre = stg[i, x].astype(F32) + rrs[i, 0].astype(F32) + rrs[i, 1].astype(F32)
        pre_c[pl.ds(pl.multiple_of(i * RC, 8), RI), :] = pre[0:RI]
        hid[i, x] = gelu_tanh(pre).astype(BF16)
        ag_img(i).first()

    def join_text():
        for h in range(2):
            rs_txt(h).join()

    def act_text():
        for h in range(2):
            rs_txt(h).wait()
        pre = stgt[x].astype(F32) + rrst[0].astype(F32) + rrst[1].astype(F32)
        for i in range(NZ):
            pre_c[i * RC + RI : (i + 1) * RC, :] = pre[i * 16 : i * 16 + RT]
        hidt[x] = gelu_tanh(pre).astype(BF16)
        for h in range(2):
            ag_txt(h).first()

    def pass_text():
        for h in range(2):
            ag_txt(h).forward()

    def zslot(i):
        half = (i + 1) // 2
        return (NZ + half - 2 * half * (i % 2)) % NZ

    def mz(i, rows):
        return remote(zst.at[i, rows], zr.at[zslot(i), rows], s_sent.at[9], s_mz, zdev(zslot(i)))

    def mz_main(i):
        return mz(i, pl.ds(0, 48))

    def mz_rest(i):
        return mz(i, pl.ds(48, 16))

    def down_chunk(i):
        ag_img(i).wait()
        out = dot_nt(hid[i, 0], W[2, :, 0:HQ])
        for q in range(1, NX):
            out = out + dot_nt(hid[i, q], W[2, :, q * HQ : (q + 1) * HQ])
        diff = mod[0, 2, 0:1, :] * out[0:RI] - mod[0, 2, 1:2, :] * out[RI : 2 * RI]
        zst[i, 0:48, :] = diff[0:48].astype(BF16)
        rem[i, 0:8, :] = diff[48:56]

        @pl.when(i > 0)
        def _():
            mz_main(i).start()

        for q in range(NX):
            h32[q, pl.ds(pl.multiple_of(i * RC, 8), RI), :] = hid[i, q].astype(F32)[0:RI]

    def rest_chunk(i, _):
        zst[i, 48:64, :] = rem[i].astype(BF16)

        @pl.when(i > 0)
        def _():
            mz_rest(i).start()

        return 0

    def down_text():
        for h in range(2):
            ag_txt(h).wait()
        out = dot_nt(hidt[0], W[3, :, 0:HQ])
        for q in range(1, NX):
            out = out + dot_nt(hidt[q], W[3, :, q * HQ : (q + 1) * HQ])
        for i in range(NZ):
            rem[i, 8:16, :] = (
                mod[1, 2, 0:1, :] * out[i * 16 : i * 16 + RT] - mod[1, 2, 1:2, :] * out[i * 16 + RT : (i + 1) * 16]
            )
        for q in range(NX):
            full = hidt[q].astype(F32)
            text = [full[i * 16 : i * 16 + RT] for i in range(NZ)]
            for i in range(NZ):
                h32[q, i * RC + RI : (i + 1) * RC, :] = text[i]
            TS[1, q] = jnp.concatenate(text, axis=0).astype(BF16)
        send_text(1)

    def down_rest():
        w_step3(3)
        down_text()
        lax.fori_loop(5, NZ, rest_chunk, 0)

    def order(k):
        return k + 5 * (1 - (k + 5) // 8) + (k // 5) * (7 - 2 * k)

    def hidden_step(k, _):
        @pl.when(k < NZ)
        def _():
            act_chunk(order(k))

        at(k, 1, join_text)
        at(k, 3, act_text)

        @pl.when(jnp.logical_and(k >= LAG, k < NZ + LAG))
        def _():
            ag_img(order(k - LAG)).forward()

        at(k, LAG + 1, w_step2, 3)
        at(k, LAG + 1, w_step3, 2)
        at(k, LAG + 3, pass_text)

        @pl.when(k >= LAG + 2)
        def _():
            down_chunk(order(k - LAG - 2))

        at(k, LAG + 4, down_rest)
        at(k, LAG + 5, send_text, 0)

        @pl.when(k >= LAG + 5)
        def _():
            rest_chunk(order(k - LAG - 2), 0)

        return 0

    lax.fori_loop(0, NZ + LAG + 2, hidden_step, 0)

    lane = lax.broadcasted_iota(jnp.int32, (CH, SEQ), 1)
    img_lane = lane % RC < RI
    uT[...] = jnp.where(img_lane, u32[...].T, 0.0).astype(BF16)
    hc[...] = h32[...].astype(BF16)
    pre_c[...] = gelu_slope(pre_c[...])

    total = ndiff[...] + zst[0].astype(F32)
    remote(zr.at[1:NZ], zr.at[1:NZ], s_sent.at[9], s_mz, core).wait_recv()
    for s in range(1, NZ):
        total = total + zr[s].astype(F32)
    total = total * coef[:, 0:1]
    err_i = mod[0, 2, 0:1, :] * total[0:RI]
    err_t = mod[1, 2, 0:1, :] * total[RI : RI + RT]
    errz[0] = jnp.concatenate([err_i, err_t], axis=0).astype(BF16)

    def send_e(i, to, p, who):
        rows = pl.ds(p * 32, 32)
        return remote(errz.at[i, rows], errz.at[to, rows], s_sent.at[10], s_ez.at[to, p], who)

    for p in range(2):
        send_e(0, 1, p, zdev(1)).start()
        send_e(0, 2, p, zdev(-1)).start()

    def rs_hg(i):
        return Sum(
            lambda q: hgs.at[i, q], hgr.at[2, i], lambda k: hgr.at[k, i], hgr.at[0:2, i],
            s_sent.at[11], (s_hg.at[i, 0], s_hg.at[i, 1]), x, xdev, sign(i),
        )

    def ag_early(i):
        rows = pl.ds(pl.multiple_of(i * RC, RC), RC)
        return Gather(
            lambda q: pg.at[:, q, rows], None, s_sent.at[12], (s_pge.at[i], s_pgeg), x, xdev, sign(i)
        )

    def ag_late(j, h):
        rows = pl.ds(SEQ // 2 + h * (SEQ // 4), SEQ // 4)
        return Gather(
            lambda q: pg.at[j, q, rows], pg.at[j, 0:2, rows], s_sent.at[12], (s_pg.at[j, h], s_pgg.at[j, h]),
            x, xdev, 1 - 2 * h,
        )

    def pre_early(i):
        rs_hg(i).wait()
        g = hgs[i, x].astype(F32) + hgr[0, i].astype(F32) + hgr[1, i].astype(F32)
        rows = pl.ds(pl.multiple_of(i * RC, RC), RC)
        g = (g * pre_c[rows, :]).astype(BF16)
        for j in range(NJ):
            pg[j, x, rows, :] = g[:, j * HJ : (j + 1) * HJ]
        ag_early(i).first()

    def pre_late(j):
        lanes = slice(j * HJ, (j + 1) * HJ)
        late = slice(NZ // 2, NZ)
        g = hgs[late, x, :, lanes].astype(F32) + hgr[0, late, :, lanes].astype(F32) + hgr[1, late, :, lanes].astype(F32)
        pg[j, x, SEQ // 2 :, :] = (g.reshape(SEQ // 2, HJ) * pre_c[SEQ // 2 :, lanes]).astype(BF16)
        for h in range(2):
            ag_late(j, h).first()

    def pass_late(j):
        for h in range(2):
            ag_late(j, h).forward()

    def err_pass(i, p):
        send_e(i, i, p, zdev(1)).wait_recv()

        @pl.when(i < 6)
        def _():
            send_e(i, i + 2, p, zdev((i % 2) * 2 - 1)).start()

    def err_chunk(i):
        full = errz[i].astype(F32)
        image = full[0:RI].astype(BF16)
        text = full[RI:RC].astype(BF16)
        t32[pl.ds(pl.multiple_of(i * RT, 8), RT), :] = full[RI:RC]
        for q in range(NX):
            lanes = slice(q * HQ, (q + 1) * HQ)
            hgs[i, q] = jnp.concatenate([dot(image, W[2, :, lanes]), dot(text, W[3, :, lanes])], axis=0).astype(BF16)
        rs_hg(i).first()

    err_chunk(0)

    def err_step(k, _):
        for p in range(2):
            err_pass(2 * k - 1, p)

            @pl.when(k < 4)
            def _():
                err_pass(2 * k, p)

        err_chunk(2 * k - 1)

        @pl.when(k < 4)
        def _():
            err_chunk(2 * k)

        for i in (3, 2):

            @pl.when(2 * k - i >= 0)
            def _():
                rs_hg(2 * k - i).join()

        at(k, 2, pre_early, 0)
        at(k, 3, pre_early, 1)
        at(k, 4, pre_early, 2)
        at(k, 4, pre_early, 3)

        @pl.when(k >= 3)
        def _():
            ag_early(k - 3).forward()

        @pl.when(k == 3)
        def _():
            halves(2, slice(0, 32))
            send_text(2, slice(0, 32))

        return 0

    lax.fori_loop(1, 5, err_step, 0)
    halves(2, slice(32, TXT))
    send_text(2, slice(32, TXT))

    def cols(j):
        return pl.ds(j * HJ, HJ)

    def core_cp(m, j, l):
        return remote(G.at[m, l * 2 + 1 - c, :, cols(j)], CR.at[m, l, :, cols(j)], s_sent.at[13], s_core.at[m, j], core)

    def rs_y(m, j, h):
        rows = pl.ds(h * HR, HR)
        return Sum(
            lambda yy: G.at[m, (yy % 2) * 2 + c, pl.ds(pl.multiple_of((yy // 2) * ROWS + h * HR, HR), HR), cols(j)],
            YR.at[m, 2, rows, cols(j)], lambda k: YR.at[m, k, rows, cols(j)], None,
            s_sent.at[14], (s_y.at[m, j, 0], s_y.at[m, j, 1]), y, ydev, 1 - 2 * h,
        )

    def grad(m, j, left, wide):
        g = dot(left, wide).astype(BF16)
        for q in range(NX):
            G[m, q, :, j * HJ : (j + 1) * HJ] = g[:, q * HJ : (q + 1) * HJ]
        for l in range(2):
            core_cp(m, j, l).start()

    def after_core(m, j):
        both = CR.at[m, :, :, cols(j)]
        remote(both, both, s_sent.at[13], s_core.at[m, j], core).wait_recv()
        for l in range(2):
            G[m, l * 2 + c, :, cols(j)] = (
                G[m, l * 2 + c, :, cols(j)].astype(F32) + CR[m, l, :, cols(j)].astype(F32)
            ).astype(BF16)
        for h in range(2):
            rs_y(m, j, h).relayed.start()
        for h in range(2):
            rs_y(m, j, h).direct.start()

    def join_y(m, j):
        both = YR.at[m, 2, :, cols(j)]
        remote(both, both, s_sent.at[14], s_y.at[m, j, 0], core).wait_recv()
        for h in range(2):
            rs_y(m, j, h).add()

    mine = pl.ds(pl.multiple_of(hi * ROWS, ROWS), ROWS)
    outs = (out_ui, out_di, out_ut, out_dt)

    def out_cp(o, j):
        return pltpu.make_async_copy(OB.at[o, :, cols(j)], outs[o].at[:, cols(j)], s_out.at[o])

    def finish(m, j):
        both = YR.at[m, 0:2, :, cols(j)]
        remote(both, both, s_sent.at[14], s_y.at[m, j, 1], core).wait_recv()
        g = G[m, lo * 2 + c, mine, cols(j)].astype(F32)
        for k in range(2):
            g = g + YR[m, k, :, cols(j)].astype(F32)
        OB[1 - m, :, cols(j)] = g
        out_cp(1 - m, j).start()

    def text_grad(o, fl, fr):
        left = TA[fl].reshape(8 * TXT, ROWS).astype(F32).T.astype(BF16)
        OB[o] = dot(left, TA[fr].reshape(8 * TXT, HQ))
        for j in range(NJ):
            out_cp(o, j).start()

    eT[...] = jnp.where(img_lane, errz[...].reshape(SEQ, CH).astype(F32).T, 0.0).astype(BF16)
    for j in range(NJ):
        grad(0, j, eT[...], jnp.concatenate([hc[q, :, j * HJ : (j + 1) * HJ] for q in range(NX)], axis=1))
    rs_hg(7).join()
    ag_early(2).forward()
    for j in range(NJ):
        after_core(0, j)
    ag_early(3).forward()
    for i in range(NZ // 2, NZ):
        rs_hg(i).wait()
    for j in range(NJ):
        pre_late(j)
    def pg_text(part):
        rows = slice(part * 32, part * 32 + 32)
        tokens = slice(part * (SEQ // 2), (part + 1) * (SEQ // 2))
        for q in range(NX):
            for j in range(NJ):
                text = pg[j, q, tokens, :].astype(F32).reshape(NZ // 2, RC, HJ)[:, RI:RC]
                TS[3, q, rows, j * HJ : (j + 1) * HJ] = text.reshape(32, HJ).astype(BF16)
        send_text(3, rows)

    pass_late(0)
    join_y(0, 0)
    early = pg.at[:, 0:2, 0 : SEQ // 2]
    remote(early, early, s_sent.at[12], s_pgeg, core).wait_recv()
    pass_late(1)
    pg_text(0)
    join_y(0, 1)
    pass_late(2)
    join_y(0, 2)

    def up_grad(j):
        for h in range(2):
            ag_late(j, h).wait()
        grad(1, j, uT[...], jnp.concatenate([pg[j, q] for q in range(NX)], axis=1))

    for j in range(NJ - 1):
        up_grad(j)
    after_core(1, 0)
    up_grad(NJ - 1)
    for j in range(1, NJ):
        after_core(1, j)
    pg_text(1)

    join_y(1, 0)
    for j in range(NJ):
        finish(0, j)
    join_y(1, 1)
    wait_text(1)
    wait_text(2)
    text_grad(3, 2, 1)
    join_y(1, 2)
    wait_text(0)
    wait_text(3)
    text_grad(2, 0, 3)
    for j in range(NJ):
        finish(1, j)

    sent = (
        W.at[:, 0:QR], W.at[:, 0:QR], W.at[:, 0 : 2 * QR], uall.at[0:7], rrs, rrs, rrst, rrst,
        hgs.at[0:7], zst.at[0:7], errz.at[0:7], hgr, hgr, CR, YR,
    )
    for k, whole in enumerate(sent):
        remote(whole, whole, s_sent.at[k], s_sent.at[k], core).wait_send()
    for o in range(4):
        pltpu.make_async_copy(OB.at[o], outs[o], s_out.at[o]).wait()


def hand_on(a, b, c, d, oa, ob, oc, od, buf, s_in, s_out):
    ins = [pltpu.make_async_copy(src, buf.at[i], s_in.at[i]) for i, src in enumerate((a, b, c, d))]
    outs = [pltpu.make_async_copy(buf.at[i], dst, s_out.at[i]) for i, dst in enumerate((oa, ob, oc, od))]
    for cp in ins:
        cp.start()
    for i in range(4):
        ins[i].wait()
        outs[i].start()
    for cp in outs:
        cp.wait()


def body(
    latent_image, latent_text, noise_image, noise_text, up_image, down_image, up_text, down_text,
    modulation, timesteps, skips, text_lengths,
):
    any_ = pl.BlockSpec(memory_space=pl.ANY)
    vmem = pl.BlockSpec(memory_space=pltpu.VMEM)
    smem = pl.BlockSpec(memory_space=pltpu.SMEM)
    V = pltpu.VMEM
    dma = lambda *s: pltpu.SemaphoreType.DMA(s)
    out = jax.ShapeDtypeStruct((ROWS, HQ), F32)
    grads = pl.pallas_call(
        kernel,
        out_shape=(out, out, out, out),
        in_specs=[any_] * 8 + [vmem, smem, smem, smem],
        out_specs=(any_,) * 4,
        scratch_shapes=[
            V((RI, D), BF16), V((RT, D), BF16), V((RI, D), BF16), V((RT, D), BF16),
            V((4, CH, HB), BF16), V((NZ, 2 * RC, CH), BF16),
            V((RI + RT, CH), F32), V((2, 3, 2, CH), F32), V((RI + RT, 128), F32), V((SEQ, CH), F32),
            V((NZ, NX, 2 * RI, HQ), BF16), V((NX, 128, HQ), BF16),
            V((NZ, 3, 2 * RI, HQ), BF16), V((3, 128, HQ), BF16),
            V((NZ, NX, 2 * RI, HQ), BF16), V((NX, 128, HQ), BF16),
            V((SEQ, HQ), F32), V((NX, SEQ, HQ), F32), V((NX, SEQ, HQ), BF16),
            V((NZ, 64, CH), BF16), V((NZ, 16, CH), F32), V((NZ, 64, CH), BF16), V((NZ, 64, CH), BF16),
            V((TXT, CH), F32), V((CH, SEQ), BF16), V((CH, SEQ), BF16),
            V((NZ, NX, RC, HQ), BF16), V((3, NZ, RC, HQ), BF16), V((NJ, NX, SEQ, HJ), BF16),
            V((2, NX, CH, HQ), BF16), V((2, 2, CH, HQ), BF16), V((2, 3, ROWS, HQ), BF16),
            V((4, 4, TXT, HQ), BF16), V((4, 2, 4, TXT, HQ), BF16), V((4, ROWS, HQ), F32),
            dma(4), dma(4), dma(7), dma(7), dma(7), dma(NZ, 2), dma(NZ, 2), dma(2, 2), dma(NZ, 2), dma(2, 2),
            pltpu.SemaphoreType.DMA, dma(NZ, 2), dma(NZ, 2), dma(4), pltpu.SemaphoreType.DMA, dma(NJ, 2), dma(NJ, 2), dma(2, NJ), dma(2, NJ, 2), dma(4), dma(4), dma(15),
        ],
        compiler_params=pltpu.CompilerParams(
            collective_id=0, has_side_effects=True, vmem_limit_bytes=60 * 1024 * 1024
        ),
    )(
        latent_image, latent_text, noise_image, noise_text, up_image, up_text, down_image, down_text,
        modulation, timesteps, skips, text_lengths,
    )
    return pl.pallas_call(
        hand_on, out_shape=(out, out, out, out), in_specs=[any_] * 4, out_specs=(any_,) * 4,
        scratch_shapes=[V((4, ROWS, HQ), F32), dma(4), dma(4)],
    )(*grads)


def solution(mesh):
    placed = (
        P("dp", "col", None),
        P("dp", "col", None),
        P("dp", "col", None),
        P("dp", "col", None),
        P("row", "col"),
        P("row", "col"),
        P("row", "col"),
        P("row", "col"),
        P(),
        P("dp"),
        P("dp"),
        P("dp"),
    )
    grads = P("row", ("col", "dp"))
    return jax.shard_map(
        body, mesh=mesh, in_specs=placed, out_specs=(grads, grads, grads, grads), check_vma=False
    )
```
